32 devices in a mesh: groups: 2 (over x), tensor: 4 (over y, core), replica: 4 (over z).
Axes of the slice: x: 2, y: 2, z: 4, core: 2. Of those that a mesh axis runs over, the one named last changes fastest.
Arguments:
- acts: bfloat16 [2, 1024, 16384], P(None, ('groups', 'replica'), 'tensor'), parts along dimension 1, may hold values from -6 to 6
- cots: bfloat16 [2, 1024, 16384], P(None, ('groups', 'replica'), 'tensor'), parts along dimension 1, may hold values from -6 to 6
- down_factor: float32 [4, 16384, 32], P('groups', 'tensor'), parts along dimension 0, may hold values from -4 to 4
- up_factor: float32 [4, 32, 16384], P('groups', None, 'tensor'), parts along dimension 0, may hold values from -4 to 4
- down_first_moment: float32 [4, 16384, 32], P('groups', 'tensor'), parts along dimension 0, may hold values from -6 to 6
- down_second_moment: float32 [4, 16384, 32], P('groups', 'tensor'), parts along dimension 0, may hold values from 0.01 to 1
- up_first_moment: float32 [4, 32, 16384], P('groups', None, 'tensor'), parts along dimension 0, may hold values from -6 to 6
- up_second_moment: float32 [4, 32, 16384], P('groups', None, 'tensor'), parts along dimension 0, may hold values from 0.01 to 1
- rollout_weight: bfloat16 [16384, 16384], P('replica', 'tensor'), may hold values from -6 to 6
- owner: int32 [4], replicated, may hold values from 0 to 3, each once
- projection_index: int32 [8], P('groups'), parts along dimension 0, may hold values from 0 to 1
Outputs:
- fresh_down_factor: float32 [4, 16384, 32], P('groups', 'tensor'), parts along dimension 0
- fresh_up_factor: float32 [4, 32, 16384], P('groups', None, 'tensor'), parts along dimension 0
- fresh_down_first: float32 [4, 16384, 32], P('groups', 'tensor'), parts along dimension 0
- fresh_down_second: float32 [4, 16384, 32], P('groups', 'tensor'), parts along dimension 0
- fresh_up_first: float32 [4, 32, 16384], P('groups', None, 'tensor'), parts along dimension 0
- fresh_up_second: float32 [4, 32, 16384], P('groups', None, 'tensor'), parts along dimension 0
- fresh_rollout_weight: bfloat16 [32768, 16384], P(('groups', 'replica'), 'tensor'), parts along dimension 0
The draws below stay inside these ranges and needn't reach their ends.
There are 2 independent parts, one for each index of `groups`. The reference program is written for one: setup_inputs(seed, part) draws one part's arguments, and reference() takes and returns one part's arrays. A program takes and returns all parts, laid end to end along the dimension named above; an argument that names none is the same for every part. Nothing has to cross between parts.
Inputs may be any that keep to these rules, and one draw needn't show every extreme that they name: owner lists every index of 0 to 3 exactly once.
All inputs are finite; a program needn't handle non-finite values.
Results may differ from the reference program's by a relative error of at most 0.0095.
Values may be sent and summed in bfloat16 or wider, within the bound.
No kernel may reach another device: no remote copies, remote signals or barrier semaphores. Data moves between devices by JAX's collectives and lax.ppermute only.
A program may use at most 192 MiB of HBM per device.

```python
import math
import jax
import jax.numpy as jnp

MODEL_WIDTH = 16384
ADAPTER_RANK = 32
TOKEN_COUNT = 512
N_TENSOR = 4
N_REPLICA = 4


def place_ends(array, rng, low, high):
    extent = array.shape
    spot = [jax.random.randint(jax.random.fold_in(rng, axis), (), 0, extent[axis]) for axis in range(len(extent))]
    array = array.at[tuple(spot)].set(low)
    longest = extent.index(max(extent))
    spot[longest] = (spot[longest] + 1) % extent[longest]
    return array.at[tuple(spot)].set(high)


def block_scale(key, dims, pieces, low, top_value):
    factor_of, own = 1.0, jax.random.fold_in(key, 6)
    for dim, shards_of in pieces:
        draws = jnp.exp(jax.random.uniform(jax.random.fold_in(own, dim), (shards_of,), jnp.float32, low / len(pieces), top_value / len(pieces)))
        factor_of = factor_of * jnp.repeat(draws, dims[dim] // shards_of).reshape([-1 if axis == dim else 1 for axis in range(len(dims))])
    return factor_of


def centred(stream_key, extent, scale, limit, split=(), kind=jnp.bfloat16):
    entries = jax.random.normal(stream_key, extent, jnp.float32) * scale
    if len(split) > 0:
        entries = block_scale(stream_key, extent, split, -0.22, 0.18) * entries
    return jnp.clip(entries, min=-limit, max=limit).astype(kind)


def setup_inputs(seed: int = 0, part: int = 0) -> dict:
    key_of = jax.random.split(jax.random.key(seed), 12)
    part_keys = jax.random.split(jax.random.fold_in(key_of[11], part), 12)
    return {
        "acts": centred(part_keys[0], (2, TOKEN_COUNT, MODEL_WIDTH), 1.0, 6.0, ((1, 4), (2, 4))),
        "cots": centred(part_keys[1], (2, TOKEN_COUNT, MODEL_WIDTH), 1.0, 6.0, ((1, 4), (2, 4))),
        "down_factor": centred(part_keys[2], (2, MODEL_WIDTH, ADAPTER_RANK), 0.5, 4.0, ((1, 4),), jnp.float32),
        "up_factor": centred(part_keys[3], (2, ADAPTER_RANK, MODEL_WIDTH), 0.5, 4.0, ((2, 4),), jnp.float32),
        "down_first_moment": centred(part_keys[4], (2, MODEL_WIDTH, ADAPTER_RANK), 1.0, 6.0, ((1, 4),), jnp.float32),
        "down_second_moment": jnp.clip(jnp.exp(math.log(1.0) - 4.6051702 * jax.random.uniform(part_keys[5], (2, MODEL_WIDTH, ADAPTER_RANK), jnp.float32) ** block_scale(part_keys[5], (2, MODEL_WIDTH, ADAPTER_RANK), ((1, 4),), -0.2, 0.2)), 0.01, 1.0),
        "up_first_moment": centred(part_keys[6], (2, ADAPTER_RANK, MODEL_WIDTH), 1.0, 6.0, ((2, 4),), jnp.float32),
        "up_second_moment": jnp.clip(jnp.exp(math.log(1.0) - 4.6051702 * jax.random.uniform(part_keys[7], (2, ADAPTER_RANK, MODEL_WIDTH), jnp.float32) ** block_scale(part_keys[7], (2, ADAPTER_RANK, MODEL_WIDTH), ((2, 4),), -0.2, 0.2)), 0.01, 1.0),
        "rollout_weight": centred(key_of[8], (MODEL_WIDTH, MODEL_WIDTH), 1.0, 6.0, ((0, 4), (1, 4))),
        "owner": jax.random.permutation(key_of[9], N_TENSOR).astype(jnp.int32),
        "projection_index": place_ends(jax.random.randint(part_keys[10], (N_REPLICA,), 0, 2), jax.random.fold_in(part_keys[10], 1), 0, 1).astype(jnp.int32),
    }


adapter_scale = 2.0
learn_rate = 0.05
beta_one = 0.9
beta_two = 0.999
adam_eps = 1e-08
fix_one = 1.0 - 0.9 ** 10
fix_two = 1.0 - 0.999 ** 10

def moment_update(param, first, second, grad):
    first_new = beta_one * first + (1.0 - beta_one) * grad
    second_new = beta_two * second + (1.0 - beta_two) * grad * grad
    param_new = param - learn_rate * (first_new / fix_one) / (jnp.sqrt(second_new / fix_two) + adam_eps)
    return (param_new, first_new, second_new)

def reference(acts, cots, down_factor, up_factor, down_first_moment, down_second_moment, up_first_moment, up_second_moment, rollout_weight, owner, projection_index):
    down_broadcast = down_factor.astype(jnp.bfloat16).astype(jnp.float32)
    up_broadcast = up_factor.astype(jnp.bfloat16).astype(jnp.float32)
    acts_f = acts.astype(jnp.float32)
    cots_f = cots.astype(jnp.float32)
    low_in = jnp.einsum('ptd,pdr->ptr', acts_f, down_broadcast).astype(jnp.bfloat16).astype(jnp.float32)
    low_out = jnp.einsum('ptd,prd->ptr', cots_f, up_broadcast).astype(jnp.bfloat16).astype(jnp.float32)
    coefficient = adapter_scale / TOKEN_COUNT
    down_gradient = jnp.einsum('ptd,ptr->pdr', acts_f, low_out) * coefficient
    up_gradient = jnp.einsum('ptr,ptd->prd', low_in, cots_f) * coefficient
    fresh_down_factor, fresh_down_first, fresh_down_second = moment_update(down_factor, down_first_moment, down_second_moment, down_gradient)
    fresh_up_factor, fresh_up_first, fresh_up_second = moment_update(up_factor, up_first_moment, up_second_moment, up_gradient)
    a_send = fresh_down_factor.astype(jnp.bfloat16)
    b_send = fresh_up_factor.astype(jnp.bfloat16)
    block_cols = MODEL_WIDTH // N_TENSOR
    block_rows = MODEL_WIDTH // N_REPLICA
    b_perm = b_send.reshape(2, ADAPTER_RANK, N_TENSOR, block_cols)[:, :, owner, :].reshape(2, ADAPTER_RANK, MODEL_WIDTH)
    block_parts = []
    for index in range(N_REPLICA):
        proj = projection_index[index]
        a_rows = a_send[proj, index * block_rows:(index + 1) * block_rows, :]
        weight_change = jnp.dot(a_rows, b_perm[proj], preferred_element_type=jnp.float32)
        frozen_matrix = rollout_weight[index * block_rows:(index + 1) * block_rows, :].astype(jnp.float32)
        block_parts.append((frozen_matrix + adapter_scale * weight_change).astype(jnp.bfloat16))
    fresh_rollout_weight = jnp.concatenate(block_parts, axis=0)
    return (fresh_down_factor, fresh_up_factor, fresh_down_first, fresh_down_second, fresh_up_first, fresh_up_second, fresh_rollout_weight)
```

```python
import functools

import jax
import jax.numpy as jnp
from jax import lax
from jax.experimental import pallas as pl
from jax.experimental.pallas import tpu as pltpu
from jax.sharding import PartitionSpec as P

adapter_scale = 2.0
learn_rate = 0.05
beta_one = 0.9
beta_two = 0.999
adam_eps = 1e-08
fix_one = 1.0 - 0.9**10
fix_two = 1.0 - 0.999**10

MIB = 1024 * 1024


def moment_update(param, first, second, grad):
    first_new = beta_one * first + (1.0 - beta_one) * grad
    second_new = beta_two * second + (1.0 - beta_two) * grad * grad
    param_new = param - learn_rate * (first_new / fix_one) / (
        jnp.sqrt(second_new / fix_two) + adam_eps
    )
    return (param_new, first_new, second_new)


def move(x, axis, pairs):
    return lax.ppermute(x, axis, pairs)


def swap(x, axis, size, distance):
    return lax.ppermute(x, axis, [(i, i ^ distance) for i in range(size)])


def low_kernel(acts, cots, down, up, out, total):
    step = pl.program_id(0)

    @pl.when(step == 0)
    def _():
        total[...] = jnp.zeros_like(total)

    rank = down.shape[1]
    for spot, (tokens, factor) in enumerate(((cots, up), (acts, down))):
        for p in range(2):
            rows = pl.ds((2 * spot + p) * rank, rank)
            total[rows, :] += lax.dot_general(
                factor[p].astype(jnp.bfloat16),
                tokens[p],
                (((1,), (1,)), ((), ())),
                preferred_element_type=jnp.float32,
            )

    @pl.when(step == pl.num_programs(0) - 1)
    def _():
        out[...] = total[...].astype(out.dtype)


def low_parts(acts, cots, down, up):
    tokens, width = acts.shape[1:]
    rank = down.shape[1]
    steps = max(1, width // 1024)
    cut = width // steps
    token_spec = pl.BlockSpec((2, tokens, cut), lambda k: (0, 0, k))
    factor_spec = pl.BlockSpec((2, rank, cut), lambda k: (0, 0, k))
    return pl.pallas_call(
        low_kernel,
        grid=(steps,),
        in_specs=[token_spec, token_spec, factor_spec, factor_spec],
        out_specs=pl.BlockSpec((4 * rank, tokens), lambda k: (0, 0)),
        out_shape=jax.ShapeDtypeStruct((4 * rank, tokens), jnp.bfloat16),
        scratch_shapes=[pltpu.VMEM((4 * rank, tokens), jnp.float32)],
        compiler_params=pltpu.CompilerParams(vmem_limit_bytes=16 * MIB),
        name="low_parts",
    )(acts, cots, down, up)


def gradient_kernel(parity, *refs, base, rank, coefficient, parts):
    lows = refs[:parts]
    tokens, send, keep, total = refs[parts:]
    j, k = pl.program_id(0), pl.program_id(1)

    @pl.when((j == 0) & (k == 0))
    def _():
        acc = lows[0][...].astype(jnp.float32)
        for other in lows[1:]:
            acc = acc + other[...].astype(jnp.float32)
        total[...] = acc.astype(jnp.bfloat16)

    p = jnp.where(j == 0, 1 - parity[0], parity[0])
    start = pl.multiple_of((base + p) * rank, rank)
    grad = coefficient * jnp.dot(
        total[pl.ds(start, rank), :], tokens[...], preferred_element_type=jnp.float32
    )

    @pl.when(j == 0)
    def _():
        send[...] = grad.astype(send.dtype)

    @pl.when(j == 1)
    def _():
        keep[...] = grad.astype(keep.dtype)


def gradient_parts(parity, lows, tokens, base, rank, coefficient):
    count, width = tokens.shape[1:]
    steps = max(1, width // 2048)
    cut = width // steps
    low_spec = pl.BlockSpec((4 * rank, count), lambda j, k, par: (0, 0))
    half = jax.ShapeDtypeStruct((rank, width), jnp.bfloat16)
    return pl.pallas_call(
        functools.partial(
            gradient_kernel, base=base, rank=rank, coefficient=coefficient, parts=len(lows)
        ),
        grid_spec=pltpu.PrefetchScalarGridSpec(
            num_scalar_prefetch=1,
            grid=(2, steps),
            in_specs=[low_spec] * len(lows)
            + [
                pl.BlockSpec(
                    (None, count, cut),
                    lambda j, k, par: (jnp.where(j == 0, 1 - par[0], par[0]), 0, k),
                )
            ],
            out_specs=[
                pl.BlockSpec((rank, cut), lambda j, k, par: (0, jnp.where(j == 0, k, steps - 1))),
                pl.BlockSpec((rank, cut), lambda j, k, par: (0, jnp.where(j == 0, 0, k))),
            ],
            scratch_shapes=[pltpu.VMEM((4 * rank, count), jnp.bfloat16)],
        ),
        out_shape=(half, half),
        compiler_params=pltpu.CompilerParams(vmem_limit_bytes=16 * MIB),
        name="gradient_parts",
    )(parity, *lows, tokens)


def refresh_kernel(rows, cols, weight, out):
    change = lax.dot_general(
        rows[...], cols[...], (((0,), (0,)), ((), ())), preferred_element_type=jnp.float32
    )
    out[...] = (weight[...].astype(jnp.float32) + adapter_scale * change).astype(out.dtype)


def refresh(rows, cols, weight):
    rank = rows.shape[0]
    height, width = weight.shape
    block = min(height, 256)
    return pl.pallas_call(
        refresh_kernel,
        grid=(height // block,),
        in_specs=[
            pl.BlockSpec((rank, block), lambda i: (0, i)),
            pl.BlockSpec((rank, width), lambda i: (0, 0)),
            pl.BlockSpec((block, width), lambda i: (i, 0)),
        ],
        out_specs=pl.BlockSpec((block, width), lambda i: (i, 0)),
        out_shape=jax.ShapeDtypeStruct((height, width), weight.dtype),
        compiler_params=pltpu.CompilerParams(vmem_limit_bytes=24 * MIB),
        cost_estimate=pl.CostEstimate(
            flops=2 * height * width * rank, bytes_accessed=4 * height * width, transcendentals=0
        ),
        name="refresh",
    )(rows, cols, weight)


def tensor_sum_parts(low, size):
    parts, stride = [low], 1
    while stride < size:
        if len(parts) > 1:
            total = functools.reduce(jnp.add, [x.astype(jnp.float32) for x in parts])
            parts = [total.astype(jnp.bfloat16)]
        radix = min(4, size // stride)
        mine = parts[0]
        for hop in range(1, radix):
            pairs = [
                (i, i - i % (stride * radix) + (i + hop * stride) % (stride * radix))
                for i in range(size)
            ]
            parts.append(move(mine, "tensor", pairs))
        stride *= radix
    return parts


def replica_sum(send, keep, size):
    own = (keep.astype(jnp.float32) + swap(send, "replica", size, 1).astype(jnp.float32)).astype(
        jnp.bfloat16
    )
    distance = 2
    while distance < size:
        other = swap(own, "replica", size, distance)
        own = (own.astype(jnp.float32) + other.astype(jnp.float32)).astype(jnp.bfloat16)
        distance *= 2
    return own, swap(own, "replica", size, 1)


def pick_columns(block, owner, index, size):
    held, names = [block], [index]
    distance = size // 2
    while distance > 1:
        came = [swap(x, "tensor", size, distance) for x in held]
        names = names + [n ^ distance for n in names]
        held = held + came
        distance //= 2
    wanted = owner[index ^ 1]
    offer = held[0]
    for name, x in zip(names[1:], held[1:]):
        offer = jnp.where(wanted == name, x, offer)
    held = held + [swap(offer, "tensor", size, 1)]
    wanted = owner[index]
    found = held[-1]
    for name, x in zip(names, held):
        found = jnp.where(wanted == name, x, found)
    return found


def pick_rows(block, tensor_idx, replica_idx, t_size, r_size):
    width = block.shape[1]
    many = max(1, t_size // r_size)
    distance = 1
    while distance < many:
        other = swap(block, "tensor", t_size, distance)
        low_first = (tensor_idx & distance) == 0
        block = jnp.where(
            low_first,
            jnp.concatenate([block, other], axis=1),
            jnp.concatenate([other, block], axis=1),
        )
        distance *= 2
    holders = [set(range(r * t_size // r_size, r * t_size // r_size + many)) for r in range(r_size)]
    steps = []
    distance = many
    while distance < t_size:
        steps.append(distance)
        distance *= 2
    for distance in reversed(steps):
        pairs = []
        for r in range(r_size):
            for t in sorted(holders[r]):
                pairs.append((t * r_size + r, (t ^ distance) * r_size + r))
            holders[r] |= {t ^ distance for t in holders[r]}
        came = move(block, ("tensor", "replica"), pairs)
        takes = jnp.asarray(
            [[1 if (t * r_size + r) in {b for _, b in pairs} else 0 for r in range(r_size)] for t in range(t_size)],
            jnp.int32,
        )[tensor_idx, replica_idx]
        block = jnp.where(takes == 1, came, block)
    parts = max(1, r_size // t_size)
    if parts > 1:
        size = width // parts
        block = lax.dynamic_slice_in_dim(block, (replica_idx % parts) * size, size, 1)
    return block


def per_device(
    acts,
    cots,
    down_factor,
    up_factor,
    down_first_moment,
    down_second_moment,
    up_first_moment,
    up_second_moment,
    rollout_weight,
    owner,
    projection_index,
):
    t_size, r_size = lax.axis_size("tensor"), lax.axis_size("replica")
    replica_idx = lax.axis_index("replica")
    tensor_idx = lax.axis_index("tensor")
    turn = lambda x: jnp.transpose(x, (0, 2, 1))
    down, down_first, down_second = map(turn, (down_factor, down_first_moment, down_second_moment))
    rank = up_factor.shape[1]
    parity = replica_idx % 2
    parity_ref = parity.reshape(1).astype(jnp.int32)
    proj = projection_index[replica_idx]

    low = low_parts(acts, cots, down, up_factor)
    lows = tensor_sum_parts(low, t_size)
    coefficient = adapter_scale / (acts.shape[1] * r_size)
    up_send, up_keep = gradient_parts(parity_ref, lows, cots, 2, rank, coefficient)
    down_send, down_keep = gradient_parts(parity_ref, lows, acts, 0, rank, coefficient)
    up_own, up_other = replica_sum(up_send, up_keep, r_size)
    down_own, down_other = replica_sum(down_send, down_keep, r_size)

    def both(own, other):
        return jnp.stack(
            [jnp.where(parity == 0, own, other), jnp.where(parity == 0, other, own)]
        ).astype(jnp.float32)

    def chosen(param, first, second, own, other):
        take = lambda x: lax.dynamic_index_in_dim(x, proj, 0, keepdims=False)
        grad = jnp.where(proj == parity, own, other).astype(jnp.float32)
        return moment_update(take(param), take(first), take(second), grad)[0].astype(jnp.bfloat16)

    b_mine = chosen(up_factor, up_first_moment, up_second_moment, up_own, up_other)
    cols = pick_columns(b_mine, owner, tensor_idx, t_size)
    a_mine = chosen(down, down_first, down_second, down_own, down_other)
    rows = pick_rows(a_mine, tensor_idx, replica_idx, t_size, r_size)
    fresh_rollout_weight = refresh(rows, cols, rollout_weight)

    fresh_up = moment_update(up_factor, up_first_moment, up_second_moment, both(up_own, up_other))
    fresh_down = moment_update(down, down_first, down_second, both(down_own, down_other))
    return (
        turn(fresh_down[0]),
        fresh_up[0],
        turn(fresh_down[1]),
        turn(fresh_down[2]),
        fresh_up[1],
        fresh_up[2],
        fresh_rollout_weight,
    )


def solution(mesh):
    placed = (
        P(None, ("groups", "replica"), "tensor"),
        P(None, ("groups", "replica"), "tensor"),
        P("groups", "tensor", None),
        P("groups", None, "tensor"),
        P("groups", "tensor", None),
        P("groups", "tensor", None),
        P("groups", None, "tensor"),
        P("groups", None, "tensor"),
        P("replica", "tensor"),
        P(),
        P("groups"),
    )
    return jax.shard_map(
        per_device,
        mesh=mesh,
        in_specs=placed,
        out_specs=(
            P("groups", "tensor", None),
            P("groups", None, "tensor"),
            P("groups", "tensor", None),
            P("groups", "tensor", None),
            P("groups", None, "tensor"),
            P("groups", None, "tensor"),
            P(("groups", "replica"), "tensor"),
        ),
        check_vma=False,
    )
```

```python
import functools

import jax
import jax.numpy as jnp
from jax import lax
from jax.experimental import pallas as pl
from jax.experimental.pallas import tpu as pltpu
from jax.sharding import PartitionSpec as P

adapter_scale = 2.0
learn_rate = 0.05
beta_one = 0.9
beta_two = 0.999
adam_eps = 1e-08
fix_one = 1.0 - 0.9**10
fix_two = 1.0 - 0.999**10

MIB = 1024 * 1024
FLAGS = ("proj", "column_proj", "mine", "partners")


def moment_update(param, first, second, grad):
    first_new = beta_one * first + (1.0 - beta_one) * grad
    second_new = beta_two * second + (1.0 - beta_two) * grad * grad
    param_new = param - learn_rate * (first_new / fix_one) / (
        jnp.sqrt(second_new / fix_two) + adam_eps
    )
    return (param_new, first_new, second_new)


def f32(x):
    return x.astype(jnp.float32)


def swap(x, axis, size, distance):
    return lax.ppermute(x, axis, [(i, i ^ distance) for i in range(size)])


def vmem(*shape, dtype=jnp.bfloat16):
    return pltpu.VMEM(shape, dtype)


def local(kernel, name, outs, ins=(), hbm=(), smem=(), ties=(), after=(), passed=(), scratch=()):
    n_ins, n_first = len(ins), len(ins) + len(hbm) + len(smem)
    n_outs = len(outs)

    def body(*refs):
        front = refs[:n_first]
        rest = refs[n_first + len(ties) + len(after) + len(passed) :]
        kernel(*front, *rest[:n_outs], *rest[n_outs + len(passed) :])

    operands = (
        [pltpu.with_memory_space_constraint(x, pltpu.VMEM) for x in ins]
        + [pltpu.with_memory_space_constraint(x, pltpu.HBM) for x in hbm]
        + list(smem)
        + [pltpu.with_memory_space_constraint(x, pltpu.VMEM) for x in ties]
        + [pltpu.with_memory_space_constraint(x, pltpu.HBM) for x in after]
        + [pltpu.with_memory_space_constraint(x, pltpu.VMEM) for x in passed]
    )
    specs = (
        [pl.BlockSpec(memory_space=pltpu.VMEM)] * n_ins
        + [pl.BlockSpec(memory_space=pltpu.HBM)] * len(hbm)
        + [pl.BlockSpec(memory_space=pltpu.SMEM)] * len(smem)
        + [pl.BlockSpec(memory_space=pl.ANY)] * (len(ties) + len(after) + len(passed))
    )
    first_passed = n_first + len(ties) + len(after)
    return pl.pallas_call(
        body,
        in_specs=specs,
        out_specs=[pl.BlockSpec(memory_space=pltpu.VMEM)] * n_outs
        + [pl.BlockSpec(memory_space=pl.ANY)] * len(passed),
        out_shape=list(outs) + [pltpu.VMEM(x.shape, x.dtype) for x in passed],
        input_output_aliases={first_passed + i: n_outs + i for i in range(len(passed))},
        scratch_shapes=list(scratch),
        compiler_params=pltpu.CompilerParams(vmem_limit_bytes=8 * MIB),
        cost_estimate=pl.CostEstimate(flops=0, bytes_accessed=1024, transcendentals=0),
        name=name,
    )(*operands)


def low_parts(acts, cots, down, up):
    tokens = acts.shape[1]
    rank = down.shape[1]

    def kernel(acts, cots, down, up, low, acts_in, cots_in, down_in, up_in, sems):
        jobs = []
        for spot, (x, x_in, f, f_in) in enumerate(
            ((cots, cots_in, up, up_in), (acts, acts_in, down, down_in))
        ):
            for p in range(2):
                i = 2 * spot + p
                pair = (
                    pltpu.make_async_copy(x.at[p], x_in.at[p], sems.at[2 * i]),
                    pltpu.make_async_copy(f.at[p], f_in.at[p], sems.at[2 * i + 1]),
                )
                for copy in pair:
                    copy.start()
                jobs.append((pair, x_in, f_in, p, i))
        for pair, x_in, f_in, p, i in jobs:
            for copy in pair:
                copy.wait()
            low[pl.ds(i * rank, rank), :] = lax.dot_general(
                f_in[p].astype(jnp.bfloat16),
                x_in[p],
                (((1,), (1,)), ((), ())),
                preferred_element_type=jnp.float32,
            ).astype(low.dtype)

    return local(
        kernel,
        "low_parts",
        [vmem(4 * rank, tokens), vmem(*acts.shape), vmem(*cots.shape)],
        hbm=(acts, cots, down, up),
        scratch=[
            vmem(*down.shape, dtype=jnp.float32),
            vmem(*up.shape, dtype=jnp.float32),
            pltpu.SemaphoreType.DMA((8,)),
        ],
    )


def chosen_state(down_state, up_state, projection_index, owner, t_size, r_size, tie):
    rank, width = down_state[0].shape[1:]

    def kernel(*refs):
        sources, (index, owner), (down_out, up_out, flags, sems) = refs[:6], refs[6:8], refs[8:]
        t, r = lax.axis_index("tensor"), lax.axis_index("replica")
        proj = index[r]
        copies = []
        for i, source in enumerate(sources):
            target = (down_out if i < 3 else up_out).at[i % 3]
            copies.append(pltpu.make_async_copy(source.at[proj], target, sems.at[i]))
            copies[-1].start()
        values = (proj, index[t * r_size // t_size], owner[t], owner[t ^ 1])
        for i, value in enumerate(values):
            flags[pl.ds(i * rank, rank), :] = jnp.full((rank, 128), value, jnp.int32)
        for copy in copies:
            copy.wait()

    state = vmem(3, rank, width, dtype=jnp.float32)
    return local(
        kernel,
        "chosen_state",
        [state, state, vmem(len(FLAGS) * rank, 128, dtype=jnp.int32)],
        hbm=(*down_state, *up_state),
        smem=(projection_index, owner),
        ties=(tie,),
        scratch=[pltpu.SemaphoreType.DMA((6,))],
    )


def flag(flags, name, rank):
    return flags[pl.ds(FLAGS.index(name) * rank, rank), :]


def column_tiles(width):
    return [pl.ds(k, 128) for k in range(0, width, 128)]


def down_parity(flags, rank, t_size, r_size):
    t, r = lax.axis_index("tensor"), lax.axis_index("replica")
    return flag(flags, "column_proj", rank) ^ ((r + t * r_size // t_size) % 2)


def up_parity(flags, rank, t_size, r_size):
    r = lax.axis_index("replica")
    return jnp.full((rank, 128), r % 2, jnp.int32)


def gradient_parts(lows, tokens, flags, base, coefficient, half, cuts, ties=()):
    rank = lows[0].shape[0] // 4
    width = tokens.shape[2]
    parts, piece = len(lows), width // cuts

    def kernel(*refs):
        lows, (tokens, flags), outs = refs[:parts], refs[parts : parts + 2], refs[parts + 2 :]
        rows = pl.ds(base * rank, 2 * rank)
        total = functools.reduce(jnp.add, [f32(x[rows, :]) for x in lows]).astype(jnp.bfloat16)
        kept = half(flags, rank) == 0
        cut = min(piece, 512)
        for k in range(0, width, cut):
            grads = [
                coefficient
                * jnp.dot(
                    total[p * rank : (p + 1) * rank],
                    tokens[p, :, pl.ds(k, cut)],
                    preferred_element_type=jnp.float32,
                )
                for p in range(2)
            ]
            send, keep = outs[k // piece], outs[cuts + k // piece]
            for j in range(0, cut, 128):
                first, second = [g[:, j : j + 128] for g in grads]
                tile = pl.ds(k % piece + j, 128)
                keep[:, tile] = jnp.where(kept, first, second).astype(keep.dtype)
                send[:, tile] = jnp.where(kept, second, first).astype(send.dtype)

    outs = local(
        kernel,
        "gradient_parts",
        [vmem(rank, piece)] * (2 * cuts),
        ins=(*lows, tokens, flags),
        ties=ties,
    )
    return outs[:cuts], outs[cuts:]


def join(*pairs, ties=(), passed=()):
    def kernel(*refs):
        for i in range(len(pairs)):
            x, y, out = refs[2 * i], refs[2 * i + 1], refs[2 * len(pairs) + i]
            out[...] = (f32(x[...]) + f32(y[...])).astype(out.dtype)

    return local(
        kernel,
        "join",
        [vmem(*x.shape) for x, _ in pairs],
        ins=[x for pair in pairs for x in pair],
        ties=ties,
        passed=passed,
    )


def load(weight, row, count, tie):
    def kernel(weight, out, token, sem):
        token[...] = jnp.zeros_like(token)
        copy = pltpu.make_async_copy(weight.at[pl.ds(row, count), :], out, sem)
        copy.start()
        copy.wait()

    return local(
        kernel,
        "load",
        [vmem(count, weight.shape[1]), vmem(8, 128, dtype=jnp.float32)],
        hbm=(weight,),
        ties=(tie,),
        scratch=[pltpu.SemaphoreType.DMA],
    )


def chosen_factor(state, own, other, flags, half, start=0, ties=()):
    rank, width = own.shape

    def kernel(state, own, other, flags, out):
        mine = flag(flags, "proj", rank) == half(flags, rank)
        for tile in column_tiles(width):
            grad = jnp.where(mine, f32(own[:, tile]), f32(other[:, tile]))
            held = [state[i, :, pl.ds(start + tile.start, 128)] for i in range(3)]
            out[:, tile] = moment_update(*held, grad)[0].astype(out.dtype)

    return local(
        kernel,
        "chosen_factor",
        [vmem(rank, width)],
        ins=(state, own, other, flags),
        ties=ties,
    )[0]


def adam(state, own, other, flags, half, ties=(), after=()):
    pieces = len(own)
    rank, piece = own[0].shape
    width = pieces * piece
    cut = min(piece, 2048)
    n_ties = len(ties) + len(after)

    def kernel(*refs):
        state, own, other = refs[:3], refs[3 : 3 + pieces], refs[3 + pieces : 3 + 2 * pieces]
        flags, outs = refs[3 + 2 * pieces], refs[4 + 2 * pieces + n_ties :]
        mine = half(flags, rank) == pl.program_id(0)
        for k in range(0, width, cut):

            @pl.when(pl.program_id(1) == k // cut)
            def _():
                for j in range(0, cut, 128):
                    tile, at = pl.ds(j, 128), pl.ds(k % piece + j, 128)
                    grad = jnp.where(mine, f32(own[k // piece][:, at]), f32(other[k // piece][:, at]))
                    fresh = moment_update(*[x[:, tile] for x in state], grad)
                    for out, value in zip(outs, fresh):
                        out[:, tile] = value

    block = pl.BlockSpec((None, rank, cut), lambda p, k: (p, 0, k))
    whole = pl.BlockSpec(memory_space=pltpu.VMEM)
    shape = jax.ShapeDtypeStruct(state[0].shape, jnp.float32)
    in_vmem = (*own, *other, flags, *ties)
    return pl.pallas_call(
        kernel,
        grid=(2, width // cut),
        in_specs=[block] * 3
        + [whole] * (2 * pieces + 1)
        + [pl.BlockSpec(memory_space=pl.ANY)] * n_ties,
        out_specs=[block] * 3,
        out_shape=[shape] * 3,
        compiler_params=pltpu.CompilerParams(vmem_limit_bytes=8 * MIB),
        cost_estimate=pl.CostEstimate(flops=0, bytes_accessed=1024, transcendentals=0),
        name="adam",
    )(
        *[pltpu.with_memory_space_constraint(x, pltpu.HBM) for x in state],
        *[pltpu.with_memory_space_constraint(x, pltpu.VMEM) for x in in_vmem],
        *[pltpu.with_memory_space_constraint(x, pltpu.HBM) for x in after],
    )


def pick(flags, name, held, ids, rank):
    wanted = flag(flags, name, rank)

    def tile_of(tile):
        found = f32(held[0][:, tile])
        for i in range(1, len(held)):
            found = jnp.where(wanted == ids[i], f32(held[i][:, tile]), found)
        return found

    return tile_of


def block_ids(t_size, many):
    t = lax.axis_index("tensor")
    ids, distance = [t], t_size // 2
    while distance > 1:
        ids = ids + [i ^ distance for i in ids]
        distance //= 2
    return ids[:many]


def offer(held, flags, t_size, after=()):
    rank, width = held[0].shape

    def kernel(*refs):
        held, flags, out = refs[:-2], refs[-2], refs[-1]
        tile_of = pick(flags, "partners", held, block_ids(t_size, len(held)), rank)
        for tile in column_tiles(width):
            out[:, tile] = tile_of(tile).astype(out.dtype)

    return local(
        kernel, "offer", [vmem(rank, width)], ins=(*held, flags), after=after
    )[0]


def refresh(rows, held, flags, weights, t_size):
    rank, width = held[0].shape
    height = sum(w.shape[0] for w in weights)
    block = min(weights[0].shape[0], 256)
    each = weights[0].shape[0] // block
    n_rows, n_held, n_weights = len(rows), len(held), len(weights)
    piece = rows[0].shape[1]

    def kernel(*refs):
        rows, held, flags = refs[:n_rows], refs[n_rows : n_rows + n_held], refs[n_rows + n_held]
        weights, (out, cols) = refs[n_rows + n_held + 1 : -2], refs[-2:]
        step = pl.program_id(0)

        @pl.when(step == 0)
        def _():
            ids = block_ids(t_size, n_held - 1)
            tile_of = pick(flags, "mine", (held[-1], *held[:-1]), (None, *ids), rank)
            for tile in column_tiles(width):
                cols[:, tile] = (adapter_scale * tile_of(tile)).astype(cols.dtype)

        start = pl.multiple_of((step % each) * block, block)
        cut = min(width, 256)
        for i, weight in enumerate(weights):

            @pl.when(step // each == i)
            def _():
                first = i * each * block
                at = pl.multiple_of(first % piece + start, block)
                left = rows[first // piece][:, pl.ds(at, block)].T
                for k in range(width // cut):
                    span = pl.ds(k * cut, cut)
                    change = jnp.dot(left, cols[:, span], preferred_element_type=jnp.float32)
                    out[:, span] = (f32(weight[pl.ds(start, block), span]) + change).astype(
                        out.dtype
                    )

    whole = pl.BlockSpec(memory_space=pltpu.VMEM)
    operands = (*rows, *held, flags, *weights)
    return pl.pallas_call(
        kernel,
        grid=(height // block,),
        in_specs=[whole] * len(operands),
        out_specs=pl.BlockSpec((block, width), lambda i: (i, 0)),
        out_shape=jax.ShapeDtypeStruct((height, width), weights[0].dtype),
        scratch_shapes=[vmem(rank, width)],
        compiler_params=pltpu.CompilerParams(vmem_limit_bytes=12 * MIB),
        cost_estimate=pl.CostEstimate(
            flops=0, bytes_accessed=1024, transcendentals=0
        ),
        name="refresh",
    )(*[pltpu.with_memory_space_constraint(x, pltpu.VMEM) for x in operands])


def tensor_sum_parts(low, size):
    parts, stride = [low], 1
    while stride < size:
        if len(parts) > 1:
            total = functools.reduce(jnp.add, [f32(x) for x in parts])
            parts = [total.astype(jnp.bfloat16)]
        radix = min(4, size // stride)
        mine = parts[0]
        for hop in range(1, radix):
            pairs = [
                (i, i - i % (stride * radix) + (i + hop * stride) % (stride * radix))
                for i in range(size)
            ]
            parts.append(lax.ppermute(mine, "tensor", pairs))
        stride *= radix
    return parts


def gather_rows(block, t_size, r_size):
    t = lax.axis_index("tensor")
    distance = 1
    while distance < max(1, t_size // r_size):
        other = swap(block, "tensor", t_size, distance)
        block = jnp.where(
            (t & distance) == 0,
            jnp.concatenate([block, other], axis=1),
            jnp.concatenate([other, block], axis=1),
        )
        distance *= 2
    return block


def spread_steps(t_size, r_size):
    distance, steps = t_size // 2, []
    while distance >= max(1, t_size // r_size):
        steps.append(distance)
        distance //= 2
    return steps


def spread(block, distance, t_size, r_size, ties=()):
    many = max(1, t_size // r_size)
    after = [d for d in spread_steps(t_size, r_size) if d <= distance]
    rest = functools.reduce(lambda a, b: a | b, after)
    pairs = []
    for r in range(r_size):
        root = r * t_size // r_size
        for t in range(t_size):
            if (t ^ root) & rest == 0:
                pairs.append((t * r_size + r, (t ^ distance) * r_size + r))
    came = lax.ppermute(block, ("tensor", "replica"), pairs)

    def kernel(came, block, out):
        t, r = lax.axis_index("tensor"), lax.axis_index("replica")
        takes = ((t ^ (r * t_size // r_size)) & rest) == distance

        @pl.when(takes)
        def _():
            out[...] = came[...]

        @pl.when(jnp.logical_not(takes))
        def _():
            out[...] = block[...]

    return local(kernel, "spread", [vmem(*block.shape)], ins=(came, block), ties=ties)[0]


def row_pieces(pieces, t_size, r_size):
    many, parts = max(1, t_size // r_size), max(1, r_size // t_size)
    if parts > 1:
        block = jnp.concatenate(pieces, axis=1)
        size = block.shape[1] // parts
        spot = (lax.axis_index("replica") % parts) * size
        return [lax.dynamic_slice_in_dim(block, spot, size, 1)]
    if many == 1:
        return pieces
    size = pieces[0].shape[1] // many
    return [x[:, i * size : (i + 1) * size] for i in range(many) for x in pieces]


def per_device(
    acts,
    cots,
    down_factor,
    up_factor,
    down_first_moment,
    down_second_moment,
    up_first_moment,
    up_second_moment,
    rollout_weight,
    owner,
    projection_index,
):
    t_size, r_size = lax.axis_size("tensor"), lax.axis_size("replica")
    turn = lambda x: jnp.transpose(x, (0, 2, 1))
    down_state = tuple(map(turn, (down_factor, down_first_moment, down_second_moment)))
    up_state = (up_factor, up_first_moment, up_second_moment)
    coefficient = adapter_scale / (acts.shape[1] * r_size)
    down_half = functools.partial(down_parity, t_size=t_size, r_size=r_size)
    up_half = functools.partial(up_parity, t_size=t_size, r_size=r_size)
    exchange = lambda x, distance: swap(x, "replica", r_size, distance)
    pieces = 4
    piece = rollout_weight.shape[0] // pieces
    weight = lambda i, tie: load(rollout_weight, i * piece, piece, tie)

    low, acts_in, cots_in = low_parts(acts, cots, down_state[0], up_state[0])
    down_chosen, up_chosen, flags = chosen_state(
        down_state, up_state, projection_index, owner, t_size, r_size, low
    )
    lows = tensor_sum_parts(low, t_size)
    (up_send,), (up_own,) = gradient_parts(lows, cots_in, flags, 2, coefficient, up_half, 1)
    up_came = exchange(up_send, 1)
    cuts = 2
    down_send, down_own = gradient_parts(
        lows, acts_in, flags, 0, coefficient, down_half, cuts, ties=(up_send,)
    )
    weights = [weight(0, down_send[0])]
    up_own, *down_send = join((up_own, up_came), ties=(weights[0][1],), passed=down_send)
    up_came, distance = exchange(up_own, 2), 4
    down_came = [exchange(x, 1) for x in down_send]
    weights += [weight(i, up_own) for i in range(1, pieces)]
    while distance < r_size:
        (up_own,) = join((up_own, up_came))
        up_came, distance = exchange(up_own, distance), 2 * distance
    tokens = [token for _, token in weights[1:]]
    up_own, *down_own = join((up_own, up_came), *zip(down_own, down_came), ties=tokens)
    up_other = exchange(up_own, 1)
    down_came, distance = [exchange(x, 2) for x in down_own], 4
    while distance < r_size:
        down_own = list(join(*zip(down_own, down_came)))
        down_came, distance = [exchange(x, distance) for x in down_own], 2 * distance

    up_mine = chosen_factor(up_chosen, up_own, up_other, flags, up_half, ties=(down_came[0],))
    held, distance = [up_mine], t_size // 2
    while distance > 1:
        held = held + [swap(x, "tensor", t_size, distance) for x in held]
        distance //= 2
    fresh_up = adam(up_state, [up_own], [up_other], flags, up_half, ties=(up_mine,))
    offered = offer(held, flags, t_size, after=(fresh_up[0],))
    held = held + [swap(offered, "tensor", t_size, 1)]

    rows, down_other, order = [], [], (up_mine, offered)
    size = down_own[0].shape[1]
    for i in range(cuts):
        (own,) = join((down_own[i], down_came[i]), ties=(order[i],))
        mine = chosen_factor(down_chosen, own, own, flags, down_half, start=i * size)
        down_own[i] = own
        down_other.append(exchange(own, 1))
        block = gather_rows(mine, t_size, r_size)
        for distance in spread_steps(t_size, r_size):
            block = spread(block, distance, t_size, r_size, ties=(held[-1],) if i else ())
        rows.append(block)
    fresh_rollout_weight = refresh(
        row_pieces(rows, t_size, r_size), held, flags, [w for w, _ in weights], t_size
    )
    fresh_down = adam(
        down_state, down_own, down_other, flags, down_half, after=(fresh_rollout_weight,)
    )
    return (
        turn(fresh_down[0]),
        fresh_up[0],
        turn(fresh_down[1]),
        turn(fresh_down[2]),
        fresh_up[1],
        fresh_up[2],
        fresh_rollout_weight,
    )


def solution(mesh):
    placed = (
        P(None, ("groups", "replica"), "tensor"),
        P(None, ("groups", "replica"), "tensor"),
        P("groups", "tensor", None),
        P("groups", None, "tensor"),
        P("groups", "tensor", None),
        P("groups", "tensor", None),
        P("groups", None, "tensor"),
        P("groups", None, "tensor"),
        P("replica", "tensor"),
        P(),
        P("groups"),
    )
    return jax.shard_map(
        per_device,
        mesh=mesh,
        in_specs=placed,
        out_specs=(
            P("groups", "tensor", None),
            P("groups", None, "tensor"),
            P("groups", "tensor", None),
            P("groups", "tensor", None),
            P("groups", None, "tensor"),
            P("groups", None, "tensor"),
            P(("groups", "replica"), "tensor"),
        ),
        check_vma=False,
    )
```

```python
import functools

import jax
import jax.numpy as jnp
from jax import lax
from jax.experimental import pallas as pl
from jax.experimental.pallas import tpu as pltpu
from jax.sharding import PartitionSpec as P

adapter_scale = 2.0
learn_rate = 0.05
beta_one = 0.9
beta_two = 0.999
adam_eps = 1e-08
fix_one = 1.0 - 0.9**10
fix_two = 1.0 - 0.999**10

MIB = 1024 * 1024
FLAGS = ("proj", "column_proj", "mine", "partners")


def moment_update(param, first, second, grad):
    first_new = beta_one * first + (1.0 - beta_one) * grad
    second_new = beta_two * second + (1.0 - beta_two) * grad * grad
    size = second_new * (1.0 / fix_two)
    param_new = param - (learn_rate / fix_one) * first_new / (size * lax.rsqrt(size) + adam_eps)
    return (param_new, first_new, second_new)


def f32(x):
    return x.astype(jnp.float32)


def swap(x, axis, size, distance):
    return lax.ppermute(x, axis, [(i, i ^ distance) for i in range(size)])


def vmem(*shape, dtype=jnp.bfloat16):
    return pltpu.VMEM(shape, dtype)


def local(kernel, name, outs, ins=(), hbm=(), smem=(), ties=(), after=(), passed=(), scratch=()):
    n_ins, n_first = len(ins), len(ins) + len(hbm) + len(smem)
    n_outs = len(outs)

    def body(*refs):
        front = refs[:n_first]
        rest = refs[n_first + len(ties) + len(after) + len(passed) :]
        kernel(*front, *rest[:n_outs], *rest[n_outs + len(passed) :])

    operands = (
        [pltpu.with_memory_space_constraint(x, pltpu.VMEM) for x in ins]
        + [pltpu.with_memory_space_constraint(x, pltpu.HBM) for x in hbm]
        + [pltpu.with_memory_space_constraint(x, pltpu.HBM) for x in smem]
        + [pltpu.with_memory_space_constraint(x, pltpu.VMEM) for x in ties]
        + [pltpu.with_memory_space_constraint(x, pltpu.HBM) for x in after]
        + [pltpu.with_memory_space_constraint(x, pltpu.VMEM) for x in passed]
    )
    specs = (
        [pl.BlockSpec(memory_space=pltpu.VMEM)] * n_ins
        + [pl.BlockSpec(memory_space=pltpu.HBM)] * len(hbm)
        + [pl.BlockSpec(memory_space=pltpu.SMEM)] * len(smem)
        + [pl.BlockSpec(memory_space=pl.ANY)] * (len(ties) + len(after) + len(passed))
    )
    first_passed = n_first + len(ties) + len(after)
    return pl.pallas_call(
        body,
        in_specs=specs,
        out_specs=[pl.BlockSpec(memory_space=pltpu.VMEM)] * n_outs
        + [pl.BlockSpec(memory_space=pl.ANY)] * len(passed),
        out_shape=list(outs) + [pltpu.VMEM(x.shape, x.dtype) for x in passed],
        input_output_aliases={first_passed + i: n_outs + i for i in range(len(passed))},
        scratch_shapes=list(scratch),
        compiler_params=pltpu.CompilerParams(vmem_limit_bytes=8 * MIB),
        cost_estimate=pl.CostEstimate(flops=0, bytes_accessed=1024, transcendentals=0),
        name=name,
    )(*operands)


def low_parts(acts, cots, down, up):
    tokens = acts.shape[1]
    rank = down.shape[1]

    def kernel(acts, cots, down, up, low, acts_in, cots_in, down_in, up_in, sems):
        jobs = []
        for spot, (x, x_in, f, f_in) in enumerate(
            ((cots, cots_in, up, up_in), (acts, acts_in, down, down_in))
        ):
            for p in range(2):
                i = 2 * spot + p
                pair = (
                    pltpu.make_async_copy(x.at[p], x_in.at[p], sems.at[2 * i]),
                    pltpu.make_async_copy(f.at[p], f_in.at[p], sems.at[2 * i + 1]),
                )
                for copy in pair:
                    copy.start()
                jobs.append((pair, x_in, f_in, p, i))
        for pair, x_in, f_in, p, i in jobs:
            for copy in pair:
                copy.wait()
            part = lax.dot_general(
                x_in[p],
                f_in[p].astype(jnp.bfloat16),
                (((1,), (1,)), ((), ())),
                preferred_element_type=jnp.float32,
            )
            low[pl.ds(i * rank, rank), :] = part.T.astype(low.dtype)

    return local(
        kernel,
        "low_parts",
        [vmem(4 * rank, tokens), vmem(*acts.shape), vmem(*cots.shape)],
        hbm=(acts, cots, down, up),
        scratch=[
            vmem(*down.shape, dtype=jnp.float32),
            vmem(*up.shape, dtype=jnp.float32),
            pltpu.SemaphoreType.DMA((8,)),
        ],
    )


def chosen_state(down_state, up_state, projection_index, owner, t_size, r_size, tie):
    rank, width = down_state[0].shape[1:]

    def kernel(*refs):
        sources, (index, owner), (down_out, up_out, flags, sems) = refs[:6], refs[6:8], refs[8:]
        t, r = lax.axis_index("tensor"), lax.axis_index("replica")
        proj = index[r]
        copies = []
        for i, source in enumerate(sources):
            target = (down_out if i < 3 else up_out).at[i % 3]
            copies.append(pltpu.make_async_copy(source.at[proj], target, sems.at[i]))
            copies[-1].start()
        values = (proj, index[t * r_size // t_size], owner[t], owner[t ^ 1])
        for i, value in enumerate(values):
            flags[pl.ds(i * rank, rank), :] = jnp.full((rank, 128), value, jnp.int32)
        for copy in copies:
            copy.wait()

    state = vmem(3, rank, width, dtype=jnp.float32)
    return local(
        kernel,
        "chosen_state",
        [state, state, vmem(len(FLAGS) * rank, 128, dtype=jnp.int32)],
        hbm=(*down_state, *up_state),
        smem=(projection_index, owner),
        ties=(tie,),
        scratch=[pltpu.SemaphoreType.DMA((6,))],
    )


def flag(flags, name, rank):
    return flags[pl.ds(FLAGS.index(name) * rank, rank), :]


def column_tiles(width):
    return [pl.ds(k, 128) for k in range(0, width, 128)]


def down_parity(flags, rank, t_size, r_size):
    t, r = lax.axis_index("tensor"), lax.axis_index("replica")
    return flag(flags, "column_proj", rank) ^ ((r + t * r_size // t_size) % 2)


def up_parity(flags, rank, t_size, r_size):
    r = lax.axis_index("replica")
    return jnp.full((rank, 128), r % 2, jnp.int32)


def gradient_parts(lows, tokens, flags, base, coefficient, half, ties=()):
    rank = lows[0].shape[0] // 4
    width = tokens.shape[2]
    parts = len(lows)

    def kernel(*refs):
        lows, tokens, flags, (send, keep) = refs[:parts], refs[parts], refs[parts + 1 : -2], refs[-2:]
        rows = pl.ds(base * rank, 2 * rank)
        total = functools.reduce(jnp.add, [f32(x[rows, :]) for x in lows]).astype(jnp.bfloat16)
        kept = half(flags[0] if flags else None, rank) == 0
        cut = min(width, 512)
        for k in range(0, width, cut):
            grads = [
                coefficient
                * jnp.dot(
                    total[p * rank : (p + 1) * rank],
                    tokens[p, :, pl.ds(k, cut)],
                    preferred_element_type=jnp.float32,
                )
                for p in range(2)
            ]
            for j in range(0, cut, 128):
                first, second = [g[:, j : j + 128] for g in grads]
                tile = pl.ds(k + j, 128)
                keep[:, tile] = jnp.where(kept, first, second).astype(keep.dtype)
                send[:, tile] = jnp.where(kept, second, first).astype(send.dtype)

    return local(
        kernel,
        "gradient_parts",
        [vmem(rank, width), vmem(rank, width)],
        ins=(*lows, tokens, *flags),
        ties=ties,
    )


def join(*sums, ties=(), passed=()):
    terms = [x for group in sums for x in group]

    def kernel(*refs):
        refs, outs = list(refs[: len(terms)]), refs[len(terms) :]
        for group, out in zip(sums, outs):
            total = functools.reduce(jnp.add, [f32(refs.pop(0)[...]) for _ in group])
            out[...] = total.astype(out.dtype)

    return local(
        kernel, "join", [vmem(*g[0].shape) for g in sums], ins=terms, ties=ties, passed=passed
    )


def load(weight, row, count, tie):
    lanes = 4

    def kernel(weight, out, token, sems):
        token[...] = jnp.zeros_like(token)
        each = count // lanes
        copies = [
            pltpu.make_async_copy(
                weight.at[pl.ds(row + i * each, each), :], out.at[pl.ds(i * each, each), :], sems.at[i]
            )
            for i in range(lanes)
        ]
        for copy in copies:
            copy.start()
        for copy in copies:
            copy.wait()

    return local(
        kernel,
        "load",
        [vmem(count, weight.shape[1]), vmem(8, 128, dtype=jnp.float32)],
        hbm=(weight,),
        ties=(tie,),
        scratch=[pltpu.SemaphoreType.DMA((lanes,))],
    )


def chosen_factor(state, own, other, flags, half, ties=(), passed=()):
    rank, width = own[0].shape
    n_own, n_other = len(own), len(other)

    def total(refs, tile):
        return f32(functools.reduce(jnp.add, [f32(x[:, tile]) for x in refs]).astype(jnp.bfloat16))

    def kernel(*refs):
        state, own, other = refs[0], refs[1 : 1 + n_own], refs[1 + n_own : 1 + n_own + n_other]
        flags, out = refs[1 + n_own + n_other :]
        for tile in column_tiles(width):
            grad = total(own, tile)
            if other:
                mine = flag(flags, "proj", rank) == half(flags, rank)
                grad = jnp.where(mine, grad, total(other, tile))
            held = [state[i, :, tile] for i in range(3)]
            out[:, tile] = moment_update(*held, grad)[0].astype(out.dtype)

    return local(
        kernel,
        "chosen_factor",
        [vmem(rank, width)],
        ins=(state, *own, *other, flags),
        ties=ties,
        passed=passed,
    )


def adam_half(state, grad, flags, half, flip, outs=(), ties=(), after=()):
    rank, width = grad.shape
    cuts = max(1, width // 1024)
    cut = width // cuts
    n_after = len(ties) + len(after)

    def kernel(*refs):
        grad, flags, sources = refs[0], refs[1], refs[2:5]
        targets = refs[5 + n_after + len(outs) :][:3]
        held, fresh, in_sems, out_sems = refs[-4:]
        p = jnp.max(half(flags, rank)[0:1, :]) ^ flip
        spans = [pl.ds(k * cut, cut) for k in range(cuts)]
        reads = [
            [
                pltpu.make_async_copy(x.at[p, :, span], held.at[i, :, span], in_sems.at[k, i])
                for i, x in enumerate(sources)
            ]
            for k, span in enumerate(spans)
        ]
        writes = [
            [
                pltpu.make_async_copy(fresh.at[i, :, span], x.at[p, :, span], out_sems.at[k, i])
                for i, x in enumerate(targets)
            ]
            for k, span in enumerate(spans)
        ]
        for group in reads:
            for copy in group:
                copy.start()
        for k in range(cuts):
            for copy in reads[k]:
                copy.wait()
            for j in range(k * cut, (k + 1) * cut, 128):
                tile = pl.ds(j, 128)
                values = moment_update(*[held[i, :, tile] for i in range(3)], f32(grad[:, tile]))
                for i, value in enumerate(values):
                    fresh[i, :, tile] = value
            for copy in writes[k]:
                copy.start()
        for group in writes:
            for copy in group:
                copy.wait()

    in_vmem, in_hbm = (grad, flags), (*state,)
    first = 5 + n_after
    whole = jax.ShapeDtypeStruct(state[0].shape, jnp.float32)
    return pl.pallas_call(
        kernel,
        in_specs=[pl.BlockSpec(memory_space=pltpu.VMEM)] * 2
        + [pl.BlockSpec(memory_space=pltpu.HBM)] * 3
        + [pl.BlockSpec(memory_space=pl.ANY)] * n_after
        + [pl.BlockSpec(memory_space=pltpu.HBM)] * len(outs),
        out_specs=[pl.BlockSpec(memory_space=pltpu.HBM)] * 3,
        out_shape=[pltpu.HBM(whole.shape, whole.dtype)] * 3,
        input_output_aliases={first + i: i for i in range(len(outs))},
        scratch_shapes=[
            vmem(3, rank, width, dtype=jnp.float32),
            vmem(3, rank, width, dtype=jnp.float32),
            pltpu.SemaphoreType.DMA((cuts, 3)),
            pltpu.SemaphoreType.DMA((cuts, 3)),
        ],
        compiler_params=pltpu.CompilerParams(vmem_limit_bytes=8 * MIB),
        cost_estimate=pl.CostEstimate(flops=0, bytes_accessed=1024, transcendentals=0),
        name="adam_half",
    )(
        *[pltpu.with_memory_space_constraint(x, pltpu.VMEM) for x in in_vmem],
        *[pltpu.with_memory_space_constraint(x, pltpu.HBM) for x in in_hbm],
        *[pltpu.with_memory_space_constraint(x, pltpu.VMEM) for x in ties],
        *[pltpu.with_memory_space_constraint(x, pltpu.HBM) for x in after],
        *[pltpu.with_memory_space_constraint(x, pltpu.HBM) for x in outs],
    )


def pick(flags, name, held, ids, rank):
    wanted = flag(flags, name, rank)

    def tile_of(tile):
        found = f32(held[0][:, tile])
        for i in range(1, len(held)):
            found = jnp.where(wanted == ids[i], f32(held[i][:, tile]), found)
        return found

    return tile_of


def block_ids(t_size, many):
    t = lax.axis_index("tensor")
    ids, distance = [t], t_size // 2
    while distance > 1:
        ids = ids + [i ^ distance for i in ids]
        distance //= 2
    return ids[:many]


def offer(held, flags, t_size, after=()):
    rank, width = held[0].shape

    def kernel(*refs):
        held, flags, out = refs[:-2], refs[-2], refs[-1]
        tile_of = pick(flags, "partners", held, block_ids(t_size, len(held)), rank)
        for tile in column_tiles(width):
            out[:, tile] = tile_of(tile).astype(out.dtype)

    return local(
        kernel, "offer", [vmem(rank, width)], ins=(*held, flags), after=after
    )[0]


def refresh(rows, held, flags, weights, t_size, after=()):
    rank, width = held[0].shape
    height = sum(w.shape[0] for w in weights)
    block = min(weights[0].shape[0], 256)
    each = weights[0].shape[0] // block
    n_rows, n_held, n_weights = len(rows), len(held), len(weights)
    piece = rows[0].shape[1]
    n_first = n_rows + n_held + 1

    def kernel(*refs):
        rows, held, flags = refs[:n_rows], refs[n_rows : n_rows + n_held], refs[n_first - 1]
        weights, (out, cols, left) = refs[n_first : n_first + n_weights], refs[-3:]
        step = pl.program_id(0)

        @pl.when(step == 0)
        def _():
            ids = block_ids(t_size, n_held - 1)
            tile_of = pick(flags, "mine", (held[-1], *held[:-1]), (None, *ids), rank)
            for tile in column_tiles(width):
                cols[:, tile] = (adapter_scale * tile_of(tile)).astype(cols.dtype)
            for j in range(0, height, 128):
                left[pl.ds(j, 128), :] = rows[j // piece][:, pl.ds(j % piece, 128)].T

        start = pl.multiple_of((step % each) * block, block)
        tall, wide = min(block, 128), min(width, 256)
        for i, weight in enumerate(weights):

            @pl.when(step // each == i)
            def _():
                for k in range(0, width, wide):
                    span = pl.ds(k, wide)
                    for j in range(0, block, tall):
                        at = pl.ds(pl.multiple_of(start + j, tall), tall)
                        from_top = pl.multiple_of(step * block + j, tall)
                        change = jnp.dot(
                            left[pl.ds(from_top, tall), :],
                            cols[:, span],
                            preferred_element_type=jnp.float32,
                        )
                        out[pl.ds(j, tall), span] = (f32(weight[at, span]) + change).astype(out.dtype)

    whole = pl.BlockSpec(memory_space=pltpu.VMEM)
    operands = (*rows, *held, flags, *weights)
    return pl.pallas_call(
        kernel,
        grid=(height // block,),
        in_specs=[whole] * len(operands) + [pl.BlockSpec(memory_space=pl.ANY)] * len(after),
        out_specs=pl.BlockSpec((block, width), lambda i: (i, 0)),
        out_shape=jax.ShapeDtypeStruct((height, width), weights[0].dtype),
        scratch_shapes=[vmem(rank, width), vmem(height, rank)],
        compiler_params=pltpu.CompilerParams(vmem_limit_bytes=12 * MIB),
        cost_estimate=pl.CostEstimate(flops=0, bytes_accessed=1024, transcendentals=0),
        name="refresh",
    )(
        *[pltpu.with_memory_space_constraint(x, pltpu.VMEM) for x in operands],
        *[pltpu.with_memory_space_constraint(x, pltpu.HBM) for x in after],
    )


def tensor_sum_parts(low, size):
    parts, stride = [low], 1
    while stride < size:
        if len(parts) > 1:
            total = functools.reduce(jnp.add, [f32(x) for x in parts])
            parts = [total.astype(jnp.bfloat16)]
        radix = min(4, size // stride)
        mine = parts[0]
        for hop in range(1, radix):
            pairs = [
                (i, i - i % (stride * radix) + (i + hop * stride) % (stride * radix))
                for i in range(size)
            ]
            parts.append(lax.ppermute(mine, "tensor", pairs))
        stride *= radix
    return parts


def toward(block, distance, t_size, r_size, first):
    pairs = []
    for t in range(t_size):
        root = t * r_size // t_size
        for r in range(r_size):
            same_side = ((r ^ root) & distance) == 0
            same_half = (r ^ root) % 2 == 0
            if (same_side != same_half) == first:
                pairs.append((t * r_size + r, t * r_size + (r ^ distance)))
    return lax.ppermute(block, ("tensor", "replica"), pairs)


def gather_rows(block, t_size, r_size):
    t = lax.axis_index("tensor")
    distance = 1
    while distance < max(1, t_size // r_size):
        other = swap(block, "tensor", t_size, distance)
        block = jnp.where(
            (t & distance) == 0,
            jnp.concatenate([block, other], axis=1),
            jnp.concatenate([other, block], axis=1),
        )
        distance *= 2
    return block


def spread_steps(t_size, r_size):
    distance, steps = t_size // 2, []
    while distance >= max(1, t_size // r_size):
        steps.append(distance)
        distance //= 2
    return steps


def spread(block, distance, t_size, r_size, ties=()):
    many = max(1, t_size // r_size)
    after = [d for d in spread_steps(t_size, r_size) if d <= distance]
    rest = functools.reduce(lambda a, b: a | b, after)
    pairs = []
    for r in range(r_size):
        root = r * t_size // r_size
        for t in range(t_size):
            if (t ^ root) & rest == 0:
                pairs.append((t * r_size + r, (t ^ distance) * r_size + r))
    came = lax.ppermute(block, ("tensor", "replica"), pairs)

    def kernel(came, block, out):
        t, r = lax.axis_index("tensor"), lax.axis_index("replica")
        takes = ((t ^ (r * t_size // r_size)) & rest) == distance

        @pl.when(takes)
        def _():
            out[...] = came[...]

        @pl.when(jnp.logical_not(takes))
        def _():
            out[...] = block[...]

    return local(kernel, "spread", [vmem(*block.shape)], ins=(came, block), ties=ties)[0]


def row_pieces(pieces, t_size, r_size):
    many, parts = max(1, t_size // r_size), max(1, r_size // t_size)
    if parts > 1:
        block = jnp.concatenate(pieces, axis=1)
        size = block.shape[1] // parts
        spot = (lax.axis_index("replica") % parts) * size
        return [lax.dynamic_slice_in_dim(block, spot, size, 1)]
    if many == 1:
        return pieces
    size = pieces[0].shape[1] // many
    return [x[:, i * size : (i + 1) * size] for i in range(many) for x in pieces]


def per_device(
    acts,
    cots,
    down_factor,
    up_factor,
    down_first_moment,
    down_second_moment,
    up_first_moment,
    up_second_moment,
    rollout_weight,
    owner,
    projection_index,
):
    t_size, r_size = lax.axis_size("tensor"), lax.axis_size("replica")
    turn = lambda x: jnp.transpose(x, (0, 2, 1))
    down_state = tuple(map(turn, (down_factor, down_first_moment, down_second_moment)))
    up_state = (up_factor, up_first_moment, up_second_moment)
    coefficient = adapter_scale / (acts.shape[1] * r_size)
    down_half = functools.partial(down_parity, t_size=t_size, r_size=r_size)
    up_half = functools.partial(up_parity, t_size=t_size, r_size=r_size)
    exchange = lambda x, distance: swap(x, "replica", r_size, distance)
    pieces = 4
    piece = rollout_weight.shape[0] // pieces
    weight = lambda i, tie: load(rollout_weight, i * piece, piece, tie)

    low, acts_in, cots_in = low_parts(acts, cots, down_state[0], up_state[0])
    weights = [weight(0, low)]
    lows = tensor_sum_parts(low, t_size)
    up_send, up_own = gradient_parts(
        lows, cots_in, (), 2, coefficient, up_half, ties=(weights[0][1],)
    )
    up_came = exchange(up_send, 1)
    down_chosen, up_chosen, flags = chosen_state(
        down_state, up_state, projection_index, owner, t_size, r_size, up_send
    )
    down_send, down_own = gradient_parts(lows, acts_in, (flags,), 0, coefficient, down_half)
    weights.append(weight(1, down_send))
    up_own, down_send = join((up_own, up_came), ties=(weights[1][1],), passed=(down_send,))
    up_came, distance = exchange(up_own, 2), 4
    down_came = exchange(down_send, 1)
    weights += [weight(i, up_own) for i in range(2, pieces)]
    while distance < r_size:
        (up_own,) = join((up_own, up_came))
        up_came, distance = exchange(up_own, distance), 2 * distance
    tokens = [token for _, token in weights[2:]]
    up_own, down_own = join((up_own, up_came), (down_own, down_came), ties=tokens)
    up_other = exchange(up_own, 1)
    distance = 2
    while 2 * distance < r_size:
        (down_own,) = join((down_own, exchange(down_own, distance)))
        distance *= 2
    down_first = toward(down_own, distance, t_size, r_size, True)

    up_mine, down_own = chosen_factor(
        up_chosen, [up_own], [up_other], flags, up_half, ties=(down_first,), passed=(down_own,)
    )
    held, shift = [up_mine], t_size // 2
    while shift > 1:
        held = held + [swap(x, "tensor", t_size, shift) for x in held]
        shift //= 2
    down_rest = toward(down_own, distance, t_size, r_size, False)
    (block,) = chosen_factor(
        down_chosen, [down_own, down_first], [], flags, down_half, ties=(up_mine,)
    )
    block = gather_rows(block, t_size, r_size)
    fresh_up = adam_half(up_state, up_own, flags, up_half, 0, ties=(block,))
    fresh_up = adam_half(up_state, up_other, flags, up_half, 1, outs=fresh_up)
    offered = offer(held, flags, t_size, after=(fresh_up[0],))
    held = held + [swap(offered, "tensor", t_size, 1)]
    for i, shift in enumerate(spread_steps(t_size, r_size)):
        block = spread(block, shift, t_size, r_size, ties=(held[-1],) if i else (offered,))
    (down_own,) = join((down_own, down_first, down_rest), ties=(offered,))
    down_other = exchange(down_own, 1)
    fresh_down = adam_half(down_state, down_own, flags, down_half, 0)
    fresh_rollout_weight = refresh(
        row_pieces([block], t_size, r_size),
        held,
        flags,
        [w for w, _ in weights],
        t_size,
        after=(fresh_down[0],),
    )
    fresh_down = adam_half(
        down_state,
        down_other,
        flags,
        down_half,
        1,
        outs=fresh_down,
        after=(fresh_rollout_weight,),
    )
    return (
        turn(fresh_down[0]),
        fresh_up[0],
        turn(fresh_down[1]),
        turn(fresh_down[2]),
        fresh_up[1],
        fresh_up[2],
        fresh_rollout_weight,
    )


def solution(mesh):
    placed = (
        P(None, ("groups", "replica"), "tensor"),
        P(None, ("groups", "replica"), "tensor"),
        P("groups", "tensor", None),
        P("groups", None, "tensor"),
        P("groups", "tensor", None),
        P("groups", "tensor", None),
        P("groups", None, "tensor"),
        P("groups", None, "tensor"),
        P("replica", "tensor"),
        P(),
        P("groups"),
    )
    return jax.shard_map(
        per_device,
        mesh=mesh,
        in_specs=placed,
        out_specs=(
            P("groups", "tensor", None),
            P("groups", None, "tensor"),
            P("groups", "tensor", None),
            P("groups", "tensor", None),
            P("groups", None, "tensor"),
            P("groups", None, "tensor"),
            P(("groups", "replica"), "tensor"),
        ),
        check_vma=False,
    )
```

```python
import functools

import jax
import jax.numpy as jnp
from jax import lax
from jax.experimental import pallas as pl
from jax.experimental.pallas import tpu as pltpu
from jax.sharding import PartitionSpec as P

adapter_scale = 2.0
learn_rate = 0.05
beta_one = 0.9
beta_two = 0.999
adam_eps = 1e-08
fix_one = 1.0 - 0.9**10
fix_two = 1.0 - 0.999**10

MIB = 1024 * 1024
FLAGS = ("proj", "column_proj", "mine", "partners")


def moment_update(param, first, second, grad):
    first_new = beta_one * first + (1.0 - beta_one) * grad
    second_new = beta_two * second + (1.0 - beta_two) * grad * grad
    size = second_new * (1.0 / fix_two)
    param_new = param - (learn_rate / fix_one) * first_new / (size * lax.rsqrt(size) + adam_eps)
    return (param_new, first_new, second_new)


def f32(x):
    return x.astype(jnp.float32)


def swap(x, axis, size, distance):
    return lax.ppermute(x, axis, [(i, i ^ distance) for i in range(size)])


def vmem(*shape, dtype=jnp.bfloat16):
    return pltpu.VMEM(shape, dtype)


def local(kernel, name, outs, ins=(), hbm=(), smem=(), ties=(), after=(), passed=(), scratch=(), work=1024):
    n_ins, n_first = len(ins), len(ins) + len(hbm) + len(smem)
    n_outs = len(outs)

    def body(*refs):
        front = refs[:n_first]
        rest = refs[n_first + len(ties) + len(after) + len(passed) :]
        kernel(*front, *rest[:n_outs], *rest[n_outs + len(passed) :])

    operands = (
        [pltpu.with_memory_space_constraint(x, pltpu.VMEM) for x in ins]
        + [pltpu.with_memory_space_constraint(x, pltpu.HBM) for x in hbm]
        + [pltpu.with_memory_space_constraint(x, pltpu.HBM) for x in smem]
        + [pltpu.with_memory_space_constraint(x, pltpu.VMEM) for x in ties]
        + [pltpu.with_memory_space_constraint(x, pltpu.HBM) for x in after]
        + [pltpu.with_memory_space_constraint(x, pltpu.VMEM) for x in passed]
    )
    specs = (
        [pl.BlockSpec(memory_space=pltpu.VMEM)] * n_ins
        + [pl.BlockSpec(memory_space=pltpu.HBM)] * len(hbm)
        + [pl.BlockSpec(memory_space=pltpu.SMEM)] * len(smem)
        + [pl.BlockSpec(memory_space=pl.ANY)] * (len(ties) + len(after) + len(passed))
    )
    first_passed = n_first + len(ties) + len(after)
    return pl.pallas_call(
        body,
        in_specs=specs,
        out_specs=[pl.BlockSpec(memory_space=pltpu.VMEM)] * n_outs
        + [pl.BlockSpec(memory_space=pl.ANY)] * len(passed),
        out_shape=list(outs) + [pltpu.VMEM(x.shape, x.dtype) for x in passed],
        input_output_aliases={first_passed + i: n_outs + i for i in range(len(passed))},
        scratch_shapes=list(scratch),
        compiler_params=pltpu.CompilerParams(vmem_limit_bytes=8 * MIB),
        cost_estimate=pl.CostEstimate(flops=0, bytes_accessed=work, transcendentals=0),
        name=name,
    )(*operands)


def low_parts(acts, cots, down, up):
    tokens = acts.shape[1]
    rank = down.shape[1]

    def kernel(acts, cots, down, up, low, acts_in, cots_in, down_in, up_in, sems):
        jobs = []
        for spot, (x, x_in, f, f_in) in enumerate(
            ((cots, cots_in, up, up_in), (acts, acts_in, down, down_in))
        ):
            for p in range(2):
                i = 2 * spot + p
                pair = (
                    pltpu.make_async_copy(x.at[p], x_in.at[p], sems.at[2 * i]),
                    pltpu.make_async_copy(f.at[p], f_in.at[p], sems.at[2 * i + 1]),
                )
                jobs.append((pair, x_in, f_in, p, i))
        for pair, *_ in jobs[:2]:
            for copy in pair:
                copy.start()
        for pair, x_in, f_in, p, i in jobs:
            for copy in pair:
                copy.wait()
            if i + 2 < len(jobs):
                for copy in jobs[i + 2][0]:
                    copy.start()
            part = lax.dot_general(
                x_in[p],
                f_in[p].astype(jnp.bfloat16),
                (((1,), (1,)), ((), ())),
                preferred_element_type=jnp.float32,
            )
            low[pl.ds(i * rank, rank), :] = part.T.astype(low.dtype)

    return local(
        kernel,
        "low_parts",
        [vmem(4 * rank, tokens), vmem(*acts.shape), vmem(*cots.shape)],
        hbm=(acts, cots, down, up),
        scratch=[
            vmem(*down.shape, dtype=jnp.float32),
            vmem(*up.shape, dtype=jnp.float32),
            pltpu.SemaphoreType.DMA((8,)),
        ],
    )


def chosen_state(down_state, up_state, projection_index, owner, t_size, r_size, tie):
    rank, width = down_state[0].shape[1:]

    def kernel(*refs):
        sources, (index, owner), (down_out, up_out, flags, sems) = refs[:6], refs[6:8], refs[8:]
        t, r = lax.axis_index("tensor"), lax.axis_index("replica")
        proj = index[r]
        copies = []
        for i, source in enumerate(sources):
            target = (down_out if i < 3 else up_out).at[i % 3]
            copies.append(pltpu.make_async_copy(source.at[proj], target, sems.at[i]))
            copies[-1].start()
        values = (proj, index[t * r_size // t_size], owner[t], owner[t ^ 1])
        for i, value in enumerate(values):
            flags[pl.ds(i * rank, rank), :] = jnp.full((rank, 128), value, jnp.int32)
        for copy in copies:
            copy.wait()

    state = vmem(3, rank, width, dtype=jnp.float32)
    return local(
        kernel,
        "chosen_state",
        [state, state, vmem(len(FLAGS) * rank, 128, dtype=jnp.int32)],
        hbm=(*down_state, *up_state),
        smem=(projection_index, owner),
        ties=(tie,),
        scratch=[pltpu.SemaphoreType.DMA((6,))],
    )


def flag(flags, name, rank):
    return flags[pl.ds(FLAGS.index(name) * rank, rank), :]


def column_tiles(width):
    return [pl.ds(k, 128) for k in range(0, width, 128)]


def down_parity(flags, rank, t_size, r_size):
    t, r = lax.axis_index("tensor"), lax.axis_index("replica")
    return flag(flags, "column_proj", rank) ^ ((r + t * r_size // t_size) % 2)


def up_parity(flags, rank, t_size, r_size):
    r = lax.axis_index("replica")
    return jnp.full((rank, 128), r % 2, jnp.int32)


def gradient_parts(lows, tokens, flags, base, coefficient, half, ties=()):
    rank = lows[0].shape[0] // 4
    width = tokens.shape[2]
    parts = len(lows)

    def kernel(*refs):
        lows, tokens, flags, (send, keep) = refs[:parts], refs[parts], refs[parts + 1 : -2], refs[-2:]
        rows = pl.ds(base * rank, 2 * rank)
        total = functools.reduce(jnp.add, [f32(x[rows, :]) for x in lows]).astype(jnp.bfloat16)
        kept = half(flags[0] if flags else None, rank) == 0
        cut = min(width, 512)
        for k in range(0, width, cut):
            grads = [
                coefficient
                * jnp.dot(
                    total[p * rank : (p + 1) * rank],
                    tokens[p, :, pl.ds(k, cut)],
                    preferred_element_type=jnp.float32,
                )
                for p in range(2)
            ]
            for j in range(0, cut, 128):
                first, second = [g[:, j : j + 128] for g in grads]
                tile = pl.ds(k + j, 128)
                keep[:, tile] = jnp.where(kept, first, second).astype(keep.dtype)
                send[:, tile] = jnp.where(kept, second, first).astype(send.dtype)

    return local(
        kernel,
        "gradient_parts",
        [vmem(rank, width), vmem(rank, width)],
        ins=(*lows, tokens, *flags),
        ties=ties,
    )


def join(*sums, ties=(), passed=()):
    terms = [x for group in sums for x in group]

    def kernel(*refs):
        refs, outs = list(refs[: len(terms)]), refs[len(terms) :]
        for group, out in zip(sums, outs):
            total = functools.reduce(jnp.add, [f32(refs.pop(0)[...]) for _ in group])
            out[...] = total.astype(out.dtype)

    return local(
        kernel, "join", [vmem(*g[0].shape) for g in sums], ins=terms, ties=ties, passed=passed
    )


def chosen_factor(state, own, other, flags, half, ties=(), after=(), passed=()):
    rank, width = own[0].shape
    n_own, n_other = len(own), len(other)

    def total(refs, tile):
        return f32(functools.reduce(jnp.add, [f32(x[:, tile]) for x in refs]).astype(jnp.bfloat16))

    def kernel(*refs):
        state, own, other = refs[0], refs[1 : 1 + n_own], refs[1 + n_own : 1 + n_own + n_other]
        flags, out = refs[1 + n_own + n_other :]
        for tile in column_tiles(width):
            grad = total(own, tile)
            if other:
                mine = flag(flags, "proj", rank) == half(flags, rank)
                grad = jnp.where(mine, grad, total(other, tile))
            held = [state[i, :, tile] for i in range(3)]
            out[:, tile] = moment_update(*held, grad)[0].astype(out.dtype)

    return local(
        kernel,
        "chosen_factor",
        [vmem(rank, width)],
        ins=(state, *own, *other, flags),
        ties=ties,
        after=after,
        passed=passed,
    )


def adam_half(state, grad, flags, half, flip, outs=(), ties=(), after=()):
    rank, width = grad.shape
    cuts = max(1, width // 1024)
    cut = width // cuts
    n_after = len(ties) + len(after)

    def kernel(*refs):
        grad, flags, sources = refs[0], refs[1], refs[2:5]
        targets = refs[5 + n_after + len(outs) :][:3]
        held, fresh, in_sems, out_sems = refs[-4:]
        p = jnp.max(half(flags, rank)[0:1, :]) ^ flip
        spans = [pl.ds(k * cut, cut) for k in range(cuts)]
        reads = [
            [
                pltpu.make_async_copy(x.at[p, :, span], held.at[i, :, span], in_sems.at[k, i])
                for i, x in enumerate(sources)
            ]
            for k, span in enumerate(spans)
        ]
        writes = [
            [
                pltpu.make_async_copy(fresh.at[i, :, span], x.at[p, :, span], out_sems.at[k, i])
                for i, x in enumerate(targets)
            ]
            for k, span in enumerate(spans)
        ]
        for group in reads:
            for copy in group:
                copy.start()
        for k in range(cuts):
            for copy in reads[k]:
                copy.wait()
            for j in range(k * cut, (k + 1) * cut, 128):
                tile = pl.ds(j, 128)
                values = moment_update(*[held[i, :, tile] for i in range(3)], f32(grad[:, tile]))
                for i, value in enumerate(values):
                    fresh[i, :, tile] = value
            for copy in writes[k]:
                copy.start()
        for group in writes:
            for copy in group:
                copy.wait()

    in_vmem, in_hbm = (grad, flags), (*state,)
    first = 5 + n_after
    whole = jax.ShapeDtypeStruct(state[0].shape, jnp.float32)
    return pl.pallas_call(
        kernel,
        in_specs=[pl.BlockSpec(memory_space=pltpu.VMEM)] * 2
        + [pl.BlockSpec(memory_space=pltpu.HBM)] * 3
        + [pl.BlockSpec(memory_space=pl.ANY)] * n_after
        + [pl.BlockSpec(memory_space=pltpu.HBM)] * len(outs),
        out_specs=[pl.BlockSpec(memory_space=pltpu.HBM)] * 3,
        out_shape=[pltpu.HBM(whole.shape, whole.dtype)] * 3,
        input_output_aliases={first + i: i for i in range(len(outs))},
        scratch_shapes=[
            vmem(3, rank, width, dtype=jnp.float32),
            vmem(3, rank, width, dtype=jnp.float32),
            pltpu.SemaphoreType.DMA((cuts, 3)),
            pltpu.SemaphoreType.DMA((cuts, 3)),
        ],
        compiler_params=pltpu.CompilerParams(vmem_limit_bytes=8 * MIB),
        cost_estimate=pl.CostEstimate(flops=0, bytes_accessed=1024, transcendentals=0),
        name="adam_half",
    )(
        *[pltpu.with_memory_space_constraint(x, pltpu.VMEM) for x in in_vmem],
        *[pltpu.with_memory_space_constraint(x, pltpu.HBM) for x in in_hbm],
        *[pltpu.with_memory_space_constraint(x, pltpu.VMEM) for x in ties],
        *[pltpu.with_memory_space_constraint(x, pltpu.HBM) for x in after],
        *[pltpu.with_memory_space_constraint(x, pltpu.HBM) for x in outs],
    )


def pick(flags, name, held, ids, rank):
    wanted = flag(flags, name, rank)

    def tile_of(tile):
        found = f32(held[0][:, tile])
        for i in range(1, len(held)):
            found = jnp.where(wanted == ids[i], f32(held[i][:, tile]), found)
        return found

    return tile_of


def block_ids(t_size, many):
    t = lax.axis_index("tensor")
    ids, distance = [t], t_size // 2
    while distance > 1:
        ids = ids + [i ^ distance for i in ids]
        distance //= 2
    return ids[:many]


def offer(held, flags, t_size, after=()):
    rank, width = held[0].shape

    def kernel(*refs):
        held, flags, out = refs[:-2], refs[-2], refs[-1]
        tile_of = pick(flags, "partners", held, block_ids(t_size, len(held)), rank)
        for tile in column_tiles(width):
            out[:, tile] = tile_of(tile).astype(out.dtype)

    return local(
        kernel, "offer", [vmem(rank, width)], ins=(*held, flags), after=after
    )[0]


def refresh(rows, held, flags, weights, t_size, after=()):
    rank, width = held[0].shape
    height = sum(w.shape[0] for w in weights)
    block = min(weights[0].shape[0], 256)
    each = weights[0].shape[0] // block
    n_rows, n_held, n_weights = len(rows), len(held), len(weights)
    piece = rows[0].shape[1]
    n_first = n_rows + n_held + 1

    def kernel(*refs):
        rows, held, flags = refs[:n_rows], refs[n_rows : n_rows + n_held], refs[n_first - 1]
        weights, (out, cols, left) = refs[n_first : n_first + n_weights], refs[-3:]
        step = pl.program_id(0)

        @pl.when(step == 0)
        def _():
            ids = block_ids(t_size, n_held - 1)
            tile_of = pick(flags, "mine", (held[-1], *held[:-1]), (None, *ids), rank)
            for tile in column_tiles(width):
                cols[:, tile] = (adapter_scale * tile_of(tile)).astype(cols.dtype)
            for j in range(0, height, 128):
                left[pl.ds(j, 128), :] = rows[j // piece][:, pl.ds(j % piece, 128)].T

        start = pl.multiple_of((step % each) * block, block)
        tall, wide = min(block, 128), min(width, 256)
        for i, weight in enumerate(weights):

            @pl.when(step // each == i)
            def _():
                for k in range(0, width, wide):
                    span = pl.ds(k, wide)
                    for j in range(0, block, tall):
                        at = pl.ds(pl.multiple_of(start + j, tall), tall)
                        from_top = pl.multiple_of(step * block + j, tall)
                        change = jnp.dot(
                            left[pl.ds(from_top, tall), :],
                            cols[:, span],
                            preferred_element_type=jnp.float32,
                        )
                        out[pl.ds(j, tall), span] = weight[at, span] + change.astype(out.dtype)

    whole = pl.BlockSpec(memory_space=pltpu.VMEM)
    operands = (*rows, *held, flags, *weights)
    return pl.pallas_call(
        kernel,
        grid=(height // block,),
        in_specs=[whole] * len(operands) + [pl.BlockSpec(memory_space=pl.ANY)] * len(after),
        out_specs=pl.BlockSpec((block, width), lambda i: (i, 0)),
        out_shape=jax.ShapeDtypeStruct((height, width), weights[0].dtype),
        scratch_shapes=[vmem(rank, width), vmem(height, rank)],
        compiler_params=pltpu.CompilerParams(vmem_limit_bytes=12 * MIB),
        cost_estimate=pl.CostEstimate(flops=0, bytes_accessed=1024, transcendentals=0),
        name="refresh",
    )(
        *[pltpu.with_memory_space_constraint(x, pltpu.VMEM) for x in operands],
        *[pltpu.with_memory_space_constraint(x, pltpu.HBM) for x in after],
    )


def tensor_sum_parts(low, size):
    parts, stride = [low], 1
    while stride < size:
        if len(parts) > 1:
            total = functools.reduce(jnp.add, [f32(x) for x in parts])
            parts = [total.astype(jnp.bfloat16)]
        radix = min(4, size // stride)
        mine = parts[0]
        for hop in range(1, radix):
            pairs = [
                (i, i - i % (stride * radix) + (i + hop * stride) % (stride * radix))
                for i in range(size)
            ]
            parts.append(lax.ppermute(mine, "tensor", pairs))
        stride *= radix
    return parts


def toward(block, distance, t_size, r_size, first):
    pairs = []
    for t in range(t_size):
        root = t * r_size // t_size
        for r in range(r_size):
            same_side = ((r ^ root) & distance) == 0
            same_half = (r ^ root) % 2 == 0
            if (same_side != same_half) == first:
                pairs.append((t * r_size + r, t * r_size + (r ^ distance)))
    return lax.ppermute(block, ("tensor", "replica"), pairs)


def gather_rows(block, t_size, r_size):
    t = lax.axis_index("tensor")
    distance = 1
    while distance < max(1, t_size // r_size):
        other = swap(block, "tensor", t_size, distance)
        block = jnp.where(
            (t & distance) == 0,
            jnp.concatenate([block, other], axis=1),
            jnp.concatenate([other, block], axis=1),
        )
        distance *= 2
    return block


def spread_steps(t_size, r_size):
    distance, steps = t_size // 2, []
    while distance >= max(1, t_size // r_size):
        steps.append(distance)
        distance //= 2
    return steps


def spread(block, distance, t_size, r_size, ties=()):
    many = max(1, t_size // r_size)
    after = [d for d in spread_steps(t_size, r_size) if d <= distance]
    rest = functools.reduce(lambda a, b: a | b, after)
    pairs = []
    for r in range(r_size):
        root = r * t_size // r_size
        for t in range(t_size):
            if (t ^ root) & rest == 0:
                pairs.append((t * r_size + r, (t ^ distance) * r_size + r))
    came = lax.ppermute(block, ("tensor", "replica"), pairs)

    def kernel(came, block, out):
        t, r = lax.axis_index("tensor"), lax.axis_index("replica")
        takes = ((t ^ (r * t_size // r_size)) & rest) == distance

        @pl.when(takes)
        def _():
            out[...] = came[...]

        @pl.when(jnp.logical_not(takes))
        def _():
            out[...] = block[...]

    return local(kernel, "spread", [vmem(*block.shape)], ins=(came, block), ties=ties)[0]


def row_pieces(pieces, t_size, r_size):
    many, parts = max(1, t_size // r_size), max(1, r_size // t_size)
    if parts > 1:
        block = jnp.concatenate(pieces, axis=1)
        size = block.shape[1] // parts
        spot = (lax.axis_index("replica") % parts) * size
        return [lax.dynamic_slice_in_dim(block, spot, size, 1)]
    if many == 1:
        return pieces
    size = pieces[0].shape[1] // many
    return [x[:, i * size : (i + 1) * size] for i in range(many) for x in pieces]


def per_device(
    acts,
    cots,
    down_factor,
    up_factor,
    down_first_moment,
    down_second_moment,
    up_first_moment,
    up_second_moment,
    rollout_weight,
    owner,
    projection_index,
):
    t_size, r_size = lax.axis_size("tensor"), lax.axis_size("replica")
    turn = lambda x: jnp.transpose(x, (0, 2, 1))
    down_state = tuple(map(turn, (down_factor, down_first_moment, down_second_moment)))
    up_state = (up_factor, up_first_moment, up_second_moment)
    coefficient = adapter_scale / (acts.shape[1] * r_size)
    down_half = functools.partial(down_parity, t_size=t_size, r_size=r_size)
    up_half = functools.partial(up_parity, t_size=t_size, r_size=r_size)
    exchange = lambda x, distance: swap(x, "replica", r_size, distance)

    low, acts_in, cots_in = low_parts(acts, cots, down_state[0], up_state[0])
    lows = tensor_sum_parts(low, t_size)
    up_send, up_own = gradient_parts(
        lows, cots_in, (), 2, coefficient, up_half,
    )
    up_came = exchange(up_send, 1)
    down_chosen, up_chosen, flags = chosen_state(
        down_state, up_state, projection_index, owner, t_size, r_size, up_send
    )
    down_send, down_own = gradient_parts(lows, acts_in, (flags,), 0, coefficient, down_half)
    up_own, down_send = join((up_own, up_came), passed=(down_send,))
    up_came, distance = exchange(up_own, 2), 4
    down_came = exchange(down_send, 1)
    while distance < r_size:
        (up_own,) = join((up_own, up_came))
        up_came, distance = exchange(up_own, distance), 2 * distance
    up_own, down_own = join((up_own, up_came), (down_own, down_came))
    up_other = exchange(up_own, 1)
    distance = 2
    while 2 * distance < r_size:
        (down_own,) = join((down_own, exchange(down_own, distance)))
        distance *= 2
    down_first = toward(down_own, distance, t_size, r_size, True)

    fresh_up = adam_half(up_state, up_own, flags, up_half, 0)
    up_mine, down_own = chosen_factor(
        up_chosen,
        [up_own],
        [up_other],
        flags,
        up_half,
        ties=(down_first,),
        after=(fresh_up[0],),
        passed=(down_own,),
    )
    held, shift = [up_mine], t_size // 2
    while shift > 1:
        held = held + [swap(x, "tensor", t_size, shift) for x in held]
        shift //= 2
    down_rest = toward(down_own, distance, t_size, r_size, False)
    (block,) = chosen_factor(
        down_chosen, [down_own, down_first], [], flags, down_half, ties=(up_mine,)
    )
    block = gather_rows(block, t_size, r_size)
    fresh_up = adam_half(up_state, up_other, flags, up_half, 1, outs=fresh_up, ties=(block,))
    offered = offer(held, flags, t_size, after=(fresh_up[0],))
    held = held + [swap(offered, "tensor", t_size, 1)]
    for i, shift in enumerate(spread_steps(t_size, r_size)):
        block = spread(block, shift, t_size, r_size, ties=(held[-1],) if i else (offered,))
    (down_own,) = join((down_own, down_first, down_rest), ties=(offered,))
    down_other = exchange(down_own, 1)
    fresh_down = adam_half(down_state, down_own, flags, down_half, 0)
    fresh_rollout_weight = refresh(
        row_pieces([block], t_size, r_size),
        held,
        flags,
        [rollout_weight],
        t_size,
        after=(fresh_down[0],),
    )
    fresh_down = adam_half(
        down_state,
        down_other,
        flags,
        down_half,
        1,
        outs=fresh_down,
        after=(fresh_rollout_weight,),
    )
    return (
        turn(fresh_down[0]),
        fresh_up[0],
        turn(fresh_down[1]),
        turn(fresh_down[2]),
        fresh_up[1],
        fresh_up[2],
        fresh_rollout_weight,
    )


def solution(mesh):
    placed = (
        P(None, ("groups", "replica"), "tensor"),
        P(None, ("groups", "replica"), "tensor"),
        P("groups", "tensor", None),
        P("groups", None, "tensor"),
        P("groups", "tensor", None),
        P("groups", "tensor", None),
        P("groups", None, "tensor"),
        P("groups", None, "tensor"),
        P("replica", "tensor"),
        P(),
        P("groups"),
    )
    return jax.shard_map(
        per_device,
        mesh=mesh,
        in_specs=placed,
        out_specs=(
            P("groups", "tensor", None),
            P("groups", None, "tensor"),
            P("groups", "tensor", None),
            P("groups", "tensor", None),
            P("groups", None, "tensor"),
            P("groups", None, "tensor"),
            P(("groups", "replica"), "tensor"),
        ),
        check_vma=False,
    )
```

```python
import functools

import jax
import jax.numpy as jnp
from jax import lax
from jax.experimental import pallas as pl
from jax.experimental.pallas import tpu as pltpu
from jax.sharding import PartitionSpec as P

adapter_scale = 2.0
learn_rate = 0.05
beta_one = 0.9
beta_two = 0.999
adam_eps = 1e-08
fix_one = 1.0 - 0.9**10
fix_two = 1.0 - 0.999**10

MIB = 1024 * 1024
FLAGS = ("proj", "column_proj", "mine", "partners")


def moment_update(param, first, second, grad):
    first_new = beta_one * first + (1.0 - beta_one) * grad
    second_new = beta_two * second + (1.0 - beta_two) * grad * grad
    size = second_new * (1.0 / fix_two)
    param_new = param - (learn_rate / fix_one) * first_new / (size * lax.rsqrt(size) + adam_eps)
    return (param_new, first_new, second_new)


def f32(x):
    return x.astype(jnp.float32)


def swap(x, axis, size, distance):
    return lax.ppermute(x, axis, [(i, i ^ distance) for i in range(size)])


def vmem(*shape, dtype=jnp.bfloat16):
    return pltpu.VMEM(shape, dtype)


def local(kernel, name, outs, ins=(), hbm=(), smem=(), ties=(), after=(), passed=(), scratch=(), work=1024):
    n_ins, n_first = len(ins), len(ins) + len(hbm) + len(smem)
    n_outs = len(outs)

    def body(*refs):
        front = refs[:n_first]
        rest = refs[n_first + len(ties) + len(after) + len(passed) :]
        kernel(*front, *rest[:n_outs], *rest[n_outs + len(passed) :])

    operands = (
        [pltpu.with_memory_space_constraint(x, pltpu.VMEM) for x in ins]
        + [pltpu.with_memory_space_constraint(x, pltpu.HBM) for x in hbm]
        + [pltpu.with_memory_space_constraint(x, pltpu.HBM) for x in smem]
        + [pltpu.with_memory_space_constraint(x, pltpu.VMEM) for x in ties]
        + [pltpu.with_memory_space_constraint(x, pltpu.HBM) for x in after]
        + [pltpu.with_memory_space_constraint(x, pltpu.VMEM) for x in passed]
    )
    specs = (
        [pl.BlockSpec(memory_space=pltpu.VMEM)] * n_ins
        + [pl.BlockSpec(memory_space=pltpu.HBM)] * len(hbm)
        + [pl.BlockSpec(memory_space=pltpu.SMEM)] * len(smem)
        + [pl.BlockSpec(memory_space=pl.ANY)] * (len(ties) + len(after) + len(passed))
    )
    first_passed = n_first + len(ties) + len(after)
    return pl.pallas_call(
        body,
        in_specs=specs,
        out_specs=[pl.BlockSpec(memory_space=pltpu.VMEM)] * n_outs
        + [pl.BlockSpec(memory_space=pl.ANY)] * len(passed),
        out_shape=list(outs) + [pltpu.VMEM(x.shape, x.dtype) for x in passed],
        input_output_aliases={first_passed + i: n_outs + i for i in range(len(passed))},
        scratch_shapes=list(scratch),
        compiler_params=pltpu.CompilerParams(vmem_limit_bytes=8 * MIB),
        cost_estimate=pl.CostEstimate(flops=0, bytes_accessed=work, transcendentals=0),
        name=name,
    )(*operands)


def low_parts(acts, cots, down, up):
    tokens = acts.shape[1]
    rank = down.shape[1]

    def kernel(acts, cots, down, up, low, acts_in, cots_in, down_in, up_in, sems):
        jobs = []
        for spot, (x, x_in, f, f_in) in enumerate(
            ((cots, cots_in, up, up_in), (acts, acts_in, down, down_in))
        ):
            for p in range(2):
                i = 2 * spot + p
                pair = (
                    pltpu.make_async_copy(x.at[p], x_in.at[p], sems.at[2 * i]),
                    pltpu.make_async_copy(f.at[p], f_in.at[p], sems.at[2 * i + 1]),
                )
                for copy in pair:
                    copy.start()
                jobs.append((pair, x_in, f_in, p, i))
        for pair, x_in, f_in, p, i in jobs:
            for copy in pair:
                copy.wait()
            low[pl.ds(i * rank, rank), :] = lax.dot_general(
                f_in[p].astype(jnp.bfloat16),
                x_in[p],
                (((1,), (1,)), ((), ())),
                preferred_element_type=jnp.float32,
            ).astype(low.dtype)

    return local(
        kernel,
        "low_parts",
        [vmem(4 * rank, tokens), vmem(*acts.shape), vmem(*cots.shape)],
        hbm=(acts, cots, down, up),
        scratch=[
            vmem(*down.shape, dtype=jnp.float32),
            vmem(*up.shape, dtype=jnp.float32),
            pltpu.SemaphoreType.DMA((8,)),
        ],
    )


def chosen_state(down_state, up_state, projection_index, owner, t_size, r_size, tie):
    rank, width = down_state[0].shape[1:]

    def kernel(*refs):
        sources, (index, owner), (down_out, up_out, flags, sems) = refs[:6], refs[6:8], refs[8:]
        t, r = lax.axis_index("tensor"), lax.axis_index("replica")
        proj = index[r]
        copies = []
        for i, source in enumerate(sources):
            target = (down_out if i < 3 else up_out).at[i % 3]
            copies.append(pltpu.make_async_copy(source.at[proj], target, sems.at[i]))
            copies[-1].start()
        values = (proj, index[t * r_size // t_size], owner[t], owner[t ^ (t_size // 2)])
        for i, value in enumerate(values):
            flags[pl.ds(i * rank, rank), :] = jnp.full((rank, 128), value, jnp.int32)
        for copy in copies:
            copy.wait()

    state = vmem(3, rank, width, dtype=jnp.float32)
    return local(
        kernel,
        "chosen_state",
        [state, state, vmem(len(FLAGS) * rank, 128, dtype=jnp.int32)],
        hbm=(*down_state, *up_state),
        smem=(projection_index, owner),
        ties=(tie,),
        scratch=[pltpu.SemaphoreType.DMA((6,))],
    )


def flag(flags, name, rank):
    return flags[pl.ds(FLAGS.index(name) * rank, rank), :]


def column_tiles(width):
    return [pl.ds(k, 128) for k in range(0, width, 128)]


def down_parity(flags, rank, t_size, r_size):
    t, r = lax.axis_index("tensor"), lax.axis_index("replica")
    return flag(flags, "column_proj", rank) ^ ((r + t * r_size // t_size) % 2)


def up_parity(flags, rank, t_size, r_size):
    r = lax.axis_index("replica")
    return jnp.full((rank, 128), r % 2, jnp.int32)


def gradient_parts(lows, tokens, flags, base, coefficient, half, ties=()):
    rank = lows[0].shape[0] // 4
    width = tokens.shape[2]
    parts = len(lows)

    def kernel(*refs):
        lows, tokens, flags, (send, keep) = refs[:parts], refs[parts], refs[parts + 1 : -2], refs[-2:]
        rows = pl.ds(base * rank, 2 * rank)
        total = functools.reduce(jnp.add, [f32(x[rows, :]) for x in lows]).astype(jnp.bfloat16)
        kept = half(flags[0] if flags else None, rank) == 0
        cut = min(width, 512)
        for k in range(0, width, cut):
            grads = [
                coefficient
                * jnp.dot(
                    total[p * rank : (p + 1) * rank],
                    tokens[p, :, pl.ds(k, cut)],
                    preferred_element_type=jnp.float32,
                )
                for p in range(2)
            ]
            for j in range(0, cut, 128):
                first, second = [g[:, j : j + 128] for g in grads]
                tile = pl.ds(k + j, 128)
                keep[:, tile] = jnp.where(kept, first, second).astype(keep.dtype)
                send[:, tile] = jnp.where(kept, second, first).astype(send.dtype)

    return local(
        kernel,
        "gradient_parts",
        [vmem(rank, width), vmem(rank, width)],
        ins=(*lows, tokens, *flags),
        ties=ties,
    )


def join(*sums, ties=(), passed=()):
    terms = [x for group in sums for x in group]

    def kernel(*refs):
        refs, outs = list(refs[: len(terms)]), refs[len(terms) :]
        for group, out in zip(sums, outs):
            total = functools.reduce(jnp.add, [f32(refs.pop(0)[...]) for _ in group])
            out[...] = total.astype(out.dtype)

    return local(
        kernel, "join", [vmem(*g[0].shape) for g in sums], ins=terms, ties=ties, passed=passed
    )


def chosen_factor(state, own, other, flags, half, ties=(), after=(), passed=()):
    rank, width = own[0].shape
    n_own, n_other = len(own), len(other)

    def total(refs, tile):
        return f32(functools.reduce(jnp.add, [f32(x[:, tile]) for x in refs]).astype(jnp.bfloat16))

    def kernel(*refs):
        state, own, other = refs[0], refs[1 : 1 + n_own], refs[1 + n_own : 1 + n_own + n_other]
        flags, out = refs[1 + n_own + n_other :]
        for tile in column_tiles(width):
            grad = total(own, tile)
            if other:
                mine = flag(flags, "proj", rank) == half(flags, rank)
                grad = jnp.where(mine, grad, total(other, tile))
            held = [state[i, :, tile] for i in range(3)]
            out[:, tile] = moment_update(*held, grad)[0].astype(out.dtype)

    return local(
        kernel,
        "chosen_factor",
        [vmem(rank, width)],
        ins=(state, *own, *other, flags),
        ties=ties,
        after=after,
        passed=passed,
    )


def adam_half(state, grad, flags, half, flip, outs=(), ties=(), after=()):
    rank, width = grad.shape
    cuts = max(1, width // 1024)
    cut = width // cuts
    n_after = len(ties) + len(after)

    def kernel(*refs):
        grad, flags, sources = refs[0], refs[1], refs[2:5]
        targets = refs[5 + n_after + len(outs) :][:3]
        held, fresh, in_sems, out_sems = refs[-4:]
        p = jnp.max(half(flags, rank)[0:1, :]) ^ flip
        spans = [pl.ds(k * cut, cut) for k in range(cuts)]
        reads = [
            [
                pltpu.make_async_copy(x.at[p, :, span], held.at[i, :, span], in_sems.at[k, i])
                for i, x in enumerate(sources)
            ]
            for k, span in enumerate(spans)
        ]
        writes = [
            [
                pltpu.make_async_copy(fresh.at[i, :, span], x.at[p, :, span], out_sems.at[k, i])
                for i, x in enumerate(targets)
            ]
            for k, span in enumerate(spans)
        ]
        for group in reads:
            for copy in group:
                copy.start()
        for k in range(cuts):
            for copy in reads[k]:
                copy.wait()
            for j in range(k * cut, (k + 1) * cut, 128):
                tile = pl.ds(j, 128)
                values = moment_update(*[held[i, :, tile] for i in range(3)], f32(grad[:, tile]))
                for i, value in enumerate(values):
                    fresh[i, :, tile] = value
            for copy in writes[k]:
                copy.start()
        for group in writes:
            for copy in group:
                copy.wait()

    in_vmem, in_hbm = (grad, flags), (*state,)
    first = 5 + n_after
    whole = jax.ShapeDtypeStruct(state[0].shape, jnp.float32)
    return pl.pallas_call(
        kernel,
        in_specs=[pl.BlockSpec(memory_space=pltpu.VMEM)] * 2
        + [pl.BlockSpec(memory_space=pltpu.HBM)] * 3
        + [pl.BlockSpec(memory_space=pl.ANY)] * n_after
        + [pl.BlockSpec(memory_space=pltpu.HBM)] * len(outs),
        out_specs=[pl.BlockSpec(memory_space=pltpu.HBM)] * 3,
        out_shape=[pltpu.HBM(whole.shape, whole.dtype)] * 3,
        input_output_aliases={first + i: i for i in range(len(outs))},
        scratch_shapes=[
            vmem(3, rank, width, dtype=jnp.float32),
            vmem(3, rank, width, dtype=jnp.float32),
            pltpu.SemaphoreType.DMA((cuts, 3)),
            pltpu.SemaphoreType.DMA((cuts, 3)),
        ],
        compiler_params=pltpu.CompilerParams(vmem_limit_bytes=8 * MIB),
        cost_estimate=pl.CostEstimate(flops=0, bytes_accessed=1024, transcendentals=0),
        name="adam_half",
    )(
        *[pltpu.with_memory_space_constraint(x, pltpu.VMEM) for x in in_vmem],
        *[pltpu.with_memory_space_constraint(x, pltpu.HBM) for x in in_hbm],
        *[pltpu.with_memory_space_constraint(x, pltpu.VMEM) for x in ties],
        *[pltpu.with_memory_space_constraint(x, pltpu.HBM) for x in after],
        *[pltpu.with_memory_space_constraint(x, pltpu.HBM) for x in outs],
    )


def pick(flags, name, held, ids, rank):
    wanted = flag(flags, name, rank)

    def tile_of(tile):
        found = f32(held[0][:, tile])
        for i in range(1, len(held)):
            found = jnp.where(wanted == ids[i], f32(held[i][:, tile]), found)
        return found

    return tile_of


def block_ids(t_size, many):
    t = lax.axis_index("tensor")
    ids, distance = [t], 1
    while distance < t_size // 2:
        ids = ids + [i ^ distance for i in ids]
        distance *= 2
    return ids[:many]


def offer(held, flags, t_size, passed=()):
    rank, width = held[0].shape

    def kernel(*refs):
        held, flags, out = refs[:-2], refs[-2], refs[-1]
        tile_of = pick(flags, "partners", held, block_ids(t_size, len(held)), rank)
        for tile in column_tiles(width):
            out[:, tile] = tile_of(tile).astype(out.dtype)

    return local(kernel, "offer", [vmem(rank, width)], ins=(*held, flags), passed=passed)


def prepare(rows, held, flags, t_size):
    rank, width = held[0].shape
    n_rows, n_held = len(rows), len(held)
    piece = rows[0].shape[1]
    height = n_rows * piece

    def kernel(*refs):
        rows, held, flags, (left, cols) = refs[:n_rows], refs[n_rows:-3], refs[-3], refs[-2:]
        ids = block_ids(t_size, n_held - 1)
        tile_of = pick(flags, "mine", (held[-1], *held[:-1]), (None, *ids), rank)
        for tile in column_tiles(width):
            cols[:, tile] = (adapter_scale * tile_of(tile)).astype(cols.dtype)
        for j in range(0, height, 128):
            left[pl.ds(j, 128), :] = rows[j // piece][:, pl.ds(j % piece, 128)].T

    return local(
        kernel, "prepare", [vmem(height, rank), vmem(rank, width)], ins=(*rows, *held, flags)
    )


def refresh(left, cols, flags, weight, jobs):
    height, width = weight.shape
    rank = cols.shape[0]
    block = min(height, 256)
    steps = height // block
    slots = min(4, steps)
    chunks = max(1, width // 1024)
    cut, apart = width // chunks, max(1, (steps - 2) // chunks)
    turns = [min(2 + apart * k, steps - 1) for k in range(chunks)]
    n_jobs = len(jobs)
    given = [x for job in jobs for x in job[4]]

    def kernel(*refs):
        refs = list(refs)
        left, cols, flags, weight = refs[:4]
        grads, sources = refs[4 : 4 + n_jobs], refs[4 + n_jobs : 4 + 4 * n_jobs]
        refs = refs[4 + 4 * n_jobs + len(given) :]
        out, targets, (ring, sems) = refs[0], refs[1 : 1 + 3 * n_jobs], refs[1 + 3 * n_jobs :][:2]
        held, fresh, in_sems, out_sems = refs[3 + 3 * n_jobs :] if n_jobs else [None] * 4
        step = pl.program_id(0)
        slot = step % slots

        def emit(i):
            at = pl.ds(pl.multiple_of(i * block, block), block)
            return pltpu.make_async_copy(ring.at[i % slots], out.at[at, :], sems.at[i % slots])

        def moves(j, k, reads):
            _, _, half, flip, _ = jobs[j]
            p = jnp.max(half(flags, rank)[0:1, :]) ^ flip
            span = pl.ds(k * cut, cut)
            if reads:
                return [
                    pltpu.make_async_copy(
                        sources[3 * j + i].at[p, :, span], held.at[j, i, :, span], in_sems.at[j, k]
                    )
                    for i in range(3)
                ]
            return [
                pltpu.make_async_copy(
                    fresh.at[j, i, :, span], targets[3 * j + i].at[p, :, span], out_sems.at[j, k]
                )
                for i in range(3)
            ]

        @pl.when(step == 0)
        def _():
            for k in range(chunks):
                for j in range(n_jobs):
                    for copy in moves(j, k, True):
                        copy.start()

        @pl.when(step >= slots)
        def _():
            emit(step - slots).wait()

        tall, wide = min(block, 128), min(width, 256)
        for k in range(0, width, wide):
            span = pl.ds(k, wide)
            for j in range(0, block, tall):
                at = pl.ds(pl.multiple_of(step * block + j, tall), tall)
                change = jnp.dot(left[at, :], cols[:, span], preferred_element_type=jnp.float32)
                ring[slot, pl.ds(j, tall), span] = (f32(weight[at, span]) + change).astype(ring.dtype)
        emit(step).start()

        for chunk, turn in enumerate(turns):

            @pl.when(step == turn)
            def _():
                for j in range(n_jobs):
                    for copy in moves(j, chunk, True):
                        copy.wait()
                    for k in range(chunk * cut, (chunk + 1) * cut, 128):
                        tile = pl.ds(k, 128)
                        values = moment_update(
                            *[held[j, i, :, tile] for i in range(3)], f32(grads[j][:, tile])
                        )
                        for i, value in enumerate(values):
                            fresh[j, i, :, tile] = value
                    for copy in moves(j, chunk, False):
                        copy.start()

        @pl.when(step == steps - 1)
        def _():
            for i in range(steps - slots, steps):
                emit(i).wait()
            for k in range(chunks):
                for j in range(n_jobs):
                    for copy in moves(j, k, False):
                        copy.wait()

    in_vmem = (left, cols, flags, weight, *[job[1] for job in jobs])
    in_hbm = (*[x for job in jobs for x in job[0]], *given)
    outs = [pltpu.HBM((height, width), weight.dtype)]
    aliases, at = {}, len(in_vmem) + 3 * n_jobs
    for j, job in enumerate(jobs):
        outs += [pltpu.HBM(job[0][0].shape, jnp.float32)] * 3
        for i in range(len(job[4])):
            aliases[at] = 1 + 3 * j + i
            at += 1
    state = vmem(max(n_jobs, 1), 3, rank, width, dtype=jnp.float32)
    results = pl.pallas_call(
        kernel,
        grid=(steps,),
        in_specs=[pl.BlockSpec(memory_space=pltpu.VMEM)] * len(in_vmem)
        + [pl.BlockSpec(memory_space=pltpu.HBM)] * len(in_hbm),
        out_specs=[pl.BlockSpec(memory_space=pltpu.HBM)] * len(outs),
        out_shape=outs,
        input_output_aliases=aliases,
        scratch_shapes=[
            vmem(slots, block, width),
            pltpu.SemaphoreType.DMA((slots,)),
            state,
            state,
            pltpu.SemaphoreType.DMA((max(n_jobs, 1), chunks)),
            pltpu.SemaphoreType.DMA((max(n_jobs, 1), chunks)),
        ],
        compiler_params=pltpu.CompilerParams(vmem_limit_bytes=20 * MIB),
        cost_estimate=pl.CostEstimate(flops=0, bytes_accessed=1024, transcendentals=0),
        name="refresh",
    )(
        *[pltpu.with_memory_space_constraint(x, pltpu.VMEM) for x in in_vmem],
        *[pltpu.with_memory_space_constraint(x, pltpu.HBM) for x in in_hbm],
    )
    return results[0], [results[1 + 3 * j : 4 + 3 * j] for j in range(n_jobs)]


def tensor_sum_parts(low, size):
    parts, stride = [low], 1
    while stride < size:
        if len(parts) > 1:
            total = functools.reduce(jnp.add, [f32(x) for x in parts])
            parts = [total.astype(jnp.bfloat16)]
        radix = min(4, size // stride)
        mine = parts[0]
        for hop in range(1, radix):
            pairs = [
                (i, i - i % (stride * radix) + (i + hop * stride) % (stride * radix))
                for i in range(size)
            ]
            parts.append(lax.ppermute(mine, "tensor", pairs))
        stride *= radix
    return parts


def toward(block, distance, t_size, r_size, first):
    pairs = []
    for t in range(t_size):
        root = t * r_size // t_size
        for r in range(r_size):
            same_side = ((r ^ root) & distance) == 0
            same_half = (r ^ root) % 2 == 0
            if (same_side != same_half) == first:
                pairs.append((t * r_size + r, t * r_size + (r ^ distance)))
    return lax.ppermute(block, ("tensor", "replica"), pairs)


def gather_rows(block, t_size, r_size):
    t = lax.axis_index("tensor")
    distance = 1
    while distance < max(1, t_size // r_size):
        other = swap(block, "tensor", t_size, distance)
        block = jnp.where(
            (t & distance) == 0,
            jnp.concatenate([block, other], axis=1),
            jnp.concatenate([other, block], axis=1),
        )
        distance *= 2
    return block


def spread_steps(t_size, r_size):
    distance, steps = t_size // 2, []
    while distance >= max(1, t_size // r_size):
        steps.append(distance)
        distance //= 2
    return steps


def spread(block, distance, t_size, r_size, ties=()):
    many = max(1, t_size // r_size)
    after = [d for d in spread_steps(t_size, r_size) if d <= distance]
    rest = functools.reduce(lambda a, b: a | b, after)
    pairs = []
    for r in range(r_size):
        root = r * t_size // r_size
        for t in range(t_size):
            if (t ^ root) & rest == 0:
                pairs.append((t * r_size + r, (t ^ distance) * r_size + r))
    came = lax.ppermute(block, ("tensor", "replica"), pairs)

    def kernel(came, block, out):
        t, r = lax.axis_index("tensor"), lax.axis_index("replica")
        takes = ((t ^ (r * t_size // r_size)) & rest) == distance

        @pl.when(takes)
        def _():
            out[...] = came[...]

        @pl.when(jnp.logical_not(takes))
        def _():
            out[...] = block[...]

    return local(kernel, "spread", [vmem(*block.shape)], ins=(came, block), ties=ties)[0]


def row_pieces(pieces, t_size, r_size):
    many, parts = max(1, t_size // r_size), max(1, r_size // t_size)
    if parts > 1:
        block = jnp.concatenate(pieces, axis=1)
        size = block.shape[1] // parts
        spot = (lax.axis_index("replica") % parts) * size
        return [lax.dynamic_slice_in_dim(block, spot, size, 1)]
    if many == 1:
        return pieces
    size = pieces[0].shape[1] // many
    return [x[:, i * size : (i + 1) * size] for i in range(many) for x in pieces]


def per_device(
    acts,
    cots,
    down_factor,
    up_factor,
    down_first_moment,
    down_second_moment,
    up_first_moment,
    up_second_moment,
    rollout_weight,
    owner,
    projection_index,
):
    t_size, r_size = lax.axis_size("tensor"), lax.axis_size("replica")
    turn = lambda x: jnp.transpose(x, (0, 2, 1))
    down_state = tuple(map(turn, (down_factor, down_first_moment, down_second_moment)))
    up_state = (up_factor, up_first_moment, up_second_moment)
    coefficient = adapter_scale / (acts.shape[1] * r_size)
    down_half = functools.partial(down_parity, t_size=t_size, r_size=r_size)
    up_half = functools.partial(up_parity, t_size=t_size, r_size=r_size)
    exchange = lambda x, distance: swap(x, "replica", r_size, distance)

    low, acts_in, cots_in = low_parts(acts, cots, down_state[0], up_state[0])
    lows = tensor_sum_parts(low, t_size)
    up_send, up_own = gradient_parts(
        lows, cots_in, (), 2, coefficient, up_half,
    )
    up_came = exchange(up_send, 1)
    down_chosen, up_chosen, flags = chosen_state(
        down_state, up_state, projection_index, owner, t_size, r_size, up_send
    )
    down_send, down_own = gradient_parts(lows, acts_in, (flags,), 0, coefficient, down_half)
    up_own, down_send = join((up_own, up_came), passed=(down_send,))
    up_came, distance = exchange(up_own, 2), 4
    down_came = exchange(down_send, 1)
    while distance < r_size:
        (up_own,) = join((up_own, up_came))
        up_came, distance = exchange(up_own, distance), 2 * distance
    up_own, down_own = join((up_own, up_came), (down_own, down_came))
    up_other = exchange(up_own, 1)
    distance = 2
    while 2 * distance < r_size:
        (down_own,) = join((down_own, exchange(down_own, distance)))
        distance *= 2
    down_first = toward(down_own, distance, t_size, r_size, True)

    fresh_up = adam_half(up_state, up_own, flags, up_half, 0)
    up_mine, down_own = chosen_factor(
        up_chosen,
        [up_own],
        [up_other],
        flags,
        up_half,
        ties=(down_first,),
        after=(fresh_up[0],),
        passed=(down_own,),
    )
    held, shift = [up_mine], 1
    while shift < t_size // 2:
        held = held + [swap(x, "tensor", t_size, shift) for x in held]
        shift *= 2
    (block,) = chosen_factor(
        down_chosen, [down_own, down_first], [], flags, down_half, ties=(up_mine,)
    )
    block = gather_rows(block, t_size, r_size)
    offered, down_own = offer(held, flags, t_size, passed=(down_own,))
    held = held + [swap(offered, "tensor", t_size, t_size // 2)]
    down_rest = toward(down_own, distance, t_size, r_size, False)
    for shift in spread_steps(t_size, r_size):
        block = spread(block, shift, t_size, r_size, ties=(offered,))
    left, cols = prepare(row_pieces([block], t_size, r_size), held, flags, t_size)
    (down_own,) = join((down_own, down_first, down_rest), ties=(cols,))
    down_other = exchange(down_own, 1)
    up_job = (up_state, up_other, up_half, 1, fresh_up)
    down_job = (down_state, down_own, down_half, 0, ())
    fresh_rollout_weight, (fresh_up, fresh_down) = refresh(
        left, cols, flags, rollout_weight, [up_job, down_job]
    )
    fresh_down = adam_half(
        down_state,
        down_other,
        flags,
        down_half,
        1,
        outs=fresh_down,
        after=(fresh_rollout_weight,),
    )
    return (
        turn(fresh_down[0]),
        fresh_up[0],
        turn(fresh_down[1]),
        turn(fresh_down[2]),
        fresh_up[1],
        fresh_up[2],
        fresh_rollout_weight,
    )


def solution(mesh):
    placed = (
        P(None, ("groups", "replica"), "tensor"),
        P(None, ("groups", "replica"), "tensor"),
        P("groups", "tensor", None),
        P("groups", None, "tensor"),
        P("groups", "tensor", None),
        P("groups", "tensor", None),
        P("groups", None, "tensor"),
        P("groups", None, "tensor"),
        P("replica", "tensor"),
        P(),
        P("groups"),
    )
    return jax.shard_map(
        per_device,
        mesh=mesh,
        in_specs=placed,
        out_specs=(
            P("groups", "tensor", None),
            P("groups", None, "tensor"),
            P("groups", "tensor", None),
            P("groups", "tensor", None),
            P("groups", None, "tensor"),
            P("groups", None, "tensor"),
            P(("groups", "replica"), "tensor"),
        ),
        check_vma=False,
    )
```

```python
import functools

import jax
import jax.numpy as jnp
from jax import lax
from jax.experimental import pallas as pl
from jax.experimental.pallas import tpu as pltpu
from jax.sharding import PartitionSpec as P

adapter_scale = 2.0
learn_rate = 0.05
beta_one = 0.9
beta_two = 0.999
adam_eps = 1e-08
fix_one = 1.0 - 0.9**10
fix_two = 1.0 - 0.999**10

MIB = 1024 * 1024
FLAGS = ("proj", "column_proj", "mine", "partners")


def moment_update(param, first, second, grad):
    first_new = beta_one * first + (1.0 - beta_one) * grad
    second_new = beta_two * second + (1.0 - beta_two) * grad * grad
    size = second_new * (1.0 / fix_two)
    param_new = param - (learn_rate / fix_one) * first_new / (size * lax.rsqrt(size) + adam_eps)
    return (param_new, first_new, second_new)


def f32(x):
    return x.astype(jnp.float32)


def swap(x, axis, size, distance):
    return lax.ppermute(x, axis, [(i, i ^ distance) for i in range(size)])


def vmem(*shape, dtype=jnp.bfloat16):
    return pltpu.VMEM(shape, dtype)


def local(kernel, name, outs, ins=(), hbm=(), smem=(), ties=(), after=(), passed=(), scratch=(), work=1024):
    n_ins, n_first = len(ins), len(ins) + len(hbm) + len(smem)
    n_outs = len(outs)

    def body(*refs):
        front = refs[:n_first]
        rest = refs[n_first + len(ties) + len(after) + len(passed) :]
        kernel(*front, *rest[:n_outs], *rest[n_outs + len(passed) :])

    operands = (
        [pltpu.with_memory_space_constraint(x, pltpu.VMEM) for x in ins]
        + [pltpu.with_memory_space_constraint(x, pltpu.HBM) for x in hbm]
        + [pltpu.with_memory_space_constraint(x, pltpu.HBM) for x in smem]
        + [pltpu.with_memory_space_constraint(x, pltpu.VMEM) for x in ties]
        + [pltpu.with_memory_space_constraint(x, pltpu.HBM) for x in after]
        + [pltpu.with_memory_space_constraint(x, pltpu.VMEM) for x in passed]
    )
    specs = (
        [pl.BlockSpec(memory_space=pltpu.VMEM)] * n_ins
        + [pl.BlockSpec(memory_space=pltpu.HBM)] * len(hbm)
        + [pl.BlockSpec(memory_space=pltpu.SMEM)] * len(smem)
        + [pl.BlockSpec(memory_space=pl.ANY)] * (len(ties) + len(after) + len(passed))
    )
    first_passed = n_first + len(ties) + len(after)
    return pl.pallas_call(
        body,
        in_specs=specs,
        out_specs=[pl.BlockSpec(memory_space=pltpu.VMEM)] * n_outs
        + [pl.BlockSpec(memory_space=pl.ANY)] * len(passed),
        out_shape=list(outs) + [pltpu.VMEM(x.shape, x.dtype) for x in passed],
        input_output_aliases={first_passed + i: n_outs + i for i in range(len(passed))},
        scratch_shapes=list(scratch),
        compiler_params=pltpu.CompilerParams(vmem_limit_bytes=8 * MIB),
        cost_estimate=pl.CostEstimate(flops=0, bytes_accessed=work, transcendentals=0),
        name=name,
    )(*operands)


def low_parts(acts, cots, down, up):
    tokens = acts.shape[1]
    rank = down.shape[1]

    def kernel(acts, cots, down, up, low, acts_in, cots_in, down_in, up_in, sems):
        jobs = []
        for spot, (x, x_in, f, f_in) in enumerate(
            ((cots, cots_in, up, up_in), (acts, acts_in, down, down_in))
        ):
            for p in range(2):
                i = 2 * spot + p
                pair = (
                    pltpu.make_async_copy(x.at[p], x_in.at[p], sems.at[2 * i]),
                    pltpu.make_async_copy(f.at[p], f_in.at[p], sems.at[2 * i + 1]),
                )
                for copy in pair:
                    copy.start()
                jobs.append((pair, x_in, f_in, p, i))
        for pair, x_in, f_in, p, i in jobs:
            for copy in pair:
                copy.wait()
            low[pl.ds(i * rank, rank), :] = lax.dot_general(
                f_in[p].astype(jnp.bfloat16),
                x_in[p],
                (((1,), (1,)), ((), ())),
                preferred_element_type=jnp.float32,
            ).astype(low.dtype)

    return local(
        kernel,
        "low_parts",
        [vmem(4 * rank, tokens), vmem(*acts.shape), vmem(*cots.shape)],
        hbm=(acts, cots, down, up),
        scratch=[
            vmem(*down.shape, dtype=jnp.float32),
            vmem(*up.shape, dtype=jnp.float32),
            pltpu.SemaphoreType.DMA((8,)),
        ],
    )


def load_state(down_state, up_state, projection_index, owner, t_size, r_size, tie):
    rank = down_state[0].shape[1]

    def kernel(*refs):
        sources, (index, owner), targets, (flags, sems) = refs[:6], refs[6:8], refs[8:14], refs[14:]
        copies = [
            pltpu.make_async_copy(x, y, sems.at[i]) for i, (x, y) in enumerate(zip(sources, targets))
        ]
        for copy in copies:
            copy.start()
        t, r = lax.axis_index("tensor"), lax.axis_index("replica")
        values = (index[r], index[t * r_size // t_size], owner[t], owner[t ^ (t_size // 2)])
        for i, value in enumerate(values):
            flags[pl.ds(i * rank, rank), :] = jnp.full((rank, 128), value, jnp.int32)
        for copy in copies:
            copy.wait()

    *state, flags = local(
        kernel,
        "load_state",
        [vmem(*x.shape, dtype=jnp.float32) for x in (*down_state, *up_state)]
        + [vmem(len(FLAGS) * rank, 128, dtype=jnp.int32)],
        hbm=(*down_state, *up_state),
        smem=(projection_index, owner),
        ties=(tie,),
        scratch=[pltpu.SemaphoreType.DMA((6,))],
    )
    return state[:3], state[3:], flags


def flag(flags, name, rank):
    return flags[pl.ds(FLAGS.index(name) * rank, rank), :]


def column_tiles(width):
    return [pl.ds(k, 128) for k in range(0, width, 128)]


def down_parity(flags, rank, t_size, r_size):
    t, r = lax.axis_index("tensor"), lax.axis_index("replica")
    return flag(flags, "column_proj", rank) ^ ((r + t * r_size // t_size) % 2)


def up_parity(flags, rank, t_size, r_size):
    r = lax.axis_index("replica")
    return jnp.full((rank, 128), r % 2, jnp.int32)


def gradient_parts(lows, tokens, flags, base, coefficient, half, ties=()):
    rank = lows[0].shape[0] // 4
    width = tokens.shape[2]
    parts = len(lows)

    def kernel(*refs):
        lows, tokens, flags, (send, keep) = refs[:parts], refs[parts], refs[parts + 1 : -2], refs[-2:]
        rows = pl.ds(base * rank, 2 * rank)
        total = functools.reduce(jnp.add, [f32(x[rows, :]) for x in lows]).astype(jnp.bfloat16)
        kept = half(flags[0] if flags else None, rank) == 0
        cut = min(width, 512)
        for k in range(0, width, cut):
            grads = [
                coefficient
                * jnp.dot(
                    total[p * rank : (p + 1) * rank],
                    tokens[p, :, pl.ds(k, cut)],
                    preferred_element_type=jnp.float32,
                )
                for p in range(2)
            ]
            for j in range(0, cut, 128):
                first, second = [g[:, j : j + 128] for g in grads]
                tile = pl.ds(k + j, 128)
                keep[:, tile] = jnp.where(kept, first, second).astype(keep.dtype)
                send[:, tile] = jnp.where(kept, second, first).astype(send.dtype)

    return local(
        kernel,
        "gradient_parts",
        [vmem(rank, width), vmem(rank, width)],
        ins=(*lows, tokens, *flags),
        ties=ties,
    )


def join(*sums, ties=(), passed=()):
    terms = [x for group in sums for x in group]

    def kernel(*refs):
        refs, outs = list(refs[: len(terms)]), refs[len(terms) :]
        for group, out in zip(sums, outs):
            total = functools.reduce(jnp.add, [f32(refs.pop(0)[...]) for _ in group])
            out[...] = total.astype(out.dtype)

    return local(
        kernel, "join", [vmem(*g[0].shape) for g in sums], ins=terms, ties=ties, passed=passed
    )


def chosen_factor(state, own, other, flags, half, ties=(), after=(), passed=()):
    rank, width = own[0].shape
    n_own, n_other = len(own), len(other)

    def total(refs, tile):
        return f32(functools.reduce(jnp.add, [f32(x[:, tile]) for x in refs]).astype(jnp.bfloat16))

    def kernel(*refs):
        state, own, other = refs[:3], refs[3 : 3 + n_own], refs[3 + n_own : 3 + n_own + n_other]
        flags, out = refs[3 + n_own + n_other :]
        p = jnp.max(flag(flags, "proj", rank)[0:1, :])
        for tile in column_tiles(width):
            grad = total(own, tile)
            if other:
                mine = flag(flags, "proj", rank) == half(flags, rank)
                grad = jnp.where(mine, grad, total(other, tile))
            held = [x[p, :, tile] for x in state]
            out[:, tile] = moment_update(*held, grad)[0].astype(out.dtype)

    return local(
        kernel,
        "chosen_factor",
        [vmem(rank, width)],
        ins=(*state, *own, *other, flags),
        ties=ties,
        after=after,
        passed=passed,
    )


def adam(state, own, other, flags, half, ties=()):
    rank, width = own.shape
    cuts = max(1, width // 1024)
    cut = width // cuts

    def kernel(*refs):
        state, own, other, flags, outs, (fresh, sems) = refs[:3], *refs[3:6], refs[-5:-2], refs[-2:]
        kept = half(flags, rank)
        copies = []
        for k in range(cuts):
            for j in range(k * cut, (k + 1) * cut, 128):
                tile = pl.ds(j, 128)
                grads = f32(own[:, tile]), f32(other[:, tile])
                for p in range(2):
                    grad = jnp.where(kept == p, *grads)
                    values = moment_update(*[x[p, :, tile] for x in state], grad)
                    for i, value in enumerate(values):
                        fresh[i, p, :, tile] = value
            span = pl.ds(k * cut, cut)
            for i, x in enumerate(outs):
                copies.append(
                    pltpu.make_async_copy(fresh.at[i, :, :, span], x.at[:, :, span], sems.at[k, i])
                )
                copies[-1].start()
        for copy in copies:
            copy.wait()

    in_vmem = (*state, own, other, flags, *ties)
    return pl.pallas_call(
        kernel,
        in_specs=[pl.BlockSpec(memory_space=pltpu.VMEM)] * 6
        + [pl.BlockSpec(memory_space=pl.ANY)] * len(ties),
        out_specs=[pl.BlockSpec(memory_space=pltpu.HBM)] * 3,
        out_shape=[pltpu.HBM(x.shape, x.dtype) for x in state],
        scratch_shapes=[
            vmem(3, 2, rank, width, dtype=jnp.float32),
            pltpu.SemaphoreType.DMA((cuts, 3)),
        ],
        compiler_params=pltpu.CompilerParams(vmem_limit_bytes=8 * MIB),
        cost_estimate=pl.CostEstimate(flops=0, bytes_accessed=1024, transcendentals=0),
        name="adam",
    )(*[pltpu.with_memory_space_constraint(x, pltpu.VMEM) for x in in_vmem])


def adam_half(state, grad, flags, half, flip, outs, after):
    rank, width = grad.shape
    cuts = max(1, width // 1024)
    cut = width // cuts

    def kernel(*refs):
        grad, flags, state = refs[0], refs[1], refs[2:5]
        targets, (fresh, sems) = refs[-5:-2], refs[-2:]
        p = jnp.max(half(flags, rank)[0:1, :]) ^ flip
        copies = []
        for k in range(cuts):
            for j in range(k * cut, (k + 1) * cut, 128):
                tile = pl.ds(j, 128)
                values = moment_update(*[x[p, :, tile] for x in state], f32(grad[:, tile]))
                for i, value in enumerate(values):
                    fresh[i, :, tile] = value
            span = pl.ds(k * cut, cut)
            for i, x in enumerate(targets):
                copies.append(
                    pltpu.make_async_copy(fresh.at[i, :, span], x.at[p, :, span], sems.at[k, i])
                )
                copies[-1].start()
        for copy in copies:
            copy.wait()

    in_vmem, in_hbm = (grad, flags, *state), (*after, *outs)
    first = len(in_vmem) + len(after)
    return pl.pallas_call(
        kernel,
        in_specs=[pl.BlockSpec(memory_space=pltpu.VMEM)] * len(in_vmem)
        + [pl.BlockSpec(memory_space=pltpu.HBM)] * len(in_hbm),
        out_specs=[pl.BlockSpec(memory_space=pltpu.HBM)] * 3,
        out_shape=[pltpu.HBM(x.shape, x.dtype) for x in state],
        input_output_aliases={first + i: i for i in range(3)},
        scratch_shapes=[
            vmem(3, rank, width, dtype=jnp.float32),
            pltpu.SemaphoreType.DMA((cuts, 3)),
        ],
        compiler_params=pltpu.CompilerParams(vmem_limit_bytes=8 * MIB),
        cost_estimate=pl.CostEstimate(flops=0, bytes_accessed=1024, transcendentals=0),
        name="adam_half",
    )(
        *[pltpu.with_memory_space_constraint(x, pltpu.VMEM) for x in in_vmem],
        *[pltpu.with_memory_space_constraint(x, pltpu.HBM) for x in in_hbm],
    )


def pick(flags, name, held, ids, rank):
    wanted = flag(flags, name, rank)

    def tile_of(tile):
        found = f32(held[0][:, tile])
        for i in range(1, len(held)):
            found = jnp.where(wanted == ids[i], f32(held[i][:, tile]), found)
        return found

    return tile_of


def block_ids(t_size, many):
    t = lax.axis_index("tensor")
    ids, distance = [t], 1
    while distance < t_size // 2:
        ids = ids + [i ^ distance for i in ids]
        distance *= 2
    return ids[:many]


def offer(held, flags, t_size, passed=()):
    rank, width = held[0].shape

    def kernel(*refs):
        held, flags, out = refs[:-2], refs[-2], refs[-1]
        tile_of = pick(flags, "partners", held, block_ids(t_size, len(held)), rank)
        for tile in column_tiles(width):
            out[:, tile] = tile_of(tile).astype(out.dtype)

    return local(kernel, "offer", [vmem(rank, width)], ins=(*held, flags), passed=passed)


def prepare(block, came, held, flags, t_size, r_size):
    rank, width = held[0].shape
    n_came, n_held = len(came), len(held)
    height = block.shape[1]

    def kernel(*refs):
        block, came, held = refs[0], refs[1 : 1 + n_came], refs[1 + n_came : -3]
        flags, (left, cols) = refs[-3], refs[-2:]
        ids = block_ids(t_size, n_held - 1)
        tile_of = pick(flags, "mine", (held[-1], *held[:-1]), (None, *ids), rank)
        for tile in column_tiles(width):
            cols[:, tile] = (adapter_scale * tile_of(tile)).astype(cols.dtype)
        root = is_root(t_size, r_size)
        for j in range(0, height, 128):
            tile = pl.ds(j, 128)
            got = functools.reduce(jnp.add, [f32(x[:, tile]) for x in came])
            rows = jnp.where(root, f32(block[:, tile]), got).astype(left.dtype)
            left[tile, :] = rows.T

    return local(
        kernel, "prepare", [vmem(height, rank), vmem(rank, width)], ins=(block, *came, *held, flags)
    )


def refresh(left, cols, flags, weight, state, grad, half):
    height, width = weight.shape
    rank = cols.shape[0]
    block = min(height, 256)
    steps = height // block
    slots = min(4, steps)
    chunks = max(1, width // 1024)
    cut, apart = width // chunks, max(1, (steps - 2) // chunks)
    turns = [min(1 + apart * k, steps - 1) for k in range(chunks)]

    def kernel(*refs):
        left, cols, flags, weight, grad, *state = refs[:8]
        out, targets, (ring, sems, fresh, fresh_sems) = refs[8], refs[9:12], refs[12:]
        step = pl.program_id(0)
        slot = step % slots

        def emit(i):
            at = pl.ds(pl.multiple_of(i * block, block), block)
            return pltpu.make_async_copy(ring.at[i % slots], out.at[at, :], sems.at[i % slots])

        def writes(p, k):
            span = pl.ds(k * cut, cut)
            return [
                pltpu.make_async_copy(fresh.at[i, :, span], x.at[p, :, span], fresh_sems.at[i, k])
                for i, x in enumerate(targets)
            ]

        @pl.when(step >= slots)
        def _():
            emit(step - slots).wait()

        tall, wide = min(block, 128), min(width, 256)
        for k in range(0, width, wide):
            span = pl.ds(k, wide)
            for j in range(0, block, tall):
                at = pl.ds(pl.multiple_of(step * block + j, tall), tall)
                change = jnp.dot(left[at, :], cols[:, span], preferred_element_type=jnp.float32)
                ring[slot, pl.ds(j, tall), span] = (f32(weight[at, span]) + change).astype(ring.dtype)
        emit(step).start()

        for chunk, turn in enumerate(turns):

            @pl.when(step == turn)
            def _():
                p = jnp.max(half(flags, rank)[0:1, :])
                for k in range(chunk * cut, (chunk + 1) * cut, 128):
                    tile = pl.ds(k, 128)
                    values = moment_update(*[x[p, :, tile] for x in state], f32(grad[:, tile]))
                    for i, value in enumerate(values):
                        fresh[i, :, tile] = value
                for copy in writes(p, chunk):
                    copy.start()

        @pl.when(step == steps - 1)
        def _():
            p = jnp.max(half(flags, rank)[0:1, :])
            for k in range(chunks):
                for copy in writes(p, k):
                    copy.wait()
            for i in range(steps - slots, steps):
                emit(i).wait()

    operands = (left, cols, flags, weight, grad, *state)
    outs = [pltpu.HBM((height, width), weight.dtype)] + [pltpu.HBM(x.shape, x.dtype) for x in state]
    result, *fresh = pl.pallas_call(
        kernel,
        grid=(steps,),
        in_specs=[pl.BlockSpec(memory_space=pltpu.VMEM)] * len(operands),
        out_specs=[pl.BlockSpec(memory_space=pltpu.HBM)] * len(outs),
        out_shape=outs,
        scratch_shapes=[
            vmem(slots, block, width),
            pltpu.SemaphoreType.DMA((slots,)),
            vmem(3, rank, width, dtype=jnp.float32),
            pltpu.SemaphoreType.DMA((3, chunks)),
        ],
        compiler_params=pltpu.CompilerParams(vmem_limit_bytes=12 * MIB),
        cost_estimate=pl.CostEstimate(flops=0, bytes_accessed=1024, transcendentals=0),
        name="refresh",
    )(*[pltpu.with_memory_space_constraint(x, pltpu.VMEM) for x in operands])
    return result, fresh


def tensor_sum_parts(low, size):
    parts, stride = [low], 1
    while stride < size:
        if len(parts) > 1:
            total = functools.reduce(jnp.add, [f32(x) for x in parts])
            parts = [total.astype(jnp.bfloat16)]
        radix = min(4, size // stride)
        mine = parts[0]
        for hop in range(1, radix):
            pairs = [
                (i, i - i % (stride * radix) + (i + hop * stride) % (stride * radix))
                for i in range(size)
            ]
            parts.append(lax.ppermute(mine, "tensor", pairs))
        stride *= radix
    return parts


def toward(block, distance, t_size, r_size, first):
    pairs = []
    for t in range(t_size):
        root = t * r_size // t_size
        for r in range(r_size):
            same_side = ((r ^ root) & distance) == 0
            same_half = (r ^ root) % 2 == 0
            if (same_side != same_half) == first:
                pairs.append((t * r_size + r, t * r_size + (r ^ distance)))
    return lax.ppermute(block, ("tensor", "replica"), pairs)


def gather_rows(block, t_size, r_size):
    t = lax.axis_index("tensor")
    distance = 1
    while distance < max(1, t_size // r_size):
        other = swap(block, "tensor", t_size, distance)
        block = jnp.where(
            (t & distance) == 0,
            jnp.concatenate([block, other], axis=1),
            jnp.concatenate([other, block], axis=1),
        )
        distance *= 2
    return block


def is_root(t_size, r_size):
    t, r = lax.axis_index("tensor"), lax.axis_index("replica")
    many = max(1, t_size // r_size)
    return t // many == r * t_size // r_size // many


def spread(block, t_size, r_size):
    many = max(1, t_size // r_size)
    came = []
    for shift in range(many, t_size, many):
        pairs = []
        for r in range(r_size):
            first = r * t_size // r_size
            for t in range(first, first + many):
                pairs.append((t * r_size + r, (t ^ shift) * r_size + r))
        came.append(lax.ppermute(block, ("tensor", "replica"), pairs))
    return came


def own_rows(block, t_size, r_size):
    parts = max(1, r_size // t_size)
    if parts == 1:
        return block
    size = block.shape[1] // parts
    return lax.dynamic_slice_in_dim(block, (lax.axis_index("replica") % parts) * size, size, 1)


def per_device(
    acts,
    cots,
    down_factor,
    up_factor,
    down_first_moment,
    down_second_moment,
    up_first_moment,
    up_second_moment,
    rollout_weight,
    owner,
    projection_index,
):
    t_size, r_size = lax.axis_size("tensor"), lax.axis_size("replica")
    turn = lambda x: jnp.transpose(x, (0, 2, 1))
    down_state = tuple(map(turn, (down_factor, down_first_moment, down_second_moment)))
    up_state = (up_factor, up_first_moment, up_second_moment)
    coefficient = adapter_scale / (acts.shape[1] * r_size)
    down_half = functools.partial(down_parity, t_size=t_size, r_size=r_size)
    up_half = functools.partial(up_parity, t_size=t_size, r_size=r_size)
    exchange = lambda x, distance: swap(x, "replica", r_size, distance)

    low, acts_in, cots_in = low_parts(acts, cots, down_state[0], up_state[0])
    lows = tensor_sum_parts(low, t_size)
    up_send, up_own = gradient_parts(
        lows, cots_in, (), 2, coefficient, up_half,
    )
    up_came = exchange(up_send, 1)
    down_held, up_held, flags = load_state(
        down_state, up_state, projection_index, owner, t_size, r_size, up_send
    )
    down_send, down_own = gradient_parts(lows, acts_in, (flags,), 0, coefficient, down_half)
    up_own, down_send = join((up_own, up_came), passed=(down_send,))
    up_came, distance = exchange(up_own, 2), 4
    down_came = exchange(down_send, 1)
    while distance < r_size:
        (up_own,) = join((up_own, up_came))
        up_came, distance = exchange(up_own, distance), 2 * distance
    up_own, down_own, again = join((up_own, up_came), *[(down_own, down_came)] * 2)
    up_other = exchange(up_own, 1)
    distance = 2
    while 2 * distance < r_size:
        down_own, again = join(*[(down_own, exchange(down_own, distance))] * 2)
        distance *= 2
    down_first = toward(down_own, distance, t_size, r_size, True)

    (up_mine,) = chosen_factor(
        up_held, [up_own], [up_other], flags, up_half, ties=(down_first,)
    )
    held, shift = [up_mine], 1
    while shift < t_size // 2:
        held = held + [swap(x, "tensor", t_size, shift) for x in held]
        shift *= 2
    block, again = chosen_factor(
        down_held, [down_own, down_first], [], flags, down_half, ties=(up_mine,), passed=(again,)
    )
    block = own_rows(gather_rows(block, t_size, r_size), t_size, r_size)
    came = spread(block, t_size, r_size)
    down_rest = toward(again, distance, t_size, r_size, False)
    fresh_up = adam(up_held, up_own, up_other, flags, up_half, ties=(block,))
    (offered,) = offer(held, flags, t_size)
    held = held + [swap(offered, "tensor", t_size, t_size // 2)]
    (down_own,) = join((down_own, down_first, down_rest), ties=(offered,))
    down_other = exchange(down_own, 1)
    left, cols = prepare(block, came, held, flags, t_size, r_size)
    fresh_rollout_weight, fresh_down = refresh(
        left, cols, flags, rollout_weight, down_held, down_own, down_half
    )
    fresh_down = adam_half(
        down_held, down_other, flags, down_half, 1, fresh_down, (fresh_rollout_weight,)
    )
    return (
        turn(fresh_down[0]),
        fresh_up[0],
        turn(fresh_down[1]),
        turn(fresh_down[2]),
        fresh_up[1],
        fresh_up[2],
        fresh_rollout_weight,
    )


def solution(mesh):
    placed = (
        P(None, ("groups", "replica"), "tensor"),
        P(None, ("groups", "replica"), "tensor"),
        P("groups", "tensor", None),
        P("groups", None, "tensor"),
        P("groups", "tensor", None),
        P("groups", "tensor", None),
        P("groups", None, "tensor"),
        P("groups", None, "tensor"),
        P("replica", "tensor"),
        P(),
        P("groups"),
    )
    return jax.shard_map(
        per_device,
        mesh=mesh,
        in_specs=placed,
        out_specs=(
            P("groups", "tensor", None),
            P("groups", None, "tensor"),
            P("groups", "tensor", None),
            P("groups", "tensor", None),
            P("groups", None, "tensor"),
            P("groups", None, "tensor"),
            P(("groups", "replica"), "tensor"),
        ),
        check_vma=False,
    )
```

```python
import functools

import jax
import jax.numpy as jnp
from jax import lax
from jax.experimental import pallas as pl
from jax.experimental.pallas import tpu as pltpu
from jax.sharding import PartitionSpec as P

adapter_scale = 2.0
learn_rate = 0.05
beta_one = 0.9
beta_two = 0.999
adam_eps = 1e-08
fix_one = 1.0 - 0.9**10
fix_two = 1.0 - 0.999**10

MIB = 1024 * 1024
FLAGS = ("proj", "column_proj", "mine", "partners")


def moment_update(param, first, second, grad):
    first_new = beta_one * first + (1.0 - beta_one) * grad
    second_new = beta_two * second + (1.0 - beta_two) * grad * grad
    size = second_new * (1.0 / fix_two)
    param_new = param - (learn_rate / fix_one) * first_new / (size * lax.rsqrt(size) + adam_eps)
    return (param_new, first_new, second_new)


def f32(x):
    return x.astype(jnp.float32)


def swap(x, axis, size, distance):
    return lax.ppermute(x, axis, [(i, i ^ distance) for i in range(size)])


def vmem(*shape, dtype=jnp.bfloat16):
    return pltpu.VMEM(shape, dtype)


def local(kernel, name, outs, ins=(), hbm=(), smem=(), ties=(), after=(), passed=(), scratch=(), work=1024):
    n_ins, n_first = len(ins), len(ins) + len(hbm) + len(smem)
    n_outs = len(outs)

    def body(*refs):
        front = refs[:n_first]
        rest = refs[n_first + len(ties) + len(after) + len(passed) :]
        kernel(*front, *rest[:n_outs], *rest[n_outs + len(passed) :])

    operands = (
        [pltpu.with_memory_space_constraint(x, pltpu.VMEM) for x in ins]
        + [pltpu.with_memory_space_constraint(x, pltpu.HBM) for x in hbm]
        + [pltpu.with_memory_space_constraint(x, pltpu.HBM) for x in smem]
        + [pltpu.with_memory_space_constraint(x, pltpu.VMEM) for x in ties]
        + [pltpu.with_memory_space_constraint(x, pltpu.HBM) for x in after]
        + [pltpu.with_memory_space_constraint(x, pltpu.VMEM) for x in passed]
    )
    specs = (
        [pl.BlockSpec(memory_space=pltpu.VMEM)] * n_ins
        + [pl.BlockSpec(memory_space=pltpu.HBM)] * len(hbm)
        + [pl.BlockSpec(memory_space=pltpu.SMEM)] * len(smem)
        + [pl.BlockSpec(memory_space=pl.ANY)] * (len(ties) + len(after) + len(passed))
    )
    first_passed = n_first + len(ties) + len(after)
    return pl.pallas_call(
        body,
        in_specs=specs,
        out_specs=[pl.BlockSpec(memory_space=pltpu.VMEM)] * n_outs
        + [pl.BlockSpec(memory_space=pl.ANY)] * len(passed),
        out_shape=list(outs) + [pltpu.VMEM(x.shape, x.dtype) for x in passed],
        input_output_aliases={first_passed + i: n_outs + i for i in range(len(passed))},
        scratch_shapes=list(scratch),
        compiler_params=pltpu.CompilerParams(vmem_limit_bytes=8 * MIB),
        cost_estimate=pl.CostEstimate(flops=0, bytes_accessed=work, transcendentals=0),
        name=name,
    )(*operands)


def low_parts(acts, cots, down, up):
    tokens = acts.shape[1]
    rank = down.shape[1]

    def kernel(acts, cots, down, up, low, acts_in, cots_in, down_in, up_in, sems):
        jobs = []
        for spot, (x, x_in, f, f_in) in enumerate(
            ((cots, cots_in, up, up_in), (acts, acts_in, down, down_in))
        ):
            for p in range(2):
                i = 2 * spot + p
                pair = (
                    pltpu.make_async_copy(x.at[p], x_in.at[p], sems.at[2 * i]),
                    pltpu.make_async_copy(f.at[p], f_in.at[p], sems.at[2 * i + 1]),
                )
                for copy in pair:
                    copy.start()
                jobs.append((pair, x_in, f_in, p, i))
        for pair, x_in, f_in, p, i in jobs:
            for copy in pair:
                copy.wait()
            low[pl.ds(i * rank, rank), :] = lax.dot_general(
                f_in[p].astype(jnp.bfloat16),
                x_in[p],
                (((1,), (1,)), ((), ())),
                preferred_element_type=jnp.float32,
            ).astype(low.dtype)

    return local(
        kernel,
        "low_parts",
        [vmem(4 * rank, tokens), vmem(*acts.shape), vmem(*cots.shape)],
        hbm=(acts, cots, down, up),
        scratch=[
            vmem(*down.shape, dtype=jnp.float32),
            vmem(*up.shape, dtype=jnp.float32),
            pltpu.SemaphoreType.DMA((8,)),
        ],
    )


def load_state(down_state, up_state, projection_index, owner, t_size, r_size, tie):
    rank = down_state[0].shape[1]

    def kernel(*refs):
        sources, (index, owner), targets, (flags, sems) = refs[:6], refs[6:8], refs[8:14], refs[14:]
        copies = [
            pltpu.make_async_copy(x, y, sems.at[i]) for i, (x, y) in enumerate(zip(sources, targets))
        ]
        for copy in copies:
            copy.start()
        t, r = lax.axis_index("tensor"), lax.axis_index("replica")
        values = (index[r], index[t * r_size // t_size], owner[t], owner[t ^ (t_size // 2)])
        for i, value in enumerate(values):
            flags[pl.ds(i * rank, rank), :] = jnp.full((rank, 128), value, jnp.int32)
        for copy in copies:
            copy.wait()

    *state, flags = local(
        kernel,
        "load_state",
        [vmem(*x.shape, dtype=jnp.float32) for x in (*down_state, *up_state)]
        + [vmem(len(FLAGS) * rank, 128, dtype=jnp.int32)],
        hbm=(*down_state, *up_state),
        smem=(projection_index, owner),
        ties=(tie,),
        scratch=[pltpu.SemaphoreType.DMA((6,))],
    )
    return state[:3], state[3:], flags


def flag(flags, name, rank):
    return flags[pl.ds(FLAGS.index(name) * rank, rank), :]


def column_tiles(width):
    return [pl.ds(k, 128) for k in range(0, width, 128)]


def down_parity(flags, rank, t_size, r_size):
    t, r = lax.axis_index("tensor"), lax.axis_index("replica")
    return flag(flags, "column_proj", rank) ^ ((r + t * r_size // t_size) % 2)


def up_parity(flags, rank, t_size, r_size):
    r = lax.axis_index("replica")
    return jnp.full((rank, 128), r % 2, jnp.int32)


def gradient_parts(lows, tokens, flags, base, coefficient, half, ties=()):
    rank = lows[0].shape[0] // 4
    width = tokens.shape[2]
    parts = len(lows)

    def kernel(*refs):
        lows, tokens, flags, (send, keep) = refs[:parts], refs[parts], refs[parts + 1 : -2], refs[-2:]
        rows = pl.ds(base * rank, 2 * rank)
        total = functools.reduce(jnp.add, [f32(x[rows, :]) for x in lows]).astype(jnp.bfloat16)
        kept = half(flags[0] if flags else None, rank) == 0
        cut = min(width, 512)
        for k in range(0, width, cut):
            grads = [
                coefficient
                * jnp.dot(
                    total[p * rank : (p + 1) * rank],
                    tokens[p, :, pl.ds(k, cut)],
                    preferred_element_type=jnp.float32,
                )
                for p in range(2)
            ]
            for j in range(0, cut, 128):
                first, second = [g[:, j : j + 128] for g in grads]
                tile = pl.ds(k + j, 128)
                keep[:, tile] = jnp.where(kept, first, second).astype(keep.dtype)
                send[:, tile] = jnp.where(kept, second, first).astype(send.dtype)

    return local(
        kernel,
        "gradient_parts",
        [vmem(rank, width), vmem(rank, width)],
        ins=(*lows, tokens, *flags),
        ties=ties,
    )


def join(*sums, ties=(), passed=()):
    terms = [x for group in sums for x in group]

    def kernel(*refs):
        refs, outs = list(refs[: len(terms)]), refs[len(terms) :]
        for group, out in zip(sums, outs):
            total = functools.reduce(jnp.add, [f32(refs.pop(0)[...]) for _ in group])
            out[...] = total.astype(out.dtype)

    return local(
        kernel, "join", [vmem(*g[0].shape) for g in sums], ins=terms, ties=ties, passed=passed
    )


def chosen_factor(state, own, other, flags, half, ties=(), after=(), passed=()):
    rank, width = own[0].shape
    n_own, n_other = len(own), len(other)

    def total(refs, tile):
        return f32(functools.reduce(jnp.add, [f32(x[:, tile]) for x in refs]).astype(jnp.bfloat16))

    def kernel(*refs):
        state, own, other = refs[:3], refs[3 : 3 + n_own], refs[3 + n_own : 3 + n_own + n_other]
        flags, out = refs[3 + n_own + n_other :]
        p = jnp.max(flag(flags, "proj", rank)[0:1, :])
        for tile in column_tiles(width):
            grad = total(own, tile)
            if other:
                mine = flag(flags, "proj", rank) == half(flags, rank)
                grad = jnp.where(mine, grad, total(other, tile))
            held = [x[p, :, tile] for x in state]
            out[:, tile] = moment_update(*held, grad)[0].astype(out.dtype)

    return local(
        kernel,
        "chosen_factor",
        [vmem(rank, width)],
        ins=(*state, *own, *other, flags),
        ties=ties,
        after=after,
        passed=passed,
    )


def adam(state, own, other, flags, half, ties=()):
    rank, width = own.shape
    cuts = max(1, width // 1024)
    cut = width // cuts

    def kernel(*refs):
        state, own, other, flags, outs, (fresh, sems) = refs[:3], *refs[3:6], refs[-5:-2], refs[-2:]
        kept = half(flags, rank)
        copies = []
        for k in range(cuts):
            for j in range(k * cut, (k + 1) * cut, 128):
                tile = pl.ds(j, 128)
                grads = f32(own[:, tile]), f32(other[:, tile])
                for p in range(2):
                    grad = jnp.where(kept == p, *grads)
                    values = moment_update(*[x[p, :, tile] for x in state], grad)
                    for i, value in enumerate(values):
                        fresh[i, p, :, tile] = value
            span = pl.ds(k * cut, cut)
            for i, x in enumerate(outs):
                copies.append(
                    pltpu.make_async_copy(fresh.at[i, :, :, span], x.at[:, :, span], sems.at[k, i])
                )
                copies[-1].start()
        for copy in copies:
            copy.wait()

    in_vmem = (*state, own, other, flags, *ties)
    return pl.pallas_call(
        kernel,
        in_specs=[pl.BlockSpec(memory_space=pltpu.VMEM)] * 6
        + [pl.BlockSpec(memory_space=pl.ANY)] * len(ties),
        out_specs=[pl.BlockSpec(memory_space=pltpu.HBM)] * 3,
        out_shape=[pltpu.HBM(x.shape, x.dtype) for x in state],
        scratch_shapes=[
            vmem(3, 2, rank, width, dtype=jnp.float32),
            pltpu.SemaphoreType.DMA((cuts, 3)),
        ],
        compiler_params=pltpu.CompilerParams(vmem_limit_bytes=8 * MIB),
        cost_estimate=pl.CostEstimate(flops=0, bytes_accessed=1024, transcendentals=0),
        name="adam",
    )(*[pltpu.with_memory_space_constraint(x, pltpu.VMEM) for x in in_vmem])


def adam_half(state, grad, flags, half, flip, outs, after):
    rank, width = grad.shape
    cuts = max(1, width // 1024)
    cut = width // cuts

    def kernel(*refs):
        grad, flags, state = refs[0], refs[1], refs[2:5]
        targets, (fresh, sems) = refs[-5:-2], refs[-2:]
        p = jnp.max(half(flags, rank)[0:1, :]) ^ flip
        copies = []
        for k in range(cuts):
            for j in range(k * cut, (k + 1) * cut, 128):
                tile = pl.ds(j, 128)
                values = moment_update(*[x[p, :, tile] for x in state], f32(grad[:, tile]))
                for i, value in enumerate(values):
                    fresh[i, :, tile] = value
            span = pl.ds(k * cut, cut)
            for i, x in enumerate(targets):
                copies.append(
                    pltpu.make_async_copy(fresh.at[i, :, span], x.at[p, :, span], sems.at[k, i])
                )
                copies[-1].start()
        for copy in copies:
            copy.wait()

    in_vmem, in_hbm = (grad, flags, *state), (*after, *outs)
    first = len(in_vmem) + len(after)
    return pl.pallas_call(
        kernel,
        in_specs=[pl.BlockSpec(memory_space=pltpu.VMEM)] * len(in_vmem)
        + [pl.BlockSpec(memory_space=pltpu.HBM)] * len(in_hbm),
        out_specs=[pl.BlockSpec(memory_space=pltpu.HBM)] * 3,
        out_shape=[pltpu.HBM(x.shape, x.dtype) for x in state],
        input_output_aliases={first + i: i for i in range(3)},
        scratch_shapes=[
            vmem(3, rank, width, dtype=jnp.float32),
            pltpu.SemaphoreType.DMA((cuts, 3)),
        ],
        compiler_params=pltpu.CompilerParams(vmem_limit_bytes=8 * MIB),
        cost_estimate=pl.CostEstimate(flops=0, bytes_accessed=1024, transcendentals=0),
        name="adam_half",
    )(
        *[pltpu.with_memory_space_constraint(x, pltpu.VMEM) for x in in_vmem],
        *[pltpu.with_memory_space_constraint(x, pltpu.HBM) for x in in_hbm],
    )


def pick(flags, name, held, ids, rank):
    wanted = flag(flags, name, rank)

    def tile_of(tile):
        found = f32(held[0][:, tile])
        for i in range(1, len(held)):
            found = jnp.where(wanted == ids[i], f32(held[i][:, tile]), found)
        return found

    return tile_of


def block_ids(t_size, many):
    t = lax.axis_index("tensor")
    ids, distance = [t], 1
    while distance < t_size // 2:
        ids = ids + [i ^ distance for i in ids]
        distance *= 2
    return ids[:many]


def offer(held, flags, t_size, passed=()):
    rank, width = held[0].shape

    def kernel(*refs):
        held, flags, out = refs[:-2], refs[-2], refs[-1]
        tile_of = pick(flags, "partners", held, block_ids(t_size, len(held)), rank)
        for tile in column_tiles(width):
            out[:, tile] = tile_of(tile).astype(out.dtype)

    return local(kernel, "offer", [vmem(rank, width)], ins=(*held, flags), passed=passed)


def columns_of_b(held, flags, t_size, after=()):
    rank, width = held[0].shape

    def kernel(*refs):
        held, flags, cols = refs[:-2], refs[-2], refs[-1]
        ids = block_ids(t_size, len(held) - 1)
        tile_of = pick(flags, "mine", (held[-1], *held[:-1]), (None, *ids), rank)
        for tile in column_tiles(width):
            cols[:, tile] = (adapter_scale * tile_of(tile)).astype(cols.dtype)

    return local(
        kernel, "columns_of_b", [vmem(rank, width)], ins=(*held, flags), after=after
    )[0]


def rows_of_a(block, came, t_size, r_size, ties=()):
    rank, height = block.shape

    def kernel(*refs):
        block, came, left = refs[0], refs[1:-1], refs[-1]
        root = is_root(t_size, r_size)
        for j in range(0, height, 128):
            tile = pl.ds(j, 128)
            got = functools.reduce(jnp.add, [f32(x[:, tile]) for x in came])
            rows = jnp.where(root, f32(block[:, tile]), got).astype(left.dtype)
            left[tile, :] = rows.T

    return local(kernel, "rows_of_a", [vmem(height, rank)], ins=(block, *came), ties=ties)[0]


def refresh(left, cols, flags, weight, state, grad, half):
    height, width = weight.shape
    rank = cols.shape[0]
    block = min(height, 128)
    steps = height // block
    slots = min(8, steps)
    chunks = max(1, width // 1024)
    cut, apart = width // chunks, max(1, (steps - 2) // chunks)
    turns = [min(1 + apart * k, steps - 1) for k in range(chunks)]

    def kernel(*refs):
        left, cols, flags, weight, grad, *state = refs[:8]
        out, targets, (ring, sems, fresh, fresh_sems) = refs[8], refs[9:12], refs[12:]
        step = pl.program_id(0)
        slot = step % slots

        def emit(i):
            at = pl.ds(pl.multiple_of(i * block, block), block)
            return pltpu.make_async_copy(ring.at[i % slots], out.at[at, :], sems.at[i % slots])

        def writes(p, k):
            span = pl.ds(k * cut, cut)
            return [
                pltpu.make_async_copy(fresh.at[i, :, span], x.at[p, :, span], fresh_sems.at[i, k])
                for i, x in enumerate(targets)
            ]

        @pl.when(step >= slots)
        def _():
            emit(step - slots).wait()

        tall, wide = min(block, 128), min(width, 256)
        for k in range(0, width, wide):
            span = pl.ds(k, wide)
            for j in range(0, block, tall):
                at = pl.ds(pl.multiple_of(step * block + j, tall), tall)
                change = jnp.dot(left[at, :], cols[:, span], preferred_element_type=jnp.float32)
                ring[slot, pl.ds(j, tall), span] = (f32(weight[at, span]) + change).astype(ring.dtype)
        emit(step).start()

        for chunk, turn in enumerate(turns):

            @pl.when(step == turn)
            def _():
                p = jnp.max(half(flags, rank)[0:1, :])
                for k in range(chunk * cut, (chunk + 1) * cut, 128):
                    tile = pl.ds(k, 128)
                    values = moment_update(*[x[p, :, tile] for x in state], f32(grad[:, tile]))
                    for i, value in enumerate(values):
                        fresh[i, :, tile] = value
                for copy in writes(p, chunk):
                    copy.start()

        @pl.when(step == steps - 1)
        def _():
            p = jnp.max(half(flags, rank)[0:1, :])
            for k in range(chunks):
                for copy in writes(p, k):
                    copy.wait()
            for i in range(steps - slots, steps):
                emit(i).wait()

    operands = (left, cols, flags, weight, grad, *state)
    outs = [pltpu.HBM((height, width), weight.dtype)] + [pltpu.HBM(x.shape, x.dtype) for x in state]
    result, *fresh = pl.pallas_call(
        kernel,
        grid=(steps,),
        in_specs=[pl.BlockSpec(memory_space=pltpu.VMEM)] * len(operands),
        out_specs=[pl.BlockSpec(memory_space=pltpu.HBM)] * len(outs),
        out_shape=outs,
        scratch_shapes=[
            vmem(slots, block, width),
            pltpu.SemaphoreType.DMA((slots,)),
            vmem(3, rank, width, dtype=jnp.float32),
            pltpu.SemaphoreType.DMA((3, chunks)),
        ],
        compiler_params=pltpu.CompilerParams(vmem_limit_bytes=12 * MIB),
        cost_estimate=pl.CostEstimate(flops=0, bytes_accessed=1024, transcendentals=0),
        name="refresh",
    )(*[pltpu.with_memory_space_constraint(x, pltpu.VMEM) for x in operands])
    return result, fresh


def tensor_sum_parts(low, size):
    parts, stride = [low], 1
    while stride < size:
        if len(parts) > 1:
            total = functools.reduce(jnp.add, [f32(x) for x in parts])
            parts = [total.astype(jnp.bfloat16)]
        radix = min(4, size // stride)
        mine = parts[0]
        for hop in range(1, radix):
            pairs = [
                (i, i - i % (stride * radix) + (i + hop * stride) % (stride * radix))
                for i in range(size)
            ]
            parts.append(lax.ppermute(mine, "tensor", pairs))
        stride *= radix
    return parts


def toward(block, distance, t_size, r_size, first):
    pairs = []
    for t in range(t_size):
        root = t * r_size // t_size
        for r in range(r_size):
            same_side = ((r ^ root) & distance) == 0
            same_half = (r ^ root) % 2 == 0
            if (same_side != same_half) == first:
                pairs.append((t * r_size + r, t * r_size + (r ^ distance)))
    return lax.ppermute(block, ("tensor", "replica"), pairs)


def gather_rows(block, t_size, r_size):
    t = lax.axis_index("tensor")
    distance = 1
    while distance < max(1, t_size // r_size):
        other = swap(block, "tensor", t_size, distance)
        block = jnp.where(
            (t & distance) == 0,
            jnp.concatenate([block, other], axis=1),
            jnp.concatenate([other, block], axis=1),
        )
        distance *= 2
    return block


def is_root(t_size, r_size):
    t, r = lax.axis_index("tensor"), lax.axis_index("replica")
    many = max(1, t_size // r_size)
    return t // many == r * t_size // r_size // many


def spread(block, t_size, r_size):
    many = max(1, t_size // r_size)
    came = []
    for shift in range(many, t_size, many):
        pairs = []
        for r in range(r_size):
            first = r * t_size // r_size
            for t in range(first, first + many):
                pairs.append((t * r_size + r, (t ^ shift) * r_size + r))
        came.append(lax.ppermute(block, ("tensor", "replica"), pairs))
    return came


def own_rows(block, t_size, r_size):
    parts = max(1, r_size // t_size)
    if parts == 1:
        return block
    size = block.shape[1] // parts
    return lax.dynamic_slice_in_dim(block, (lax.axis_index("replica") % parts) * size, size, 1)


def per_device(
    acts,
    cots,
    down_factor,
    up_factor,
    down_first_moment,
    down_second_moment,
    up_first_moment,
    up_second_moment,
    rollout_weight,
    owner,
    projection_index,
):
    t_size, r_size = lax.axis_size("tensor"), lax.axis_size("replica")
    turn = lambda x: jnp.transpose(x, (0, 2, 1))
    down_state = tuple(map(turn, (down_factor, down_first_moment, down_second_moment)))
    up_state = (up_factor, up_first_moment, up_second_moment)
    coefficient = adapter_scale / (acts.shape[1] * r_size)
    down_half = functools.partial(down_parity, t_size=t_size, r_size=r_size)
    up_half = functools.partial(up_parity, t_size=t_size, r_size=r_size)
    exchange = lambda x, distance: swap(x, "replica", r_size, distance)

    low, acts_in, cots_in = low_parts(acts, cots, down_state[0], up_state[0])
    lows = tensor_sum_parts(low, t_size)
    up_send, up_own = gradient_parts(
        lows, cots_in, (), 2, coefficient, up_half,
    )
    up_came = exchange(up_send, 1)
    down_held, up_held, flags = load_state(
        down_state, up_state, projection_index, owner, t_size, r_size, up_send
    )
    down_send, down_own = gradient_parts(lows, acts_in, (flags,), 0, coefficient, down_half)
    up_own, down_send = join((up_own, up_came), passed=(down_send,))
    up_came, distance = exchange(up_own, 2), 4
    down_came = exchange(down_send, 1)
    while distance < r_size:
        (up_own,) = join((up_own, up_came))
        up_came, distance = exchange(up_own, distance), 2 * distance
    up_own, down_own, again = join((up_own, up_came), *[(down_own, down_came)] * 2)
    up_other = exchange(up_own, 1)
    distance = 2
    while 2 * distance < r_size:
        down_own, again = join(*[(down_own, exchange(down_own, distance))] * 2)
        distance *= 2
    down_first = toward(down_own, distance, t_size, r_size, True)

    (up_mine,) = chosen_factor(
        up_held, [up_own], [up_other], flags, up_half, ties=(down_first,)
    )
    held, shift = [up_mine], 1
    while shift < t_size // 2:
        held = held + [swap(x, "tensor", t_size, shift) for x in held]
        shift *= 2
    (offered,) = offer(held, flags, t_size)
    held = held + [swap(offered, "tensor", t_size, t_size // 2)]
    block, again = chosen_factor(
        down_held, [down_own, down_first], [], flags, down_half, ties=(offered,), passed=(again,)
    )
    block = own_rows(gather_rows(block, t_size, r_size), t_size, r_size)
    came = spread(block, t_size, r_size)
    down_rest = toward(again, distance, t_size, r_size, False)
    fresh_up = adam(up_held, up_own, up_other, flags, up_half, ties=(block,))
    cols = columns_of_b(held, flags, t_size, after=(fresh_up[0],))
    left = rows_of_a(block, came, t_size, r_size, ties=(cols,))
    (down_own,) = join((down_own, down_first, down_rest), ties=(left,))
    down_other = exchange(down_own, 1)
    fresh_rollout_weight, fresh_down = refresh(
        left, cols, flags, rollout_weight, down_held, down_own, down_half
    )
    fresh_down = adam_half(
        down_held, down_other, flags, down_half, 1, fresh_down, (fresh_rollout_weight,)
    )
    return (
        turn(fresh_down[0]),
        fresh_up[0],
        turn(fresh_down[1]),
        turn(fresh_down[2]),
        fresh_up[1],
        fresh_up[2],
        fresh_rollout_weight,
    )


def solution(mesh):
    placed = (
        P(None, ("groups", "replica"), "tensor"),
        P(None, ("groups", "replica"), "tensor"),
        P("groups", "tensor", None),
        P("groups", None, "tensor"),
        P("groups", "tensor", None),
        P("groups", "tensor", None),
        P("groups", None, "tensor"),
        P("groups", None, "tensor"),
        P("replica", "tensor"),
        P(),
        P("groups"),
    )
    return jax.shard_map(
        per_device,
        mesh=mesh,
        in_specs=placed,
        out_specs=(
            P("groups", "tensor", None),
            P("groups", None, "tensor"),
            P("groups", "tensor", None),
            P("groups", "tensor", None),
            P("groups", None, "tensor"),
            P("groups", None, "tensor"),
            P(("groups", "replica"), "tensor"),
        ),
        check_vma=False,
    )
```

```python
import functools

import jax
import jax.numpy as jnp
from jax import lax
from jax.experimental import pallas as pl
from jax.experimental.pallas import tpu as pltpu
from jax.sharding import PartitionSpec as P

adapter_scale = 2.0
learn_rate = 0.05
beta_one = 0.9
beta_two = 0.999
adam_eps = 1e-08
fix_one = 1.0 - 0.9**10
fix_two = 1.0 - 0.999**10

MIB = 1024 * 1024
FLAGS = ("proj", "column_proj", "mine", "partners")


def moment_update(param, first, second, grad):
    first_new = beta_one * first + (1.0 - beta_one) * grad
    second_new = beta_two * second + (1.0 - beta_two) * grad * grad
    size = second_new * (1.0 / fix_two)
    param_new = param - (learn_rate / fix_one) * first_new / (size * lax.rsqrt(size) + adam_eps)
    return (param_new, first_new, second_new)


def f32(x):
    return x.astype(jnp.float32)


def swap(x, axis, size, distance):
    return lax.ppermute(x, axis, [(i, i ^ distance) for i in range(size)])


def vmem(*shape, dtype=jnp.bfloat16):
    return pltpu.VMEM(shape, dtype)


def local(kernel, name, outs, ins=(), hbm=(), smem=(), ties=(), after=(), passed=(), scratch=(), work=1024):
    n_ins, n_first = len(ins), len(ins) + len(hbm) + len(smem)
    n_outs = len(outs)

    def body(*refs):
        front = refs[:n_first]
        rest = refs[n_first + len(ties) + len(after) + len(passed) :]
        kernel(*front, *rest[:n_outs], *rest[n_outs + len(passed) :])

    operands = (
        [pltpu.with_memory_space_constraint(x, pltpu.VMEM) for x in ins]
        + [pltpu.with_memory_space_constraint(x, pltpu.HBM) for x in hbm]
        + [pltpu.with_memory_space_constraint(x, pltpu.HBM) for x in smem]
        + [pltpu.with_memory_space_constraint(x, pltpu.VMEM) for x in ties]
        + [pltpu.with_memory_space_constraint(x, pltpu.HBM) for x in after]
        + [pltpu.with_memory_space_constraint(x, pltpu.VMEM) for x in passed]
    )
    specs = (
        [pl.BlockSpec(memory_space=pltpu.VMEM)] * n_ins
        + [pl.BlockSpec(memory_space=pltpu.HBM)] * len(hbm)
        + [pl.BlockSpec(memory_space=pltpu.SMEM)] * len(smem)
        + [pl.BlockSpec(memory_space=pl.ANY)] * (len(ties) + len(after) + len(passed))
    )
    first_passed = n_first + len(ties) + len(after)
    return pl.pallas_call(
        body,
        in_specs=specs,
        out_specs=[pl.BlockSpec(memory_space=pltpu.VMEM)] * n_outs
        + [pl.BlockSpec(memory_space=pl.ANY)] * len(passed),
        out_shape=list(outs) + [pltpu.VMEM(x.shape, x.dtype) for x in passed],
        input_output_aliases={first_passed + i: n_outs + i for i in range(len(passed))},
        scratch_shapes=list(scratch),
        compiler_params=pltpu.CompilerParams(vmem_limit_bytes=8 * MIB),
        cost_estimate=pl.CostEstimate(flops=0, bytes_accessed=work, transcendentals=0),
        name=name,
    )(*operands)


def low_parts(acts, cots, down, up):
    tokens = acts.shape[1]
    rank = down.shape[1]

    def kernel(acts, cots, down, up, low, acts_in, cots_in, down_in, up_in, sems):
        jobs = []
        for spot, (x, x_in, f, f_in) in enumerate(
            ((cots, cots_in, up, up_in), (acts, acts_in, down, down_in))
        ):
            for p in range(2):
                i = 2 * spot + p
                pair = (
                    pltpu.make_async_copy(x.at[p], x_in.at[p], sems.at[2 * i]),
                    pltpu.make_async_copy(f.at[p], f_in.at[p], sems.at[2 * i + 1]),
                )
                for copy in pair:
                    copy.start()
                jobs.append((pair, x_in, f_in, p, i))
        for pair, x_in, f_in, p, i in jobs:
            for copy in pair:
                copy.wait()
            low[pl.ds(i * rank, rank), :] = lax.dot_general(
                f_in[p].astype(jnp.bfloat16),
                x_in[p],
                (((1,), (1,)), ((), ())),
                preferred_element_type=jnp.float32,
            ).astype(low.dtype)

    return local(
        kernel,
        "low_parts",
        [vmem(4 * rank, tokens), vmem(*acts.shape), vmem(*cots.shape)],
        hbm=(acts, cots, down, up),
        scratch=[
            vmem(*down.shape, dtype=jnp.float32),
            vmem(*up.shape, dtype=jnp.float32),
            pltpu.SemaphoreType.DMA((8,)),
        ],
    )


def load_state(down_state, up_state, projection_index, owner, t_size, r_size, tie):
    rank = down_state[0].shape[1]

    def kernel(*refs):
        sources, (index, owner), targets, (flags, sems) = refs[:6], refs[6:8], refs[8:14], refs[14:]
        copies = [
            pltpu.make_async_copy(x, y, sems.at[i]) for i, (x, y) in enumerate(zip(sources, targets))
        ]
        for copy in copies:
            copy.start()
        t, r = lax.axis_index("tensor"), lax.axis_index("replica")
        values = (index[r], index[t * r_size // t_size], owner[t], owner[t ^ (t_size // 2)])
        for i, value in enumerate(values):
            flags[pl.ds(i * rank, rank), :] = jnp.full((rank, 128), value, jnp.int32)
        for copy in copies:
            copy.wait()

    *state, flags = local(
        kernel,
        "load_state",
        [vmem(*x.shape, dtype=jnp.float32) for x in (*down_state, *up_state)]
        + [vmem(len(FLAGS) * rank, 128, dtype=jnp.int32)],
        hbm=(*down_state, *up_state),
        smem=(projection_index, owner),
        ties=(tie,),
        scratch=[pltpu.SemaphoreType.DMA((6,))],
    )
    return state[:3], state[3:], flags


def flag(flags, name, rank):
    return flags[pl.ds(FLAGS.index(name) * rank, rank), :]


def column_tiles(width):
    return [pl.ds(k, 128) for k in range(0, width, 128)]


def down_parity(flags, rank, t_size, r_size):
    t, r = lax.axis_index("tensor"), lax.axis_index("replica")
    return flag(flags, "column_proj", rank) ^ ((r + t * r_size // t_size) % 2)


def up_parity(flags, rank, t_size, r_size):
    r = lax.axis_index("replica")
    return jnp.full((rank, 128), r % 2, jnp.int32)


def gradient_parts(lows, tokens, flags, base, coefficient, half, ties=()):
    rank = lows[0].shape[0] // 4
    width = tokens.shape[2]
    parts = len(lows)

    def kernel(*refs):
        lows, tokens, flags, (send, keep) = refs[:parts], refs[parts], refs[parts + 1 : -2], refs[-2:]
        rows = pl.ds(base * rank, 2 * rank)
        total = functools.reduce(jnp.add, [f32(x[rows, :]) for x in lows]).astype(jnp.bfloat16)
        kept = half(flags[0] if flags else None, rank) == 0
        cut = min(width, 512)
        for k in range(0, width, cut):
            grads = [
                coefficient
                * jnp.dot(
                    total[p * rank : (p + 1) * rank],
                    tokens[p, :, pl.ds(k, cut)],
                    preferred_element_type=jnp.float32,
                )
                for p in range(2)
            ]
            for j in range(0, cut, 128):
                first, second = [g[:, j : j + 128] for g in grads]
                tile = pl.ds(k + j, 128)
                keep[:, tile] = jnp.where(kept, first, second).astype(keep.dtype)
                send[:, tile] = jnp.where(kept, second, first).astype(send.dtype)

    return local(
        kernel,
        "gradient_parts",
        [vmem(rank, width), vmem(rank, width)],
        ins=(*lows, tokens, *flags),
        ties=ties,
    )


def join(*sums, ties=(), passed=()):
    terms = [x for group in sums for x in group]

    def kernel(*refs):
        refs, outs = list(refs[: len(terms)]), refs[len(terms) :]
        for group, out in zip(sums, outs):
            total = functools.reduce(jnp.add, [f32(refs.pop(0)[...]) for _ in group])
            out[...] = total.astype(out.dtype)

    return local(
        kernel, "join", [vmem(*g[0].shape) for g in sums], ins=terms, ties=ties, passed=passed
    )


def chosen_factor(state, own, other, flags, half, ties=(), after=(), passed=()):
    rank, width = own[0].shape
    n_own, n_other = len(own), len(other)

    def total(refs, tile):
        return f32(functools.reduce(jnp.add, [f32(x[:, tile]) for x in refs]).astype(jnp.bfloat16))

    def kernel(*refs):
        state, own, other = refs[:3], refs[3 : 3 + n_own], refs[3 + n_own : 3 + n_own + n_other]
        flags, out = refs[3 + n_own + n_other :]
        p = jnp.max(flag(flags, "proj", rank)[0:1, :])
        for tile in column_tiles(width):
            grad = total(own, tile)
            if other:
                mine = flag(flags, "proj", rank) == half(flags, rank)
                grad = jnp.where(mine, grad, total(other, tile))
            held = [x[p, :, tile] for x in state]
            out[:, tile] = moment_update(*held, grad)[0].astype(out.dtype)

    return local(
        kernel,
        "chosen_factor",
        [vmem(rank, width)],
        ins=(*state, *own, *other, flags),
        ties=ties,
        after=after,
        passed=passed,
    )


def adam(state, own, other, flags, half, ties=()):
    rank, width = own.shape
    cuts = max(1, width // 1024)
    cut = width // cuts

    def kernel(*refs):
        state, own, other, flags, outs, (fresh, sems) = refs[:3], *refs[3:6], refs[-5:-2], refs[-2:]
        kept = half(flags, rank)
        copies = []
        for k in range(cuts):
            for j in range(k * cut, (k + 1) * cut, 128):
                tile = pl.ds(j, 128)
                grads = f32(own[:, tile]), f32(other[:, tile])
                for p in range(2):
                    grad = jnp.where(kept == p, *grads)
                    values = moment_update(*[x[p, :, tile] for x in state], grad)
                    for i, value in enumerate(values):
                        fresh[i, p, :, tile] = value
            span = pl.ds(k * cut, cut)
            for i, x in enumerate(outs):
                copies.append(
                    pltpu.make_async_copy(fresh.at[i, :, :, span], x.at[:, :, span], sems.at[k, i])
                )
                copies[-1].start()
        for copy in copies:
            copy.wait()

    in_vmem = (*state, own, other, flags, *ties)
    return pl.pallas_call(
        kernel,
        in_specs=[pl.BlockSpec(memory_space=pltpu.VMEM)] * 6
        + [pl.BlockSpec(memory_space=pl.ANY)] * len(ties),
        out_specs=[pl.BlockSpec(memory_space=pltpu.HBM)] * 3,
        out_shape=[pltpu.HBM(x.shape, x.dtype) for x in state],
        scratch_shapes=[
            vmem(3, 2, rank, width, dtype=jnp.float32),
            pltpu.SemaphoreType.DMA((cuts, 3)),
        ],
        compiler_params=pltpu.CompilerParams(vmem_limit_bytes=8 * MIB),
        cost_estimate=pl.CostEstimate(flops=0, bytes_accessed=1024, transcendentals=0),
        name="adam",
    )(*[pltpu.with_memory_space_constraint(x, pltpu.VMEM) for x in in_vmem])


def adam_half(state, grad, flags, half, flip, outs, after):
    rank, width = grad.shape
    cuts = max(1, width // 1024)
    cut = width // cuts

    def kernel(*refs):
        grad, flags, state = refs[0], refs[1], refs[2:5]
        targets, (fresh, sems) = refs[-5:-2], refs[-2:]
        p = jnp.max(half(flags, rank)[0:1, :]) ^ flip
        copies = []
        for k in range(cuts):
            for j in range(k * cut, (k + 1) * cut, 128):
                tile = pl.ds(j, 128)
                values = moment_update(*[x[p, :, tile] for x in state], f32(grad[:, tile]))
                for i, value in enumerate(values):
                    fresh[i, :, tile] = value
            span = pl.ds(k * cut, cut)
            for i, x in enumerate(targets):
                copies.append(
                    pltpu.make_async_copy(fresh.at[i, :, span], x.at[p, :, span], sems.at[k, i])
                )
                copies[-1].start()
        for copy in copies:
            copy.wait()

    in_vmem, in_hbm = (grad, flags, *state), (*after, *outs)
    first = len(in_vmem) + len(after)
    return pl.pallas_call(
        kernel,
        in_specs=[pl.BlockSpec(memory_space=pltpu.VMEM)] * len(in_vmem)
        + [pl.BlockSpec(memory_space=pltpu.HBM)] * len(in_hbm),
        out_specs=[pl.BlockSpec(memory_space=pltpu.HBM)] * 3,
        out_shape=[pltpu.HBM(x.shape, x.dtype) for x in state],
        input_output_aliases={first + i: i for i in range(3)},
        scratch_shapes=[
            vmem(3, rank, width, dtype=jnp.float32),
            pltpu.SemaphoreType.DMA((cuts, 3)),
        ],
        compiler_params=pltpu.CompilerParams(vmem_limit_bytes=8 * MIB),
        cost_estimate=pl.CostEstimate(flops=0, bytes_accessed=1024, transcendentals=0),
        name="adam_half",
    )(
        *[pltpu.with_memory_space_constraint(x, pltpu.VMEM) for x in in_vmem],
        *[pltpu.with_memory_space_constraint(x, pltpu.HBM) for x in in_hbm],
    )


def pick(flags, name, held, ids, rank):
    wanted = flag(flags, name, rank)

    def tile_of(tile):
        found = f32(held[0][:, tile])
        for i in range(1, len(held)):
            found = jnp.where(wanted == ids[i], f32(held[i][:, tile]), found)
        return found

    return tile_of


def block_ids(t_size, many):
    t = lax.axis_index("tensor")
    ids, distance = [t], 1
    while distance < t_size // 2:
        ids = ids + [i ^ distance for i in ids]
        distance *= 2
    return ids[:many]


def offer(held, flags, t_size, passed=()):
    rank, width = held[0].shape

    def kernel(*refs):
        held, flags, out = refs[:-2], refs[-2], refs[-1]
        tile_of = pick(flags, "partners", held, block_ids(t_size, len(held)), rank)
        for tile in column_tiles(width):
            out[:, tile] = tile_of(tile).astype(out.dtype)

    return local(kernel, "offer", [vmem(rank, width)], ins=(*held, flags), passed=passed)


def columns_of_b(held, flags, t_size, after=()):
    rank, width = held[0].shape

    def kernel(*refs):
        held, flags, cols = refs[:-2], refs[-2], refs[-1]
        ids = block_ids(t_size, len(held) - 1)
        tile_of = pick(flags, "mine", (held[-1], *held[:-1]), (None, *ids), rank)
        for tile in column_tiles(width):
            cols[:, tile] = (adapter_scale * tile_of(tile)).astype(cols.dtype)

    return local(
        kernel, "columns_of_b", [vmem(rank, width)], ins=(*held, flags), after=after
    )[0]


def rows_of_a(block, came, t_size, r_size, ties=()):
    rank, height = block.shape

    def kernel(*refs):
        block, came, left = refs[0], refs[1:-1], refs[-1]
        root = is_root(t_size, r_size)
        for j in range(0, height, 128):
            tile = pl.ds(j, 128)
            got = functools.reduce(jnp.add, [f32(x[:, tile]) for x in came])
            rows = jnp.where(root, f32(block[:, tile]), got).astype(left.dtype)
            left[tile, :] = rows.T

    return local(kernel, "rows_of_a", [vmem(height, rank)], ins=(block, *came), ties=ties)[0]


def refresh(left, cols, flags, weight, state, grad, half):
    height, width = weight.shape
    rank = cols.shape[0]
    block = min(height, 512)
    steps = height // block
    slots = min(3, steps)
    groups = max(1, width // 1024)
    group = width // groups
    chunks = max(1, width // 1024)
    cut, apart = width // chunks, max(1, (steps - 2) // chunks)
    turns = [min(1 + apart * k, steps - 1) for k in range(chunks)]

    def kernel(*refs):
        left, cols, flags, weight, grad, *state = refs[:8]
        out, targets, (ring, sems, fresh, fresh_sems) = refs[8], refs[9:12], refs[12:]
        step = pl.program_id(0)
        slot = step % slots

        def emit(i, g):
            at, span = pl.ds(pl.multiple_of(i * block, block), block), pl.ds(g * group, group)
            return pltpu.make_async_copy(
                ring.at[i % slots, :, span], out.at[at, span], sems.at[i % slots, g]
            )

        def writes(p, k):
            span = pl.ds(k * cut, cut)
            return [
                pltpu.make_async_copy(fresh.at[i, :, span], x.at[p, :, span], fresh_sems.at[i, k])
                for i, x in enumerate(targets)
            ]

        @pl.when(step >= slots)
        def _():
            for g in range(groups):
                emit(step - slots, g).wait()

        wide = min(width, 256)
        at = pl.ds(pl.multiple_of(step * block, block), block)
        for g in range(groups):
            for k in range(g * group, (g + 1) * group, wide):
                span = pl.ds(k, wide)
                change = jnp.dot(left[at, :], cols[:, span], preferred_element_type=jnp.float32)
                ring[slot, :, span] = (f32(weight[at, span]) + change).astype(ring.dtype)
            emit(step, g).start()

        for chunk, turn in enumerate(turns):

            @pl.when(step == turn)
            def _():
                p = jnp.max(half(flags, rank)[0:1, :])
                for k in range(chunk * cut, (chunk + 1) * cut, 128):
                    tile = pl.ds(k, 128)
                    values = moment_update(*[x[p, :, tile] for x in state], f32(grad[:, tile]))
                    for i, value in enumerate(values):
                        fresh[i, :, tile] = value
                for copy in writes(p, chunk):
                    copy.start()

        @pl.when(step == steps - 1)
        def _():
            p = jnp.max(half(flags, rank)[0:1, :])
            for k in range(chunks):
                for copy in writes(p, k):
                    copy.wait()
            for i in range(steps - slots, steps):
                for g in range(groups):
                    emit(i, g).wait()

    operands = (left, cols, flags, weight, grad, *state)
    outs = [pltpu.HBM((height, width), weight.dtype)] + [pltpu.HBM(x.shape, x.dtype) for x in state]
    result, *fresh = pl.pallas_call(
        kernel,
        grid=(steps,),
        in_specs=[pl.BlockSpec(memory_space=pltpu.VMEM)] * len(operands),
        out_specs=[pl.BlockSpec(memory_space=pltpu.HBM)] * len(outs),
        out_shape=outs,
        scratch_shapes=[
            vmem(slots, block, width),
            pltpu.SemaphoreType.DMA((slots, groups)),
            vmem(3, rank, width, dtype=jnp.float32),
            pltpu.SemaphoreType.DMA((3, chunks)),
        ],
        compiler_params=pltpu.CompilerParams(vmem_limit_bytes=16 * MIB),
        cost_estimate=pl.CostEstimate(flops=0, bytes_accessed=1024, transcendentals=0),
        name="refresh",
    )(*[pltpu.with_memory_space_constraint(x, pltpu.VMEM) for x in operands])
    return result, fresh


def tensor_sum_parts(low, size):
    parts, stride = [low], 1
    while stride < size:
        if len(parts) > 1:
            total = functools.reduce(jnp.add, [f32(x) for x in parts])
            parts = [total.astype(jnp.bfloat16)]
        radix = min(4, size // stride)
        mine = parts[0]
        for hop in range(1, radix):
            pairs = [
                (i, i - i % (stride * radix) + (i + hop * stride) % (stride * radix))
                for i in range(size)
            ]
            parts.append(lax.ppermute(mine, "tensor", pairs))
        stride *= radix
    return parts


def toward(block, distance, t_size, r_size, first):
    pairs = []
    for t in range(t_size):
        root = t * r_size // t_size
        for r in range(r_size):
            same_side = ((r ^ root) & distance) == 0
            same_half = (r ^ root) % 2 == 0
            if (same_side != same_half) == first:
                pairs.append((t * r_size + r, t * r_size + (r ^ distance)))
    return lax.ppermute(block, ("tensor", "replica"), pairs)


def gather_rows(block, t_size, r_size):
    t = lax.axis_index("tensor")
    distance = 1
    while distance < max(1, t_size // r_size):
        other = swap(block, "tensor", t_size, distance)
        block = jnp.where(
            (t & distance) == 0,
            jnp.concatenate([block, other], axis=1),
            jnp.concatenate([other, block], axis=1),
        )
        distance *= 2
    return block


def is_root(t_size, r_size):
    t, r = lax.axis_index("tensor"), lax.axis_index("replica")
    many = max(1, t_size // r_size)
    return t // many == r * t_size // r_size // many


def spread(block, t_size, r_size):
    many = max(1, t_size // r_size)
    came = []
    for shift in range(many, t_size, many):
        pairs = []
        for r in range(r_size):
            first = r * t_size // r_size
            for t in range(first, first + many):
                pairs.append((t * r_size + r, (t ^ shift) * r_size + r))
        came.append(lax.ppermute(block, ("tensor", "replica"), pairs))
    return came


def own_rows(block, t_size, r_size):
    parts = max(1, r_size // t_size)
    if parts == 1:
        return block
    size = block.shape[1] // parts
    return lax.dynamic_slice_in_dim(block, (lax.axis_index("replica") % parts) * size, size, 1)


def per_device(
    acts,
    cots,
    down_factor,
    up_factor,
    down_first_moment,
    down_second_moment,
    up_first_moment,
    up_second_moment,
    rollout_weight,
    owner,
    projection_index,
):
    t_size, r_size = lax.axis_size("tensor"), lax.axis_size("replica")
    turn = lambda x: jnp.transpose(x, (0, 2, 1))
    down_state = tuple(map(turn, (down_factor, down_first_moment, down_second_moment)))
    up_state = (up_factor, up_first_moment, up_second_moment)
    coefficient = adapter_scale / (acts.shape[1] * r_size)
    down_half = functools.partial(down_parity, t_size=t_size, r_size=r_size)
    up_half = functools.partial(up_parity, t_size=t_size, r_size=r_size)
    exchange = lambda x, distance: swap(x, "replica", r_size, distance)

    low, acts_in, cots_in = low_parts(acts, cots, down_state[0], up_state[0])
    lows = tensor_sum_parts(low, t_size)
    up_send, up_own = gradient_parts(
        lows, cots_in, (), 2, coefficient, up_half,
    )
    up_came = exchange(up_send, 1)
    down_held, up_held, flags = load_state(
        down_state, up_state, projection_index, owner, t_size, r_size, up_send
    )
    down_send, down_own = gradient_parts(lows, acts_in, (flags,), 0, coefficient, down_half)
    up_own, down_send = join((up_own, up_came), passed=(down_send,))
    up_came, distance = exchange(up_own, 2), 4
    down_came = exchange(down_send, 1)
    while distance < r_size:
        (up_own,) = join((up_own, up_came))
        up_came, distance = exchange(up_own, distance), 2 * distance
    down_own, again = join(*[(down_own, down_came)] * 2)
    (up_own,) = join((up_own, up_came), ties=(down_own,))
    up_other = exchange(up_own, 1)
    distance = 2
    while 2 * distance < r_size:
        down_own, again = join(*[(down_own, exchange(down_own, distance))] * 2)
        distance *= 2
    down_first = toward(down_own, distance, t_size, r_size, True)

    (up_mine,) = chosen_factor(
        up_held, [up_own], [up_other], flags, up_half, ties=(down_first,)
    )
    held, shift = [up_mine], 1
    while shift < t_size // 2:
        held = held + [swap(x, "tensor", t_size, shift) for x in held]
        shift *= 2
    (offered,) = offer(held, flags, t_size)
    held = held + [swap(offered, "tensor", t_size, t_size // 2)]
    block, again = chosen_factor(
        down_held, [down_own, down_first], [], flags, down_half, ties=(offered,), passed=(again,)
    )
    block = own_rows(gather_rows(block, t_size, r_size), t_size, r_size)
    came = spread(block, t_size, r_size)
    down_rest = toward(again, distance, t_size, r_size, False)
    fresh_up = adam(up_held, up_own, up_other, flags, up_half, ties=(block,))
    cols = columns_of_b(held, flags, t_size, after=(fresh_up[0],))
    left = rows_of_a(block, came, t_size, r_size, ties=(cols,))
    (down_own,) = join((down_own, down_first, down_rest), ties=(left,))
    down_other = exchange(down_own, 1)
    fresh_rollout_weight, fresh_down = refresh(
        left, cols, flags, rollout_weight, down_held, down_own, down_half
    )
    fresh_down = adam_half(
        down_held, down_other, flags, down_half, 1, fresh_down, (fresh_rollout_weight,)
    )
    return (
        turn(fresh_down[0]),
        fresh_up[0],
        turn(fresh_down[1]),
        turn(fresh_down[2]),
        fresh_up[1],
        fresh_up[2],
        fresh_rollout_weight,
    )


def solution(mesh):
    placed = (
        P(None, ("groups", "replica"), "tensor"),
        P(None, ("groups", "replica"), "tensor"),
        P("groups", "tensor", None),
        P("groups", None, "tensor"),
        P("groups", "tensor", None),
        P("groups", "tensor", None),
        P("groups", None, "tensor"),
        P("groups", None, "tensor"),
        P("replica", "tensor"),
        P(),
        P("groups"),
    )
    return jax.shard_map(
        per_device,
        mesh=mesh,
        in_specs=placed,
        out_specs=(
            P("groups", "tensor", None),
            P("groups", None, "tensor"),
            P("groups", "tensor", None),
            P("groups", "tensor", None),
            P("groups", None, "tensor"),
            P("groups", None, "tensor"),
            P(("groups", "replica"), "tensor"),
        ),
        check_vma=False,
    )
```

```python
import functools

import jax
import jax.numpy as jnp
from jax import lax
from jax.experimental import pallas as pl
from jax.experimental.pallas import tpu as pltpu
from jax.sharding import PartitionSpec as P

adapter_scale = 2.0
learn_rate = 0.05
beta_one = 0.9
beta_two = 0.999
adam_eps = 1e-08
fix_one = 1.0 - 0.9**10
fix_two = 1.0 - 0.999**10

MIB = 1024 * 1024
FLAGS = ("proj", "column_proj", "mine", "partners")


def moment_update(param, first, second, grad):
    first_new = beta_one * first + (1.0 - beta_one) * grad
    second_new = beta_two * second + (1.0 - beta_two) * grad * grad
    size = second_new * (1.0 / fix_two)
    param_new = param - (learn_rate / fix_one) * first_new / (size * lax.rsqrt(size) + adam_eps)
    return (param_new, first_new, second_new)


def f32(x):
    return x.astype(jnp.float32)


def swap(x, axis, size, distance):
    return lax.ppermute(x, axis, [(i, i ^ distance) for i in range(size)])


def vmem(*shape, dtype=jnp.bfloat16):
    return pltpu.VMEM(shape, dtype)


def local(kernel, name, outs, ins=(), hbm=(), smem=(), ties=(), after=(), passed=(), scratch=(), work=1024):
    n_ins, n_first = len(ins), len(ins) + len(hbm) + len(smem)
    n_outs = len(outs)

    def body(*refs):
        front = refs[:n_first]
        rest = refs[n_first + len(ties) + len(after) + len(passed) :]
        kernel(*front, *rest[:n_outs], *rest[n_outs + len(passed) :])

    operands = (
        [pltpu.with_memory_space_constraint(x, pltpu.VMEM) for x in ins]
        + [pltpu.with_memory_space_constraint(x, pltpu.HBM) for x in hbm]
        + [pltpu.with_memory_space_constraint(x, pltpu.HBM) for x in smem]
        + [pltpu.with_memory_space_constraint(x, pltpu.VMEM) for x in ties]
        + [pltpu.with_memory_space_constraint(x, pltpu.HBM) for x in after]
        + [pltpu.with_memory_space_constraint(x, pltpu.VMEM) for x in passed]
    )
    specs = (
        [pl.BlockSpec(memory_space=pltpu.VMEM)] * n_ins
        + [pl.BlockSpec(memory_space=pltpu.HBM)] * len(hbm)
        + [pl.BlockSpec(memory_space=pltpu.SMEM)] * len(smem)
        + [pl.BlockSpec(memory_space=pl.ANY)] * (len(ties) + len(after) + len(passed))
    )
    first_passed = n_first + len(ties) + len(after)
    return pl.pallas_call(
        body,
        in_specs=specs,
        out_specs=[pl.BlockSpec(memory_space=pltpu.VMEM)] * n_outs
        + [pl.BlockSpec(memory_space=pl.ANY)] * len(passed),
        out_shape=list(outs) + [pltpu.VMEM(x.shape, x.dtype) for x in passed],
        input_output_aliases={first_passed + i: n_outs + i for i in range(len(passed))},
        scratch_shapes=list(scratch),
        compiler_params=pltpu.CompilerParams(vmem_limit_bytes=8 * MIB),
        cost_estimate=pl.CostEstimate(flops=0, bytes_accessed=work, transcendentals=0),
        name=name,
    )(*operands)


def low_parts(acts, cots, down, up):
    tokens = acts.shape[1]
    rank = down.shape[1]

    def kernel(acts, cots, down, up, low, acts_in, cots_in, down_in, up_in, sems):
        jobs = []
        for spot, (x, x_in, f, f_in) in enumerate(
            ((cots, cots_in, up, up_in), (acts, acts_in, down, down_in))
        ):
            for p in range(2):
                i = 2 * spot + p
                pair = (
                    pltpu.make_async_copy(x.at[p], x_in.at[p], sems.at[2 * i]),
                    pltpu.make_async_copy(f.at[p], f_in.at[p], sems.at[2 * i + 1]),
                )
                for copy in pair:
                    copy.start()
                jobs.append((pair, x_in, f_in, p, i))
        for pair, x_in, f_in, p, i in jobs:
            for copy in pair:
                copy.wait()
            low[pl.ds(i * rank, rank), :] = lax.dot_general(
                f_in[p].astype(jnp.bfloat16),
                x_in[p],
                (((1,), (1,)), ((), ())),
                preferred_element_type=jnp.float32,
            ).astype(low.dtype)

    return local(
        kernel,
        "low_parts",
        [vmem(4 * rank, tokens), vmem(*acts.shape), vmem(*cots.shape)],
        hbm=(acts, cots, down, up),
        scratch=[
            vmem(*down.shape, dtype=jnp.float32),
            vmem(*up.shape, dtype=jnp.float32),
            pltpu.SemaphoreType.DMA((8,)),
        ],
    )


def load_state(down_state, up_state, projection_index, owner, t_size, r_size, tie):
    rank = down_state[0].shape[1]

    def kernel(*refs):
        sources, (index, owner), targets, (flags, sems) = refs[:6], refs[6:8], refs[8:14], refs[14:]
        copies = [
            pltpu.make_async_copy(x, y, sems.at[i]) for i, (x, y) in enumerate(zip(sources, targets))
        ]
        for copy in copies:
            copy.start()
        t, r = lax.axis_index("tensor"), lax.axis_index("replica")
        values = (index[r], index[t * r_size // t_size], owner[t], owner[t ^ (t_size // 2)])
        for i, value in enumerate(values):
            flags[pl.ds(i * rank, rank), :] = jnp.full((rank, 128), value, jnp.int32)
        for copy in copies:
            copy.wait()

    *state, flags = local(
        kernel,
        "load_state",
        [vmem(*x.shape, dtype=jnp.float32) for x in (*down_state, *up_state)]
        + [vmem(len(FLAGS) * rank, 128, dtype=jnp.int32)],
        hbm=(*down_state, *up_state),
        smem=(projection_index, owner),
        ties=(tie,),
        scratch=[pltpu.SemaphoreType.DMA((6,))],
    )
    return state[:3], state[3:], flags


def flag(flags, name, rank):
    return flags[pl.ds(FLAGS.index(name) * rank, rank), :]


def column_tiles(width):
    return [pl.ds(k, 128) for k in range(0, width, 128)]


def down_parity(flags, rank, t_size, r_size):
    t, r = lax.axis_index("tensor"), lax.axis_index("replica")
    return flag(flags, "column_proj", rank) ^ ((r + t * r_size // t_size) % 2)


def up_parity(flags, rank, t_size, r_size):
    r = lax.axis_index("replica")
    return jnp.full((rank, 128), r % 2, jnp.int32)


def gradient_parts(lows, tokens, flags, base, coefficient, half, ties=()):
    rank = lows[0].shape[0] // 4
    width = tokens.shape[2]
    parts = len(lows)

    def kernel(*refs):
        lows, tokens, flags, (send, keep) = refs[:parts], refs[parts], refs[parts + 1 : -2], refs[-2:]
        rows = pl.ds(base * rank, 2 * rank)
        total = functools.reduce(jnp.add, [f32(x[rows, :]) for x in lows]).astype(jnp.bfloat16)
        kept = half(flags[0] if flags else None, rank) == 0
        cut = min(width, 512)
        for k in range(0, width, cut):
            grads = [
                coefficient
                * jnp.dot(
                    total[p * rank : (p + 1) * rank],
                    tokens[p, :, pl.ds(k, cut)],
                    preferred_element_type=jnp.float32,
                )
                for p in range(2)
            ]
            for j in range(0, cut, 128):
                first, second = [g[:, j : j + 128] for g in grads]
                tile = pl.ds(k + j, 128)
                keep[:, tile] = jnp.where(kept, first, second).astype(keep.dtype)
                send[:, tile] = jnp.where(kept, second, first).astype(send.dtype)

    return local(
        kernel,
        "gradient_parts",
        [vmem(rank, width), vmem(rank, width)],
        ins=(*lows, tokens, *flags),
        ties=ties,
    )


def join(*sums, ties=(), passed=()):
    terms = [x for group in sums for x in group]

    def kernel(*refs):
        refs, outs = list(refs[: len(terms)]), refs[len(terms) :]
        for group, out in zip(sums, outs):
            total = functools.reduce(jnp.add, [f32(refs.pop(0)[...]) for _ in group])
            out[...] = total.astype(out.dtype)

    return local(
        kernel, "join", [vmem(*g[0].shape) for g in sums], ins=terms, ties=ties, passed=passed
    )


def chosen_factor(state, own, other, flags, half, ties=(), after=(), passed=()):
    rank, width = own[0].shape
    n_own, n_other = len(own), len(other)

    def total(refs, tile):
        return f32(functools.reduce(jnp.add, [f32(x[:, tile]) for x in refs]).astype(jnp.bfloat16))

    def kernel(*refs):
        state, own, other = refs[:3], refs[3 : 3 + n_own], refs[3 + n_own : 3 + n_own + n_other]
        flags, out = refs[3 + n_own + n_other :]
        p = jnp.max(flag(flags, "proj", rank)[0:1, :])
        for tile in column_tiles(width):
            grad = total(own, tile)
            if other:
                mine = flag(flags, "proj", rank) == half(flags, rank)
                grad = jnp.where(mine, grad, total(other, tile))
            held = [x[p, :, tile] for x in state]
            out[:, tile] = moment_update(*held, grad)[0].astype(out.dtype)

    return local(
        kernel,
        "chosen_factor",
        [vmem(rank, width)],
        ins=(*state, *own, *other, flags),
        ties=ties,
        after=after,
        passed=passed,
    )


def adam(state, own, other, flags, half, ties=()):
    rank, width = own.shape
    cuts = max(1, width // 1024)
    cut = width // cuts

    def kernel(*refs):
        state, own, other, flags, outs, (fresh, sems) = refs[:3], *refs[3:6], refs[-5:-2], refs[-2:]
        kept = half(flags, rank)
        copies = []
        for k in range(cuts):
            for j in range(k * cut, (k + 1) * cut, 128):
                tile = pl.ds(j, 128)
                grads = f32(own[:, tile]), f32(other[:, tile])
                for p in range(2):
                    grad = jnp.where(kept == p, *grads)
                    values = moment_update(*[x[p, :, tile] for x in state], grad)
                    for i, value in enumerate(values):
                        fresh[i, p, :, tile] = value
            span = pl.ds(k * cut, cut)
            for i, x in enumerate(outs):
                copies.append(
                    pltpu.make_async_copy(fresh.at[i, :, :, span], x.at[:, :, span], sems.at[k, i])
                )
                copies[-1].start()
        for copy in copies:
            copy.wait()

    in_vmem = (*state, own, other, flags, *ties)
    return pl.pallas_call(
        kernel,
        in_specs=[pl.BlockSpec(memory_space=pltpu.VMEM)] * 6
        + [pl.BlockSpec(memory_space=pl.ANY)] * len(ties),
        out_specs=[pl.BlockSpec(memory_space=pltpu.HBM)] * 3,
        out_shape=[pltpu.HBM(x.shape, x.dtype) for x in state],
        scratch_shapes=[
            vmem(3, 2, rank, width, dtype=jnp.float32),
            pltpu.SemaphoreType.DMA((cuts, 3)),
        ],
        compiler_params=pltpu.CompilerParams(vmem_limit_bytes=8 * MIB),
        cost_estimate=pl.CostEstimate(flops=0, bytes_accessed=1024, transcendentals=0),
        name="adam",
    )(*[pltpu.with_memory_space_constraint(x, pltpu.VMEM) for x in in_vmem])


def adam_half(state, grad, flags, half, flip, outs, after):
    rank, width = grad.shape
    cuts = max(1, width // 1024)
    cut = width // cuts

    def kernel(*refs):
        grad, flags, state = refs[0], refs[1], refs[2:5]
        targets, (fresh, sems) = refs[-5:-2], refs[-2:]
        p = jnp.max(half(flags, rank)[0:1, :]) ^ flip
        copies = []
        for k in range(cuts):
            for j in range(k * cut, (k + 1) * cut, 128):
                tile = pl.ds(j, 128)
                values = moment_update(*[x[p, :, tile] for x in state], f32(grad[:, tile]))
                for i, value in enumerate(values):
                    fresh[i, :, tile] = value
            span = pl.ds(k * cut, cut)
            for i, x in enumerate(targets):
                copies.append(
                    pltpu.make_async_copy(fresh.at[i, :, span], x.at[p, :, span], sems.at[k, i])
                )
                copies[-1].start()
        for copy in copies:
            copy.wait()

    in_vmem, in_hbm = (grad, flags, *state), (*after, *outs)
    first = len(in_vmem) + len(after)
    return pl.pallas_call(
        kernel,
        in_specs=[pl.BlockSpec(memory_space=pltpu.VMEM)] * len(in_vmem)
        + [pl.BlockSpec(memory_space=pltpu.HBM)] * len(in_hbm),
        out_specs=[pl.BlockSpec(memory_space=pltpu.HBM)] * 3,
        out_shape=[pltpu.HBM(x.shape, x.dtype) for x in state],
        input_output_aliases={first + i: i for i in range(3)},
        scratch_shapes=[
            vmem(3, rank, width, dtype=jnp.float32),
            pltpu.SemaphoreType.DMA((cuts, 3)),
        ],
        compiler_params=pltpu.CompilerParams(vmem_limit_bytes=8 * MIB),
        cost_estimate=pl.CostEstimate(flops=0, bytes_accessed=1024, transcendentals=0),
        name="adam_half",
    )(
        *[pltpu.with_memory_space_constraint(x, pltpu.VMEM) for x in in_vmem],
        *[pltpu.with_memory_space_constraint(x, pltpu.HBM) for x in in_hbm],
    )


def pick(flags, name, held, ids, rank):
    wanted = flag(flags, name, rank)

    def tile_of(tile):
        found = f32(held[0][:, tile])
        for i in range(1, len(held)):
            found = jnp.where(wanted == ids[i], f32(held[i][:, tile]), found)
        return found

    return tile_of


def block_ids(t_size, many):
    t = lax.axis_index("tensor")
    ids, distance = [t], 1
    while distance < t_size // 2:
        ids = ids + [i ^ distance for i in ids]
        distance *= 2
    return ids[:many]


def offer(held, flags, t_size, ties=()):
    rank, width = held[0].shape

    def kernel(*refs):
        held, flags, out = refs[:-2], refs[-2], refs[-1]
        tile_of = pick(flags, "partners", held, block_ids(t_size, len(held)), rank)
        for tile in column_tiles(width):
            out[:, tile] = tile_of(tile).astype(out.dtype)

    return local(kernel, "offer", [vmem(rank, width)], ins=(*held, flags), ties=ties)


def columns_of_b(held, flags, t_size, after=()):
    rank, width = held[0].shape

    def kernel(*refs):
        held, flags, cols = refs[:-2], refs[-2], refs[-1]
        ids = block_ids(t_size, len(held) - 1)
        tile_of = pick(flags, "mine", (held[-1], *held[:-1]), (None, *ids), rank)
        for tile in column_tiles(width):
            cols[:, tile] = (adapter_scale * tile_of(tile)).astype(cols.dtype)

    return local(
        kernel, "columns_of_b", [vmem(rank, width)], ins=(*held, flags), after=after
    )[0]


def rows_of_a(block, came, t_size, r_size):
    rank, height = block.shape

    def kernel(*refs):
        block, came, left = refs[0], refs[1:-1], refs[-1]
        root = is_root(t_size, r_size)
        for j in range(0, height, 128):
            tile = pl.ds(j, 128)
            got = functools.reduce(jnp.add, [f32(x[:, tile]) for x in came])
            rows = jnp.where(root, f32(block[:, tile]), got).astype(left.dtype)
            left[tile, :] = rows.T

    return local(kernel, "rows_of_a", [vmem(height, rank)], ins=(block, *came))[0]


def refresh(left, cols, flags, weight, state, grad, half):
    height, width = weight.shape
    rank = cols.shape[0]
    block = min(height, 512)
    steps = height // block
    slots = min(3, steps)
    groups = max(1, width // 1024)
    group = width // groups
    chunks = max(1, width // 1024)
    cut, apart = width // chunks, max(1, (steps - 2) // chunks)
    turns = [min(1 + apart * k, steps - 1) for k in range(chunks)]

    def kernel(*refs):
        left, cols, flags, weight, grad, *state = refs[:8]
        out, targets, (ring, sems, fresh, fresh_sems) = refs[8], refs[9:12], refs[12:]
        step = pl.program_id(0)
        slot = step % slots

        def emit(i, g):
            at, span = pl.ds(pl.multiple_of(i * block, block), block), pl.ds(g * group, group)
            return pltpu.make_async_copy(
                ring.at[i % slots, :, span], out.at[at, span], sems.at[i % slots, g]
            )

        def writes(p, k):
            span = pl.ds(k * cut, cut)
            return [
                pltpu.make_async_copy(fresh.at[i, :, span], x.at[p, :, span], fresh_sems.at[i, k])
                for i, x in enumerate(targets)
            ]

        @pl.when(step >= slots)
        def _():
            for g in range(groups):
                emit(step - slots, g).wait()

        wide = min(width, 256)
        at = pl.ds(pl.multiple_of(step * block, block), block)
        for g in range(groups):
            for k in range(g * group, (g + 1) * group, wide):
                span = pl.ds(k, wide)
                change = jnp.dot(left[at, :], cols[:, span], preferred_element_type=jnp.float32)
                ring[slot, :, span] = (f32(weight[at, span]) + change).astype(ring.dtype)
            emit(step, g).start()

        for chunk, turn in enumerate(turns):

            @pl.when(step == turn)
            def _():
                p = jnp.max(half(flags, rank)[0:1, :])
                for k in range(chunk * cut, (chunk + 1) * cut, 128):
                    tile = pl.ds(k, 128)
                    values = moment_update(*[x[p, :, tile] for x in state], f32(grad[:, tile]))
                    for i, value in enumerate(values):
                        fresh[i, :, tile] = value
                for copy in writes(p, chunk):
                    copy.start()

        @pl.when(step == steps - 1)
        def _():
            p = jnp.max(half(flags, rank)[0:1, :])
            for k in range(chunks):
                for copy in writes(p, k):
                    copy.wait()
            for i in range(steps - slots, steps):
                for g in range(groups):
                    emit(i, g).wait()

    operands = (left, cols, flags, weight, grad, *state)
    outs = [pltpu.HBM((height, width), weight.dtype)] + [pltpu.HBM(x.shape, x.dtype) for x in state]
    result, *fresh = pl.pallas_call(
        kernel,
        grid=(steps,),
        in_specs=[pl.BlockSpec(memory_space=pltpu.VMEM)] * len(operands),
        out_specs=[pl.BlockSpec(memory_space=pltpu.HBM)] * len(outs),
        out_shape=outs,
        scratch_shapes=[
            vmem(slots, block, width),
            pltpu.SemaphoreType.DMA((slots, groups)),
            vmem(3, rank, width, dtype=jnp.float32),
            pltpu.SemaphoreType.DMA((3, chunks)),
        ],
        compiler_params=pltpu.CompilerParams(vmem_limit_bytes=16 * MIB),
        cost_estimate=pl.CostEstimate(flops=0, bytes_accessed=1024, transcendentals=0),
        name="refresh",
    )(*[pltpu.with_memory_space_constraint(x, pltpu.VMEM) for x in operands])
    return result, fresh


def tensor_sum_parts(low, size):
    parts, stride = [low], 1
    while stride < size:
        if len(parts) > 1:
            total = functools.reduce(jnp.add, [f32(x) for x in parts])
            parts = [total.astype(jnp.bfloat16)]
        radix = min(4, size // stride)
        mine = parts[0]
        for hop in range(1, radix):
            pairs = [
                (i, i - i % (stride * radix) + (i + hop * stride) % (stride * radix))
                for i in range(size)
            ]
            parts.append(lax.ppermute(mine, "tensor", pairs))
        stride *= radix
    return parts


def toward(block, distance, t_size, r_size, first):
    pairs = []
    for t in range(t_size):
        root = t * r_size // t_size
        for r in range(r_size):
            same_side = ((r ^ root) & distance) == 0
            same_half = (r ^ root) % 2 == 0
            if (same_side != same_half) == first:
                pairs.append((t * r_size + r, t * r_size + (r ^ distance)))
    return lax.ppermute(block, ("tensor", "replica"), pairs)


def gather_rows(block, t_size, r_size):
    t = lax.axis_index("tensor")
    distance = 1
    while distance < max(1, t_size // r_size):
        other = swap(block, "tensor", t_size, distance)
        block = jnp.where(
            (t & distance) == 0,
            jnp.concatenate([block, other], axis=1),
            jnp.concatenate([other, block], axis=1),
        )
        distance *= 2
    return block


def is_root(t_size, r_size):
    t, r = lax.axis_index("tensor"), lax.axis_index("replica")
    many = max(1, t_size // r_size)
    return t // many == r * t_size // r_size // many


def spread(block, t_size, r_size):
    many = max(1, t_size // r_size)
    came = []
    for shift in range(many, t_size, many):
        pairs = []
        for r in range(r_size):
            first = r * t_size // r_size
            for t in range(first, first + many):
                pairs.append((t * r_size + r, (t ^ shift) * r_size + r))
        came.append(lax.ppermute(block, ("tensor", "replica"), pairs))
    return came


def own_rows(block, t_size, r_size):
    parts = max(1, r_size // t_size)
    if parts == 1:
        return block
    size = block.shape[1] // parts
    return lax.dynamic_slice_in_dim(block, (lax.axis_index("replica") % parts) * size, size, 1)


def per_device(
    acts,
    cots,
    down_factor,
    up_factor,
    down_first_moment,
    down_second_moment,
    up_first_moment,
    up_second_moment,
    rollout_weight,
    owner,
    projection_index,
):
    t_size, r_size = lax.axis_size("tensor"), lax.axis_size("replica")
    turn = lambda x: jnp.transpose(x, (0, 2, 1))
    down_state = tuple(map(turn, (down_factor, down_first_moment, down_second_moment)))
    up_state = (up_factor, up_first_moment, up_second_moment)
    coefficient = adapter_scale / (acts.shape[1] * r_size)
    down_half = functools.partial(down_parity, t_size=t_size, r_size=r_size)
    up_half = functools.partial(up_parity, t_size=t_size, r_size=r_size)
    exchange = lambda x, distance: swap(x, "replica", r_size, distance)

    low, acts_in, cots_in = low_parts(acts, cots, down_state[0], up_state[0])
    lows = tensor_sum_parts(low, t_size)
    up_send, up_own = gradient_parts(
        lows, cots_in, (), 2, coefficient, up_half,
    )
    up_came = exchange(up_send, 1)
    down_held, up_held, flags = load_state(
        down_state, up_state, projection_index, owner, t_size, r_size, up_send
    )
    down_send, down_own = gradient_parts(lows, acts_in, (flags,), 0, coefficient, down_half)
    up_own, down_send = join((up_own, up_came), passed=(down_send,))
    up_came, distance = exchange(up_own, 2), 4
    down_came = exchange(down_send, 1)
    while distance < r_size:
        (up_own,) = join((up_own, up_came))
        up_came, distance = exchange(up_own, distance), 2 * distance
    down_own, again = join(*[(down_own, down_came)] * 2)
    (up_own,) = join((up_own, up_came), ties=(down_own,))
    up_other = exchange(up_own, 1)
    distance = 2
    while 2 * distance < r_size:
        down_own, again = join(*[(down_own, exchange(down_own, distance))] * 2)
        distance *= 2
    down_first = toward(down_own, distance, t_size, r_size, True)

    (block,) = chosen_factor(down_held, [down_own, down_first], [], flags, down_half)
    block = own_rows(gather_rows(block, t_size, r_size), t_size, r_size)
    came = spread(block, t_size, r_size)
    up_mine, again = chosen_factor(
        up_held, [up_own], [up_other], flags, up_half, ties=(block,), passed=(again,)
    )
    down_rest = toward(again, distance, t_size, r_size, False)
    held, shift = [up_mine], 1
    while shift < t_size // 2:
        held = held + [swap(x, "tensor", t_size, shift) for x in held]
        shift *= 2
    left = rows_of_a(block, came, t_size, r_size)
    (offered,) = offer(held, flags, t_size, ties=(left,))
    held = held + [swap(offered, "tensor", t_size, t_size // 2)]
    (down_own,) = join((down_own, down_first, down_rest), ties=(offered,))
    down_other = exchange(down_own, 1)
    fresh_up = adam(up_held, up_own, up_other, flags, up_half, ties=(down_own,))
    cols = columns_of_b(held, flags, t_size, after=(fresh_up[0],))
    fresh_rollout_weight, fresh_down = refresh(
        left, cols, flags, rollout_weight, down_held, down_own, down_half
    )
    fresh_down = adam_half(
        down_held, down_other, flags, down_half, 1, fresh_down, (fresh_rollout_weight,)
    )
    return (
        turn(fresh_down[0]),
        fresh_up[0],
        turn(fresh_down[1]),
        turn(fresh_down[2]),
        fresh_up[1],
        fresh_up[2],
        fresh_rollout_weight,
    )


def solution(mesh):
    placed = (
        P(None, ("groups", "replica"), "tensor"),
        P(None, ("groups", "replica"), "tensor"),
        P("groups", "tensor", None),
        P("groups", None, "tensor"),
        P("groups", "tensor", None),
        P("groups", "tensor", None),
        P("groups", None, "tensor"),
        P("groups", None, "tensor"),
        P("replica", "tensor"),
        P(),
        P("groups"),
    )
    return jax.shard_map(
        per_device,
        mesh=mesh,
        in_specs=placed,
        out_specs=(
            P("groups", "tensor", None),
            P("groups", None, "tensor"),
            P("groups", "tensor", None),
            P("groups", "tensor", None),
            P("groups", None, "tensor"),
            P("groups", None, "tensor"),
            P(("groups", "replica"), "tensor"),
        ),
        check_vma=False,
    )
```

```python
import functools

import jax
import jax.numpy as jnp
from jax import lax
from jax.experimental import pallas as pl
from jax.experimental.pallas import tpu as pltpu
from jax.sharding import PartitionSpec as P

adapter_scale = 2.0
learn_rate = 0.05
beta_one = 0.9
beta_two = 0.999
adam_eps = 1e-08
fix_one = 1.0 - 0.9**10
fix_two = 1.0 - 0.999**10

MIB = 1024 * 1024
FLAGS = ("proj", "column_proj", "mine", "partners")


def moment_update(param, first, second, grad):
    first_new = beta_one * first + (1.0 - beta_one) * grad
    second_new = beta_two * second + (1.0 - beta_two) * grad * grad
    size = second_new * (1.0 / fix_two)
    param_new = param - (learn_rate / fix_one) * first_new / (size * lax.rsqrt(size) + adam_eps)
    return (param_new, first_new, second_new)


def f32(x):
    return x.astype(jnp.float32)


def swap(x, axis, size, distance):
    return lax.ppermute(x, axis, [(i, i ^ distance) for i in range(size)])


def vmem(*shape, dtype=jnp.bfloat16):
    return pltpu.VMEM(shape, dtype)


def local(kernel, name, outs, ins=(), hbm=(), smem=(), ties=(), after=(), passed=(), scratch=(), work=1024):
    n_ins, n_first = len(ins), len(ins) + len(hbm) + len(smem)
    n_outs = len(outs)

    def body(*refs):
        front = refs[:n_first]
        rest = refs[n_first + len(ties) + len(after) + len(passed) :]
        kernel(*front, *rest[:n_outs], *rest[n_outs + len(passed) :])

    operands = (
        [pltpu.with_memory_space_constraint(x, pltpu.VMEM) for x in ins]
        + [pltpu.with_memory_space_constraint(x, pltpu.HBM) for x in hbm]
        + [pltpu.with_memory_space_constraint(x, pltpu.HBM) for x in smem]
        + [pltpu.with_memory_space_constraint(x, pltpu.VMEM) for x in ties]
        + [pltpu.with_memory_space_constraint(x, pltpu.HBM) for x in after]
        + [pltpu.with_memory_space_constraint(x, pltpu.VMEM) for x in passed]
    )
    specs = (
        [pl.BlockSpec(memory_space=pltpu.VMEM)] * n_ins
        + [pl.BlockSpec(memory_space=pltpu.HBM)] * len(hbm)
        + [pl.BlockSpec(memory_space=pltpu.SMEM)] * len(smem)
        + [pl.BlockSpec(memory_space=pl.ANY)] * (len(ties) + len(after) + len(passed))
    )
    first_passed = n_first + len(ties) + len(after)
    return pl.pallas_call(
        body,
        in_specs=specs,
        out_specs=[pl.BlockSpec(memory_space=pltpu.VMEM)] * n_outs
        + [pl.BlockSpec(memory_space=pl.ANY)] * len(passed),
        out_shape=list(outs) + [pltpu.VMEM(x.shape, x.dtype) for x in passed],
        input_output_aliases={first_passed + i: n_outs + i for i in range(len(passed))},
        scratch_shapes=list(scratch),
        compiler_params=pltpu.CompilerParams(vmem_limit_bytes=8 * MIB),
        cost_estimate=pl.CostEstimate(flops=0, bytes_accessed=work, transcendentals=0),
        name=name,
    )(*operands)


def low_parts(acts, cots, down, up):
    tokens = acts.shape[1]
    rank = down.shape[1]

    def kernel(acts, cots, down, up, low, acts_in, cots_in, down_in, up_in, sems):
        jobs = []
        for spot, (x, x_in, f, f_in) in enumerate(
            ((cots, cots_in, up, up_in), (acts, acts_in, down, down_in))
        ):
            for p in range(2):
                i = 2 * spot + p
                pair = (
                    pltpu.make_async_copy(x.at[p], x_in.at[p], sems.at[2 * i]),
                    pltpu.make_async_copy(f.at[p], f_in.at[p], sems.at[2 * i + 1]),
                )
                for copy in pair:
                    copy.start()
                jobs.append((pair, x_in, f_in, p, i))
        for pair, x_in, f_in, p, i in jobs:
            for copy in pair:
                copy.wait()
            low[pl.ds(i * rank, rank), :] = lax.dot_general(
                f_in[p].astype(jnp.bfloat16),
                x_in[p],
                (((1,), (1,)), ((), ())),
                preferred_element_type=jnp.float32,
            ).astype(low.dtype)

    return local(
        kernel,
        "low_parts",
        [vmem(4 * rank, tokens), vmem(*acts.shape), vmem(*cots.shape)],
        hbm=(acts, cots, down, up),
        scratch=[
            vmem(*down.shape, dtype=jnp.float32),
            vmem(*up.shape, dtype=jnp.float32),
            pltpu.SemaphoreType.DMA((8,)),
        ],
    )


def load_state(down_state, up_state, projection_index, owner, t_size, r_size, tie):
    rank = down_state[0].shape[1]

    def kernel(*refs):
        sources, (index, owner), targets, (flags, sems) = refs[:6], refs[6:8], refs[8:14], refs[14:]
        copies = [
            pltpu.make_async_copy(x, y, sems.at[i]) for i, (x, y) in enumerate(zip(sources, targets))
        ]
        for copy in copies:
            copy.start()
        t, r = lax.axis_index("tensor"), lax.axis_index("replica")
        values = (index[r], index[t * r_size // t_size], owner[t], owner[t ^ (t_size // 2)])
        for i, value in enumerate(values):
            flags[pl.ds(i * rank, rank), :] = jnp.full((rank, 128), value, jnp.int32)
        for copy in copies:
            copy.wait()

    *state, flags = local(
        kernel,
        "load_state",
        [vmem(*x.shape, dtype=jnp.float32) for x in (*down_state, *up_state)]
        + [vmem(len(FLAGS) * rank, 128, dtype=jnp.int32)],
        hbm=(*down_state, *up_state),
        smem=(projection_index, owner),
        ties=(tie,),
        scratch=[pltpu.SemaphoreType.DMA((6,))],
    )
    return state[:3], state[3:], flags


def flag(flags, name, rank):
    return flags[pl.ds(FLAGS.index(name) * rank, rank), :]


def column_tiles(width):
    return [pl.ds(k, 128) for k in range(0, width, 128)]


def down_parity(flags, rank, t_size, r_size):
    t, r = lax.axis_index("tensor"), lax.axis_index("replica")
    return flag(flags, "column_proj", rank) ^ ((r + t * r_size // t_size) % 2)


def up_parity(flags, rank, t_size, r_size):
    r = lax.axis_index("replica")
    return jnp.full((rank, 128), r % 2, jnp.int32)


def gradient_parts(lows, tokens, flags, base, coefficient, half, ties=()):
    rank = lows[0].shape[0] // 4
    width = tokens.shape[2]
    parts = len(lows)

    def kernel(*refs):
        lows, tokens, flags, (send, keep) = refs[:parts], refs[parts], refs[parts + 1 : -2], refs[-2:]
        rows = pl.ds(base * rank, 2 * rank)
        total = functools.reduce(jnp.add, [f32(x[rows, :]) for x in lows]).astype(jnp.bfloat16)
        kept = half(flags[0] if flags else None, rank) == 0
        cut = min(width, 512)
        for k in range(0, width, cut):
            grads = [
                coefficient
                * jnp.dot(
                    total[p * rank : (p + 1) * rank],
                    tokens[p, :, pl.ds(k, cut)],
                    preferred_element_type=jnp.float32,
                )
                for p in range(2)
            ]
            for j in range(0, cut, 128):
                first, second = [g[:, j : j + 128] for g in grads]
                tile = pl.ds(k + j, 128)
                keep[:, tile] = jnp.where(kept, first, second).astype(keep.dtype)
                send[:, tile] = jnp.where(kept, second, first).astype(send.dtype)

    return local(
        kernel,
        "gradient_parts",
        [vmem(rank, width), vmem(rank, width)],
        ins=(*lows, tokens, *flags),
        ties=ties,
    )


def join(*sums, ties=(), after=(), passed=()):
    terms = [x for group in sums for x in group]

    def kernel(*refs):
        refs, outs = list(refs[: len(terms)]), refs[len(terms) :]
        for group, out in zip(sums, outs):
            total = functools.reduce(jnp.add, [f32(refs.pop(0)[...]) for _ in group])
            out[...] = total.astype(out.dtype)

    return local(
        kernel,
        "join",
        [vmem(*group[0].shape) for group in sums],
        ins=terms,
        ties=ties,
        after=after,
        passed=passed,
    )


def chosen_factor(state, own, other, flags, half, ties=(), after=(), passed=()):
    rank, width = own[0].shape
    n_own, n_other = len(own), len(other)

    def total(refs, tile):
        return f32(functools.reduce(jnp.add, [f32(x[:, tile]) for x in refs]).astype(jnp.bfloat16))

    def kernel(*refs):
        state, own, other = refs[:3], refs[3 : 3 + n_own], refs[3 + n_own : 3 + n_own + n_other]
        flags, out = refs[3 + n_own + n_other :]
        p = jnp.max(flag(flags, "proj", rank)[0:1, :])
        for tile in column_tiles(width):
            grad = total(own, tile)
            if other:
                mine = flag(flags, "proj", rank) == half(flags, rank)
                grad = jnp.where(mine, grad, total(other, tile))
            held = [x[p, :, tile] for x in state]
            out[:, tile] = moment_update(*held, grad)[0].astype(out.dtype)

    return local(
        kernel,
        "chosen_factor",
        [vmem(rank, width)],
        ins=(*state, *own, *other, flags),
        ties=ties,
        after=after,
        passed=passed,
    )


def adam(state, own, other, flags, half, ties=()):
    rank, width = own.shape
    cuts = max(1, width // 1024)
    cut = width // cuts

    def kernel(*refs):
        state, own, other, flags, outs, (fresh, sems) = refs[:3], *refs[3:6], refs[-5:-2], refs[-2:]
        kept = half(flags, rank)
        copies = []
        for k in range(cuts):
            for j in range(k * cut, (k + 1) * cut, 128):
                tile = pl.ds(j, 128)
                grads = f32(own[:, tile]), f32(other[:, tile])
                for p in range(2):
                    grad = jnp.where(kept == p, *grads)
                    values = moment_update(*[x[p, :, tile] for x in state], grad)
                    for i, value in enumerate(values):
                        fresh[i, p, :, tile] = value
            span = pl.ds(k * cut, cut)
            for i, x in enumerate(outs):
                copies.append(
                    pltpu.make_async_copy(fresh.at[i, :, :, span], x.at[:, :, span], sems.at[k, i])
                )
                copies[-1].start()
        for copy in copies:
            copy.wait()

    in_vmem = (*state, own, other, flags, *ties)
    return pl.pallas_call(
        kernel,
        in_specs=[pl.BlockSpec(memory_space=pltpu.VMEM)] * 6
        + [pl.BlockSpec(memory_space=pl.ANY)] * len(ties),
        out_specs=[pl.BlockSpec(memory_space=pltpu.HBM)] * 3,
        out_shape=[pltpu.HBM(x.shape, x.dtype) for x in state],
        scratch_shapes=[
            vmem(3, 2, rank, width, dtype=jnp.float32),
            pltpu.SemaphoreType.DMA((cuts, 3)),
        ],
        compiler_params=pltpu.CompilerParams(vmem_limit_bytes=8 * MIB),
        cost_estimate=pl.CostEstimate(flops=0, bytes_accessed=1024, transcendentals=0),
        name="adam",
    )(*[pltpu.with_memory_space_constraint(x, pltpu.VMEM) for x in in_vmem])


def adam_half(state, grad, flags, half, flip, outs, after):
    rank, width = grad.shape
    cuts = max(1, width // 1024)
    cut = width // cuts

    def kernel(*refs):
        grad, flags, state = refs[0], refs[1], refs[2:5]
        targets, (fresh, sems) = refs[-5:-2], refs[-2:]
        p = jnp.max(half(flags, rank)[0:1, :]) ^ flip
        copies = []
        for k in range(cuts):
            for j in range(k * cut, (k + 1) * cut, 128):
                tile = pl.ds(j, 128)
                values = moment_update(*[x[p, :, tile] for x in state], f32(grad[:, tile]))
                for i, value in enumerate(values):
                    fresh[i, :, tile] = value
            span = pl.ds(k * cut, cut)
            for i, x in enumerate(targets):
                copies.append(
                    pltpu.make_async_copy(fresh.at[i, :, span], x.at[p, :, span], sems.at[k, i])
                )
                copies[-1].start()
        for copy in copies:
            copy.wait()

    in_vmem, in_hbm = (grad, flags, *state), (*after, *outs)
    first = len(in_vmem) + len(after)
    return pl.pallas_call(
        kernel,
        in_specs=[pl.BlockSpec(memory_space=pltpu.VMEM)] * len(in_vmem)
        + [pl.BlockSpec(memory_space=pltpu.HBM)] * len(in_hbm),
        out_specs=[pl.BlockSpec(memory_space=pltpu.HBM)] * 3,
        out_shape=[pltpu.HBM(x.shape, x.dtype) for x in state],
        input_output_aliases={first + i: i for i in range(3)},
        scratch_shapes=[
            vmem(3, rank, width, dtype=jnp.float32),
            pltpu.SemaphoreType.DMA((cuts, 3)),
        ],
        compiler_params=pltpu.CompilerParams(vmem_limit_bytes=8 * MIB),
        cost_estimate=pl.CostEstimate(flops=0, bytes_accessed=1024, transcendentals=0),
        name="adam_half",
    )(
        *[pltpu.with_memory_space_constraint(x, pltpu.VMEM) for x in in_vmem],
        *[pltpu.with_memory_space_constraint(x, pltpu.HBM) for x in in_hbm],
    )


def pick(flags, name, held, ids, rank):
    wanted = flag(flags, name, rank)

    def tile_of(tile):
        found = f32(held[0][:, tile])
        for i in range(1, len(held)):
            found = jnp.where(wanted == ids[i], f32(held[i][:, tile]), found)
        return found

    return tile_of


def block_ids(t_size, many):
    t = lax.axis_index("tensor")
    ids, distance = [t], 1
    while distance < t_size // 2:
        ids = ids + [i ^ distance for i in ids]
        distance *= 2
    return ids[:many]


def offer(held, flags, t_size, ties=()):
    rank, width = held[0].shape

    def kernel(*refs):
        held, flags, out = refs[:-2], refs[-2], refs[-1]
        tile_of = pick(flags, "partners", held, block_ids(t_size, len(held)), rank)
        for tile in column_tiles(width):
            out[:, tile] = tile_of(tile).astype(out.dtype)

    return local(kernel, "offer", [vmem(rank, width)], ins=(*held, flags), ties=ties)


def columns_of_b(held, flags, t_size, after=()):
    rank, width = held[0].shape

    def kernel(*refs):
        held, flags, cols = refs[:-2], refs[-2], refs[-1]
        ids = block_ids(t_size, len(held) - 1)
        tile_of = pick(flags, "mine", (held[-1], *held[:-1]), (None, *ids), rank)
        for tile in column_tiles(width):
            cols[:, tile] = (adapter_scale * tile_of(tile)).astype(cols.dtype)

    return local(
        kernel, "columns_of_b", [vmem(rank, width)], ins=(*held, flags), after=after
    )[0]


def rows_of_a(block):
    rank, height = block.shape

    def kernel(block, left):
        for j in range(0, height, 128):
            tile = pl.ds(j, 128)
            left[tile, :] = block[:, tile].T

    return local(kernel, "rows_of_a", [vmem(height, rank)], ins=(block,))[0]


def refresh(left, cols, flags, weight, state, grad, half):
    height, width = weight.shape
    rank = cols.shape[0]
    block = min(height, 512)
    steps = height // block
    slots = min(3, steps)
    groups = max(1, width // 1024)
    group = width // groups
    chunks = max(1, width // 1024)
    cut, apart = width // chunks, max(1, (steps - 2) // chunks)
    turns = [min(1 + apart * k, steps - 1) for k in range(chunks)]

    def kernel(*refs):
        left, cols, flags, weight, grad, *state = refs[:8]
        out, targets, (ring, sems, fresh, fresh_sems) = refs[8], refs[9:12], refs[12:]
        step = pl.program_id(0)
        slot = step % slots

        def emit(i, g):
            at, span = pl.ds(pl.multiple_of(i * block, block), block), pl.ds(g * group, group)
            return pltpu.make_async_copy(
                ring.at[i % slots, :, span], out.at[at, span], sems.at[i % slots, g]
            )

        def writes(p, k):
            span = pl.ds(k * cut, cut)
            return [
                pltpu.make_async_copy(fresh.at[i, :, span], x.at[p, :, span], fresh_sems.at[i, k])
                for i, x in enumerate(targets)
            ]

        @pl.when(step >= slots)
        def _():
            for g in range(groups):
                emit(step - slots, g).wait()

        wide = min(width, 256)
        at = pl.ds(pl.multiple_of(step * block, block), block)
        for g in range(groups):
            for k in range(g * group, (g + 1) * group, wide):
                span = pl.ds(k, wide)
                change = jnp.dot(left[at, :], cols[:, span], preferred_element_type=jnp.float32)
                ring[slot, :, span] = (f32(weight[at, span]) + change).astype(ring.dtype)
            emit(step, g).start()

        for chunk, turn in enumerate(turns):

            @pl.when(step == turn)
            def _():
                p = jnp.max(half(flags, rank)[0:1, :])
                for k in range(chunk * cut, (chunk + 1) * cut, 128):
                    tile = pl.ds(k, 128)
                    values = moment_update(*[x[p, :, tile] for x in state], f32(grad[:, tile]))
                    for i, value in enumerate(values):
                        fresh[i, :, tile] = value
                for copy in writes(p, chunk):
                    copy.start()

        @pl.when(step == steps - 1)
        def _():
            p = jnp.max(half(flags, rank)[0:1, :])
            for k in range(chunks):
                for copy in writes(p, k):
                    copy.wait()
            for i in range(steps - slots, steps):
                for g in range(groups):
                    emit(i, g).wait()

    operands = (left, cols, flags, weight, grad, *state)
    outs = [pltpu.HBM((height, width), weight.dtype)] + [pltpu.HBM(x.shape, x.dtype) for x in state]
    result, *fresh = pl.pallas_call(
        kernel,
        grid=(steps,),
        in_specs=[pl.BlockSpec(memory_space=pltpu.VMEM)] * len(operands),
        out_specs=[pl.BlockSpec(memory_space=pltpu.HBM)] * len(outs),
        out_shape=outs,
        scratch_shapes=[
            vmem(slots, block, width),
            pltpu.SemaphoreType.DMA((slots, groups)),
            vmem(3, rank, width, dtype=jnp.float32),
            pltpu.SemaphoreType.DMA((3, chunks)),
        ],
        compiler_params=pltpu.CompilerParams(vmem_limit_bytes=16 * MIB),
        cost_estimate=pl.CostEstimate(flops=0, bytes_accessed=1024, transcendentals=0),
        name="refresh",
    )(*[pltpu.with_memory_space_constraint(x, pltpu.VMEM) for x in operands])
    return result, fresh


def tensor_sum_parts(low, size):
    parts, stride = [low], 1
    while stride < size:
        if len(parts) > 1:
            total = functools.reduce(jnp.add, [f32(x) for x in parts])
            parts = [total.astype(jnp.bfloat16)]
        radix = min(4, size // stride)
        mine = parts[0]
        for hop in range(1, radix):
            pairs = [
                (i, i - i % (stride * radix) + (i + hop * stride) % (stride * radix))
                for i in range(size)
            ]
            parts.append(lax.ppermute(mine, "tensor", pairs))
        stride *= radix
    return parts


def toward(block, distance, t_size, r_size, first):
    pairs = []
    for t in range(t_size):
        root = t * r_size // t_size
        for r in range(r_size):
            same_side = ((r ^ root) & distance) == 0
            same_half = (r ^ root) % 2 == 0
            if (same_side != same_half) == first:
                pairs.append((t * r_size + r, t * r_size + (r ^ distance)))
    return lax.ppermute(block, ("tensor", "replica"), pairs)


def gather_rows(block, t_size, r_size):
    t = lax.axis_index("tensor")
    distance = 1
    while distance < max(1, t_size // r_size):
        other = swap(block, "tensor", t_size, distance)
        block = jnp.where(
            (t & distance) == 0,
            jnp.concatenate([block, other], axis=1),
            jnp.concatenate([other, block], axis=1),
        )
        distance *= 2
    return block


def spread_steps(t_size, r_size):
    distance, steps = t_size // 2, []
    while distance >= max(1, t_size // r_size):
        steps.append(distance)
        distance //= 2
    return steps


def spread(block, distance, t_size, r_size, ties=()):
    rest = functools.reduce(
        lambda a, b: a | b, [d for d in spread_steps(t_size, r_size) if d <= distance]
    )
    pairs = []
    for r in range(r_size):
        root = r * t_size // r_size
        for t in range(t_size):
            if (t ^ root) & rest == 0:
                pairs.append((t * r_size + r, (t ^ distance) * r_size + r))
    came = lax.ppermute(block, ("tensor", "replica"), pairs)

    def kernel(came, block, out):
        t, r = lax.axis_index("tensor"), lax.axis_index("replica")
        takes = ((t ^ (r * t_size // r_size)) & rest) == distance

        @pl.when(takes)
        def _():
            out[...] = came[...]

        @pl.when(jnp.logical_not(takes))
        def _():
            out[...] = block[...]

    return local(kernel, "spread", [vmem(*block.shape)], ins=(came, block), ties=ties)[0]


def own_rows(block, t_size, r_size):
    parts = max(1, r_size // t_size)
    if parts == 1:
        return block
    size = block.shape[1] // parts
    return lax.dynamic_slice_in_dim(block, (lax.axis_index("replica") % parts) * size, size, 1)


def per_device(
    acts,
    cots,
    down_factor,
    up_factor,
    down_first_moment,
    down_second_moment,
    up_first_moment,
    up_second_moment,
    rollout_weight,
    owner,
    projection_index,
):
    t_size, r_size = lax.axis_size("tensor"), lax.axis_size("replica")
    turn = lambda x: jnp.transpose(x, (0, 2, 1))
    down_state = tuple(map(turn, (down_factor, down_first_moment, down_second_moment)))
    up_state = (up_factor, up_first_moment, up_second_moment)
    coefficient = adapter_scale / (acts.shape[1] * r_size)
    down_half = functools.partial(down_parity, t_size=t_size, r_size=r_size)
    up_half = functools.partial(up_parity, t_size=t_size, r_size=r_size)
    exchange = lambda x, distance: swap(x, "replica", r_size, distance)

    low, acts_in, cots_in = low_parts(acts, cots, down_state[0], up_state[0])
    lows = tensor_sum_parts(low, t_size)
    up_send, up_own = gradient_parts(
        lows, cots_in, (), 2, coefficient, up_half,
    )
    up_came = exchange(up_send, 1)
    down_held, up_held, flags = load_state(
        down_state, up_state, projection_index, owner, t_size, r_size, up_send
    )
    down_send, down_own = gradient_parts(lows, acts_in, (flags,), 0, coefficient, down_half)
    up_own, down_send = join((up_own, up_came), passed=(down_send,))
    up_came, distance = exchange(up_own, 2), 4
    down_came = exchange(down_send, 1)
    while distance < r_size:
        (up_own,) = join((up_own, up_came))
        up_came, distance = exchange(up_own, distance), 2 * distance
    down_own, again = join(*[(down_own, down_came)] * 2)
    (up_own,) = join((up_own, up_came), ties=(down_own,))
    up_other = exchange(up_own, 1)
    distance = 2
    while 2 * distance < r_size:
        down_own, again = join(*[(down_own, exchange(down_own, distance))] * 2)
        distance *= 2
    down_first = toward(down_own, distance, t_size, r_size, True)

    (block,) = chosen_factor(down_held, [down_own, down_first], [], flags, down_half)
    block = gather_rows(block, t_size, r_size)
    first, *others = spread_steps(t_size, r_size)
    rows = spread(block, first, t_size, r_size)
    up_mine, again = chosen_factor(
        up_held, [up_own], [up_other], flags, up_half, ties=(block,), passed=(again,)
    )
    down_rest = toward(again, distance, t_size, r_size, False)
    held, shift = [up_mine], 1
    while shift < t_size // 2:
        held = held + [swap(x, "tensor", t_size, shift) for x in held]
        shift *= 2
    (offered,) = offer(held, flags, t_size, ties=(rows,))
    held = held + [swap(offered, "tensor", t_size, t_size // 2)]
    fresh_up = adam(up_held, up_own, up_other, flags, up_half, ties=(offered,))
    (down_own,) = join((down_own, down_first, down_rest), after=(fresh_up[0],))
    down_other = exchange(down_own, 1)
    for shift in others:
        rows = spread(rows, shift, t_size, r_size, ties=(down_own,))
    left = rows_of_a(own_rows(rows, t_size, r_size))
    cols = columns_of_b(held, flags, t_size, after=(fresh_up[0],))
    fresh_rollout_weight, fresh_down = refresh(
        left, cols, flags, rollout_weight, down_held, down_own, down_half
    )
    fresh_down = adam_half(
        down_held, down_other, flags, down_half, 1, fresh_down, (fresh_rollout_weight,)
    )
    return (
        turn(fresh_down[0]),
        fresh_up[0],
        turn(fresh_down[1]),
        turn(fresh_down[2]),
        fresh_up[1],
        fresh_up[2],
        fresh_rollout_weight,
    )


def solution(mesh):
    placed = (
        P(None, ("groups", "replica"), "tensor"),
        P(None, ("groups", "replica"), "tensor"),
        P("groups", "tensor", None),
        P("groups", None, "tensor"),
        P("groups", "tensor", None),
        P("groups", "tensor", None),
        P("groups", None, "tensor"),
        P("groups", None, "tensor"),
        P("replica", "tensor"),
        P(),
        P("groups"),
    )
    return jax.shard_map(
        per_device,
        mesh=mesh,
        in_specs=placed,
        out_specs=(
            P("groups", "tensor", None),
            P("groups", None, "tensor"),
            P("groups", "tensor", None),
            P("groups", "tensor", None),
            P("groups", None, "tensor"),
            P("groups", None, "tensor"),
            P(("groups", "replica"), "tensor"),
        ),
        check_vma=False,
    )
```

```python
import functools

import jax
import jax.numpy as jnp
from jax import lax
from jax.experimental import pallas as pl
from jax.experimental.pallas import tpu as pltpu
from jax.sharding import PartitionSpec as P

adapter_scale = 2.0
learn_rate = 0.05
beta_one = 0.9
beta_two = 0.999
adam_eps = 1e-08
fix_one = 1.0 - 0.9**10
fix_two = 1.0 - 0.999**10

MIB = 1024 * 1024
FLAGS = ("proj", "column_proj", "mine", "partners")


def moment_update(param, first, second, grad):
    first_new = beta_one * first + (1.0 - beta_one) * grad
    second_new = beta_two * second + (1.0 - beta_two) * grad * grad
    size = second_new * (1.0 / fix_two)
    param_new = param - (learn_rate / fix_one) * first_new / (size * lax.rsqrt(size) + adam_eps)
    return (param_new, first_new, second_new)


def f32(x):
    return x.astype(jnp.float32)


def swap(x, axis, size, distance):
    return lax.ppermute(x, axis, [(i, i ^ distance) for i in range(size)])


def vmem(*shape, dtype=jnp.bfloat16):
    return pltpu.VMEM(shape, dtype)


def local(kernel, name, outs, ins=(), hbm=(), smem=(), ties=(), after=(), passed=(), scratch=(), work=1024):
    n_ins, n_first = len(ins), len(ins) + len(hbm) + len(smem)
    n_outs = len(outs)

    def body(*refs):
        front = refs[:n_first]
        rest = refs[n_first + len(ties) + len(after) + len(passed) :]
        kernel(*front, *rest[:n_outs], *rest[n_outs + len(passed) :])

    operands = (
        [pltpu.with_memory_space_constraint(x, pltpu.VMEM) for x in ins]
        + [pltpu.with_memory_space_constraint(x, pltpu.HBM) for x in hbm]
        + [pltpu.with_memory_space_constraint(x, pltpu.HBM) for x in smem]
        + [pltpu.with_memory_space_constraint(x, pltpu.VMEM) for x in ties]
        + [pltpu.with_memory_space_constraint(x, pltpu.HBM) for x in after]
        + [pltpu.with_memory_space_constraint(x, pltpu.VMEM) for x in passed]
    )
    specs = (
        [pl.BlockSpec(memory_space=pltpu.VMEM)] * n_ins
        + [pl.BlockSpec(memory_space=pltpu.HBM)] * len(hbm)
        + [pl.BlockSpec(memory_space=pltpu.SMEM)] * len(smem)
        + [pl.BlockSpec(memory_space=pl.ANY)] * (len(ties) + len(after) + len(passed))
    )
    first_passed = n_first + len(ties) + len(after)
    return pl.pallas_call(
        body,
        in_specs=specs,
        out_specs=[pl.BlockSpec(memory_space=pltpu.VMEM)] * n_outs
        + [pl.BlockSpec(memory_space=pl.ANY)] * len(passed),
        out_shape=list(outs) + [pltpu.VMEM(x.shape, x.dtype) for x in passed],
        input_output_aliases={first_passed + i: n_outs + i for i in range(len(passed))},
        scratch_shapes=list(scratch),
        compiler_params=pltpu.CompilerParams(vmem_limit_bytes=8 * MIB),
        cost_estimate=pl.CostEstimate(flops=0, bytes_accessed=work, transcendentals=0),
        name=name,
    )(*operands)


def low_parts(acts, cots, down, up):
    tokens = acts.shape[1]
    rank = down.shape[1]

    def kernel(acts, cots, down, up, low, acts_in, cots_in, down_in, up_in, sems):
        jobs = []
        for spot, (x, x_in, f, f_in) in enumerate(
            ((cots, cots_in, up, up_in), (acts, acts_in, down, down_in))
        ):
            for p in range(2):
                i = 2 * spot + p
                pair = (
                    pltpu.make_async_copy(x.at[p], x_in.at[p], sems.at[2 * i]),
                    pltpu.make_async_copy(f.at[p], f_in.at[p], sems.at[2 * i + 1]),
                )
                for copy in pair:
                    copy.start()
                jobs.append((pair, x_in, f_in, p, i))
        for pair, x_in, f_in, p, i in jobs:
            for copy in pair:
                copy.wait()
            low[pl.ds(i * rank, rank), :] = lax.dot_general(
                f_in[p].astype(jnp.bfloat16),
                x_in[p],
                (((1,), (1,)), ((), ())),
                preferred_element_type=jnp.float32,
            ).astype(low.dtype)

    return local(
        kernel,
        "low_parts",
        [vmem(4 * rank, tokens), vmem(*acts.shape), vmem(*cots.shape)],
        hbm=(acts, cots, down, up),
        scratch=[
            vmem(*down.shape, dtype=jnp.float32),
            vmem(*up.shape, dtype=jnp.float32),
            pltpu.SemaphoreType.DMA((8,)),
        ],
    )


def load_state(down_state, up_state, projection_index, owner, t_size, r_size, tie):
    rank = down_state[0].shape[1]

    def kernel(*refs):
        sources, (index, owner), targets, (flags, sems) = refs[:6], refs[6:8], refs[8:14], refs[14:]
        copies = [
            pltpu.make_async_copy(x, y, sems.at[i]) for i, (x, y) in enumerate(zip(sources, targets))
        ]
        for copy in copies:
            copy.start()
        t, r = lax.axis_index("tensor"), lax.axis_index("replica")
        values = (index[r], index[t * r_size // t_size], owner[t], owner[t ^ (t_size // 2)])
        for i, value in enumerate(values):
            flags[pl.ds(i * rank, rank), :] = jnp.full((rank, 128), value, jnp.int32)
        for copy in copies:
            copy.wait()

    *state, flags = local(
        kernel,
        "load_state",
        [vmem(*x.shape, dtype=jnp.float32) for x in (*down_state, *up_state)]
        + [vmem(len(FLAGS) * rank, 128, dtype=jnp.int32)],
        hbm=(*down_state, *up_state),
        smem=(projection_index, owner),
        ties=(tie,),
        scratch=[pltpu.SemaphoreType.DMA((6,))],
    )
    return state[:3], state[3:], flags


def flag(flags, name, rank):
    return flags[pl.ds(FLAGS.index(name) * rank, rank), :]


def column_tiles(width):
    return [pl.ds(k, 128) for k in range(0, width, 128)]


def down_parity(flags, rank, t_size, r_size):
    t, r = lax.axis_index("tensor"), lax.axis_index("replica")
    return flag(flags, "column_proj", rank) ^ ((r + t * r_size // t_size) % 2)


def up_parity(flags, rank, t_size, r_size):
    r = lax.axis_index("replica")
    return jnp.full((rank, 128), r % 2, jnp.int32)


def gradient_parts(lows, tokens, flags, base, coefficient, half, ties=()):
    rank = lows[0].shape[0] // 4
    width = tokens.shape[2]
    parts = len(lows)

    def kernel(*refs):
        lows, tokens, flags, (send, keep) = refs[:parts], refs[parts], refs[parts + 1 : -2], refs[-2:]
        rows = pl.ds(base * rank, 2 * rank)
        total = functools.reduce(jnp.add, [f32(x[rows, :]) for x in lows]).astype(jnp.bfloat16)
        kept = half(flags[0] if flags else None, rank) == 0
        cut = min(width, 512)
        for k in range(0, width, cut):
            grads = [
                coefficient
                * jnp.dot(
                    total[p * rank : (p + 1) * rank],
                    tokens[p, :, pl.ds(k, cut)],
                    preferred_element_type=jnp.float32,
                )
                for p in range(2)
            ]
            for j in range(0, cut, 128):
                first, second = [g[:, j : j + 128] for g in grads]
                tile = pl.ds(k + j, 128)
                keep[:, tile] = jnp.where(kept, first, second).astype(keep.dtype)
                send[:, tile] = jnp.where(kept, second, first).astype(send.dtype)

    return local(
        kernel,
        "gradient_parts",
        [vmem(rank, width), vmem(rank, width)],
        ins=(*lows, tokens, *flags),
        ties=ties,
    )


def join(*sums, ties=(), after=(), passed=()):
    terms = [x for group in sums for x in group]

    def kernel(*refs):
        refs, outs = list(refs[: len(terms)]), refs[len(terms) :]
        for group, out in zip(sums, outs):
            total = functools.reduce(jnp.add, [f32(refs.pop(0)[...]) for _ in group])
            out[...] = total.astype(out.dtype)

    return local(
        kernel,
        "join",
        [vmem(*group[0].shape) for group in sums],
        ins=terms,
        ties=ties,
        after=after,
        passed=passed,
    )


def chosen_factor(state, own, other, flags, half, ties=(), after=(), passed=()):
    rank, width = own[0].shape
    n_own, n_other = len(own), len(other)

    def total(refs, tile):
        return f32(functools.reduce(jnp.add, [f32(x[:, tile]) for x in refs]).astype(jnp.bfloat16))

    def kernel(*refs):
        state, own, other = refs[:3], refs[3 : 3 + n_own], refs[3 + n_own : 3 + n_own + n_other]
        flags, out = refs[3 + n_own + n_other :]
        p = jnp.max(flag(flags, "proj", rank)[0:1, :])
        for tile in column_tiles(width):
            grad = total(own, tile)
            if other:
                mine = flag(flags, "proj", rank) == half(flags, rank)
                grad = jnp.where(mine, grad, total(other, tile))
            held = [x[p, :, tile] for x in state]
            out[:, tile] = moment_update(*held, grad)[0].astype(out.dtype)

    return local(
        kernel,
        "chosen_factor",
        [vmem(rank, width)],
        ins=(*state, *own, *other, flags),
        ties=ties,
        after=after,
        passed=passed,
    )


def adam(state, own, other, flags, half, ties=()):
    rank, width = own.shape
    cuts = max(1, width // 1024)
    cut = width // cuts

    def kernel(*refs):
        state, own, other, flags, outs, (fresh, sems) = refs[:3], *refs[3:6], refs[-5:-2], refs[-2:]
        kept = half(flags, rank)
        copies = []
        for k in range(cuts):
            for j in range(k * cut, (k + 1) * cut, 128):
                tile = pl.ds(j, 128)
                grads = f32(own[:, tile]), f32(other[:, tile])
                for p in range(2):
                    grad = jnp.where(kept == p, *grads)
                    values = moment_update(*[x[p, :, tile] for x in state], grad)
                    for i, value in enumerate(values):
                        fresh[i, p, :, tile] = value
            span = pl.ds(k * cut, cut)
            for i, x in enumerate(outs):
                copies.append(
                    pltpu.make_async_copy(fresh.at[i, :, :, span], x.at[:, :, span], sems.at[k, i])
                )
                copies[-1].start()
        for copy in copies:
            copy.wait()

    in_vmem = (*state, own, other, flags, *ties)
    return pl.pallas_call(
        kernel,
        in_specs=[pl.BlockSpec(memory_space=pltpu.VMEM)] * 6
        + [pl.BlockSpec(memory_space=pl.ANY)] * len(ties),
        out_specs=[pl.BlockSpec(memory_space=pltpu.HBM)] * 3,
        out_shape=[pltpu.HBM(x.shape, x.dtype) for x in state],
        scratch_shapes=[
            vmem(3, 2, rank, width, dtype=jnp.float32),
            pltpu.SemaphoreType.DMA((cuts, 3)),
        ],
        compiler_params=pltpu.CompilerParams(vmem_limit_bytes=8 * MIB),
        cost_estimate=pl.CostEstimate(flops=0, bytes_accessed=1024, transcendentals=0),
        name="adam",
    )(*[pltpu.with_memory_space_constraint(x, pltpu.VMEM) for x in in_vmem])


def adam_half(state, grad, flags, half, flip, outs, after):
    rank, width = grad.shape
    cuts = max(1, width // 1024)
    cut = width // cuts

    def kernel(*refs):
        grad, flags, state = refs[0], refs[1], refs[2:5]
        targets, (fresh, sems) = refs[-5:-2], refs[-2:]
        p = jnp.max(half(flags, rank)[0:1, :]) ^ flip
        copies = []
        for k in range(cuts):
            for j in range(k * cut, (k + 1) * cut, 128):
                tile = pl.ds(j, 128)
                values = moment_update(*[x[p, :, tile] for x in state], f32(grad[:, tile]))
                for i, value in enumerate(values):
                    fresh[i, :, tile] = value
            span = pl.ds(k * cut, cut)
            for i, x in enumerate(targets):
                copies.append(
                    pltpu.make_async_copy(fresh.at[i, :, span], x.at[p, :, span], sems.at[k, i])
                )
                copies[-1].start()
        for copy in copies:
            copy.wait()

    in_vmem, in_hbm = (grad, flags, *state), (*after, *outs)
    first = len(in_vmem) + len(after)
    return pl.pallas_call(
        kernel,
        in_specs=[pl.BlockSpec(memory_space=pltpu.VMEM)] * len(in_vmem)
        + [pl.BlockSpec(memory_space=pltpu.HBM)] * len(in_hbm),
        out_specs=[pl.BlockSpec(memory_space=pltpu.HBM)] * 3,
        out_shape=[pltpu.HBM(x.shape, x.dtype) for x in state],
        input_output_aliases={first + i: i for i in range(3)},
        scratch_shapes=[
            vmem(3, rank, width, dtype=jnp.float32),
            pltpu.SemaphoreType.DMA((cuts, 3)),
        ],
        compiler_params=pltpu.CompilerParams(vmem_limit_bytes=8 * MIB),
        cost_estimate=pl.CostEstimate(flops=0, bytes_accessed=1024, transcendentals=0),
        name="adam_half",
    )(
        *[pltpu.with_memory_space_constraint(x, pltpu.VMEM) for x in in_vmem],
        *[pltpu.with_memory_space_constraint(x, pltpu.HBM) for x in in_hbm],
    )


def pick(flags, name, held, ids, rank):
    wanted = flag(flags, name, rank)

    def tile_of(tile):
        found = f32(held[0][:, tile])
        for i in range(1, len(held)):
            found = jnp.where(wanted == ids[i], f32(held[i][:, tile]), found)
        return found

    return tile_of


def block_ids(t_size, many):
    t = lax.axis_index("tensor")
    ids, distance = [t], 1
    while distance < t_size // 2:
        ids = ids + [i ^ distance for i in ids]
        distance *= 2
    return ids[:many]


def offer(held, flags, t_size, ties=()):
    rank, width = held[0].shape

    def kernel(*refs):
        held, flags, out = refs[:-2], refs[-2], refs[-1]
        tile_of = pick(flags, "partners", held, block_ids(t_size, len(held)), rank)
        for tile in column_tiles(width):
            out[:, tile] = tile_of(tile).astype(out.dtype)

    return local(kernel, "offer", [vmem(rank, width)], ins=(*held, flags), ties=ties)


def columns_of_b(held, flags, t_size, ties=()):
    rank, width = held[0].shape

    def kernel(*refs):
        held, flags, cols = refs[:-2], refs[-2], refs[-1]
        ids = block_ids(t_size, len(held) - 1)
        tile_of = pick(flags, "mine", (held[-1], *held[:-1]), (None, *ids), rank)
        for tile in column_tiles(width):
            cols[:, tile] = (adapter_scale * tile_of(tile)).astype(cols.dtype)

    return local(
        kernel, "columns_of_b", [vmem(rank, width)], ins=(*held, flags), ties=ties
    )[0]


def rows_of_a(block):
    rank, height = block.shape

    def kernel(block, left):
        for j in range(0, height, 128):
            tile = pl.ds(j, 128)
            left[tile, :] = block[:, tile].T

    return local(kernel, "rows_of_a", [vmem(height, rank)], ins=(block,))[0]


def refresh(left, cols, flags, weight, state, grad, half):
    height, width = weight.shape
    rank = cols.shape[0]
    block = min(height, 1024)
    steps = height // block
    slots = min(2, steps)
    groups = max(1, width // 1024)
    group = width // groups
    chunks = max(1, width // 1024)
    cut, apart = width // chunks, max(1, (steps - 2) // chunks)
    turns = [min(apart * k, steps - 1) for k in range(chunks)]

    def kernel(*refs):
        left, cols, flags, weight, grad, *state = refs[:8]
        out, targets, (ring, sems, fresh, fresh_sems) = refs[8], refs[9:12], refs[12:]
        step = pl.program_id(0)
        slot = step % slots

        def emit(i, g):
            at, span = pl.ds(pl.multiple_of(i * block, block), block), pl.ds(g * group, group)
            return pltpu.make_async_copy(
                ring.at[i % slots, :, span], out.at[at, span], sems.at[i % slots, g]
            )

        def writes(p, k):
            span = pl.ds(k * cut, cut)
            return [
                pltpu.make_async_copy(fresh.at[i, :, span], x.at[p, :, span], fresh_sems.at[i, k])
                for i, x in enumerate(targets)
            ]

        @pl.when(step >= slots)
        def _():
            for g in range(groups):
                emit(step - slots, g).wait()

        wide = min(width, 256)
        at = pl.ds(pl.multiple_of(step * block, block), block)
        for g in range(groups):
            for k in range(g * group, (g + 1) * group, wide):
                span = pl.ds(k, wide)
                change = jnp.dot(left[at, :], cols[:, span], preferred_element_type=jnp.float32)
                ring[slot, :, span] = (f32(weight[at, span]) + change).astype(ring.dtype)
            emit(step, g).start()

        for chunk, turn in enumerate(turns):

            @pl.when(step == turn)
            def _():
                p = jnp.max(half(flags, rank)[0:1, :])
                for k in range(chunk * cut, (chunk + 1) * cut, 128):
                    tile = pl.ds(k, 128)
                    values = moment_update(*[x[p, :, tile] for x in state], f32(grad[:, tile]))
                    for i, value in enumerate(values):
                        fresh[i, :, tile] = value
                for copy in writes(p, chunk):
                    copy.start()

        @pl.when(step == steps - 1)
        def _():
            p = jnp.max(half(flags, rank)[0:1, :])
            for k in range(chunks):
                for copy in writes(p, k):
                    copy.wait()
            for i in range(steps - slots, steps):
                for g in range(groups):
                    emit(i, g).wait()

    operands = (left, cols, flags, weight, grad, *state)
    outs = [pltpu.HBM((height, width), weight.dtype)] + [pltpu.HBM(x.shape, x.dtype) for x in state]
    result, *fresh = pl.pallas_call(
        kernel,
        grid=(steps,),
        in_specs=[pl.BlockSpec(memory_space=pltpu.VMEM)] * len(operands),
        out_specs=[pl.BlockSpec(memory_space=pltpu.HBM)] * len(outs),
        out_shape=outs,
        scratch_shapes=[
            vmem(slots, block, width),
            pltpu.SemaphoreType.DMA((slots, groups)),
            vmem(3, rank, width, dtype=jnp.float32),
            pltpu.SemaphoreType.DMA((3, chunks)),
        ],
        compiler_params=pltpu.CompilerParams(vmem_limit_bytes=20 * MIB),
        cost_estimate=pl.CostEstimate(flops=0, bytes_accessed=1024, transcendentals=0),
        name="refresh",
    )(*[pltpu.with_memory_space_constraint(x, pltpu.VMEM) for x in operands])
    return result, fresh


def tensor_sum_parts(low, size):
    parts, stride = [low], 1
    while stride < size:
        if len(parts) > 1:
            total = functools.reduce(jnp.add, [f32(x) for x in parts])
            parts = [total.astype(jnp.bfloat16)]
        radix = min(4, size // stride)
        mine = parts[0]
        for hop in range(1, radix):
            pairs = [
                (i, i - i % (stride * radix) + (i + hop * stride) % (stride * radix))
                for i in range(size)
            ]
            parts.append(lax.ppermute(mine, "tensor", pairs))
        stride *= radix
    return parts


def toward(block, distance, t_size, r_size, first):
    pairs = []
    for t in range(t_size):
        root = t * r_size // t_size
        for r in range(r_size):
            same_side = ((r ^ root) & distance) == 0
            same_half = (r ^ root) % 2 == 0
            if (same_side != same_half) == first:
                pairs.append((t * r_size + r, t * r_size + (r ^ distance)))
    return lax.ppermute(block, ("tensor", "replica"), pairs)


def gather_rows(block, t_size, r_size):
    t = lax.axis_index("tensor")
    distance = 1
    while distance < max(1, t_size // r_size):
        other = swap(block, "tensor", t_size, distance)
        block = jnp.where(
            (t & distance) == 0,
            jnp.concatenate([block, other], axis=1),
            jnp.concatenate([other, block], axis=1),
        )
        distance *= 2
    return block


def spread_steps(t_size, r_size):
    distance, steps = t_size // 2, []
    while distance >= max(1, t_size // r_size):
        steps.append(distance)
        distance //= 2
    return steps


def spread_rest(distance, t_size, r_size):
    return functools.reduce(
        lambda a, b: a | b, [d for d in spread_steps(t_size, r_size) if d <= distance]
    )


def spread_send(block, distance, t_size, r_size):
    rest = spread_rest(distance, t_size, r_size)
    pairs = []
    for r in range(r_size):
        root = r * t_size // r_size
        for t in range(t_size):
            if (t ^ root) & rest == 0:
                pairs.append((t * r_size + r, (t ^ distance) * r_size + r))
    return lax.ppermute(block, ("tensor", "replica"), pairs)


def spread_take(came, block, distance, t_size, r_size, ties=()):
    rest = spread_rest(distance, t_size, r_size)

    def kernel(came, block, out):
        t, r = lax.axis_index("tensor"), lax.axis_index("replica")
        takes = ((t ^ (r * t_size // r_size)) & rest) == distance

        @pl.when(takes)
        def _():
            out[...] = came[...]

        @pl.when(jnp.logical_not(takes))
        def _():
            out[...] = block[...]

    return local(kernel, "spread", [vmem(*block.shape)], ins=(came, block), ties=ties)[0]


def own_rows(block, t_size, r_size):
    parts = max(1, r_size // t_size)
    if parts == 1:
        return block
    size = block.shape[1] // parts
    return lax.dynamic_slice_in_dim(block, (lax.axis_index("replica") % parts) * size, size, 1)


def per_device(
    acts,
    cots,
    down_factor,
    up_factor,
    down_first_moment,
    down_second_moment,
    up_first_moment,
    up_second_moment,
    rollout_weight,
    owner,
    projection_index,
):
    t_size, r_size = lax.axis_size("tensor"), lax.axis_size("replica")
    turn = lambda x: jnp.transpose(x, (0, 2, 1))
    down_state = tuple(map(turn, (down_factor, down_first_moment, down_second_moment)))
    up_state = (up_factor, up_first_moment, up_second_moment)
    coefficient = adapter_scale / (acts.shape[1] * r_size)
    down_half = functools.partial(down_parity, t_size=t_size, r_size=r_size)
    up_half = functools.partial(up_parity, t_size=t_size, r_size=r_size)
    exchange = lambda x, distance: swap(x, "replica", r_size, distance)

    low, acts_in, cots_in = low_parts(acts, cots, down_state[0], up_state[0])
    lows = tensor_sum_parts(low, t_size)
    up_send, up_own = gradient_parts(
        lows, cots_in, (), 2, coefficient, up_half,
    )
    up_came = exchange(up_send, 1)
    down_held, up_held, flags = load_state(
        down_state, up_state, projection_index, owner, t_size, r_size, up_send
    )
    down_send, down_own = gradient_parts(lows, acts_in, (flags,), 0, coefficient, down_half)
    up_own, down_send = join((up_own, up_came), passed=(down_send,))
    up_came, distance = exchange(up_own, 2), 4
    down_came = exchange(down_send, 1)
    while distance < r_size:
        (up_own,) = join((up_own, up_came))
        up_came, distance = exchange(up_own, distance), 2 * distance
    down_own, again = join(*[(down_own, down_came)] * 2)
    (up_own,) = join((up_own, up_came), ties=(down_own,))
    up_other = exchange(up_own, 1)
    distance = 2
    while 2 * distance < r_size:
        down_own, again = join(*[(down_own, exchange(down_own, distance))] * 2)
        distance *= 2
    down_first = toward(down_own, distance, t_size, r_size, True)

    (block,) = chosen_factor(down_held, [down_own, down_first], [], flags, down_half)
    block = gather_rows(block, t_size, r_size)
    steps = spread_steps(t_size, r_size)
    rows = spread_send(block, steps[0], t_size, r_size)
    up_mine, again = chosen_factor(
        up_held, [up_own], [up_other], flags, up_half, ties=(block,), passed=(again,)
    )
    down_rest = toward(again, distance, t_size, r_size, False)
    held, shift = [up_mine], 1
    while shift < t_size // 2:
        held = held + [swap(x, "tensor", t_size, shift) for x in held]
        shift *= 2
    rows = spread_take(rows, block, steps[0], t_size, r_size)
    (offered,) = offer(held, flags, t_size, ties=(rows,))
    held = held + [swap(offered, "tensor", t_size, t_size // 2)]
    fresh_up = adam(up_held, up_own, up_other, flags, up_half, ties=(offered,))
    (down_own,) = join((down_own, down_first, down_rest), after=(fresh_up[0],))
    down_other = exchange(down_own, 1)
    cols = columns_of_b(held, flags, t_size, ties=(down_own,))
    for shift in steps[1:]:
        came = spread_send(rows, shift, t_size, r_size)
        rows = spread_take(came, rows, shift, t_size, r_size, ties=(cols,))
    left = rows_of_a(own_rows(rows, t_size, r_size))
    fresh_rollout_weight, fresh_down = refresh(
        left, cols, flags, rollout_weight, down_held, down_own, down_half
    )
    fresh_down = adam_half(
        down_held, down_other, flags, down_half, 1, fresh_down, (fresh_rollout_weight,)
    )
    return (
        turn(fresh_down[0]),
        fresh_up[0],
        turn(fresh_down[1]),
        turn(fresh_down[2]),
        fresh_up[1],
        fresh_up[2],
        fresh_rollout_weight,
    )


def solution(mesh):
    placed = (
        P(None, ("groups", "replica"), "tensor"),
        P(None, ("groups", "replica"), "tensor"),
        P("groups", "tensor", None),
        P("groups", None, "tensor"),
        P("groups", "tensor", None),
        P("groups", "tensor", None),
        P("groups", None, "tensor"),
        P("groups", None, "tensor"),
        P("replica", "tensor"),
        P(),
        P("groups"),
    )
    return jax.shard_map(
        per_device,
        mesh=mesh,
        in_specs=placed,
        out_specs=(
            P("groups", "tensor", None),
            P("groups", None, "tensor"),
            P("groups", "tensor", None),
            P("groups", "tensor", None),
            P("groups", None, "tensor"),
            P("groups", None, "tensor"),
            P(("groups", "replica"), "tensor"),
        ),
        check_vma=False,
    )
```

```python
import functools

import jax
import jax.numpy as jnp
from jax import lax
from jax.experimental import pallas as pl
from jax.experimental.pallas import tpu as pltpu
from jax.sharding import PartitionSpec as P

adapter_scale = 2.0
learn_rate = 0.05
beta_one = 0.9
beta_two = 0.999
adam_eps = 1e-08
fix_one = 1.0 - 0.9**10
fix_two = 1.0 - 0.999**10

MIB = 1024 * 1024
FLAGS = ("proj", "column_proj", "mine", "partners")


def moment_update(param, first, second, grad):
    first_new = beta_one * first + (1.0 - beta_one) * grad
    second_new = beta_two * second + (1.0 - beta_two) * grad * grad
    size = second_new * (1.0 / fix_two)
    param_new = param - (learn_rate / fix_one) * first_new / (size * lax.rsqrt(size) + adam_eps)
    return (param_new, first_new, second_new)


def f32(x):
    return x.astype(jnp.float32)


def swap(x, axis, size, distance):
    return lax.ppermute(x, axis, [(i, i ^ distance) for i in range(size)])


def vmem(*shape, dtype=jnp.bfloat16):
    return pltpu.VMEM(shape, dtype)


def local(kernel, name, outs, ins=(), hbm=(), smem=(), ties=(), after=(), passed=(), scratch=(), work=1024):
    n_ins, n_first = len(ins), len(ins) + len(hbm) + len(smem)
    n_outs = len(outs)

    def body(*refs):
        front = refs[:n_first]
        rest = refs[n_first + len(ties) + len(after) + len(passed) :]
        kernel(*front, *rest[:n_outs], *rest[n_outs + len(passed) :])

    operands = (
        [pltpu.with_memory_space_constraint(x, pltpu.VMEM) for x in ins]
        + [pltpu.with_memory_space_constraint(x, pltpu.HBM) for x in hbm]
        + [pltpu.with_memory_space_constraint(x, pltpu.HBM) for x in smem]
        + [pltpu.with_memory_space_constraint(x, pltpu.VMEM) for x in ties]
        + [pltpu.with_memory_space_constraint(x, pltpu.HBM) for x in after]
        + [pltpu.with_memory_space_constraint(x, pltpu.VMEM) for x in passed]
    )
    specs = (
        [pl.BlockSpec(memory_space=pltpu.VMEM)] * n_ins
        + [pl.BlockSpec(memory_space=pltpu.HBM)] * len(hbm)
        + [pl.BlockSpec(memory_space=pltpu.SMEM)] * len(smem)
        + [pl.BlockSpec(memory_space=pl.ANY)] * (len(ties) + len(after) + len(passed))
    )
    first_passed = n_first + len(ties) + len(after)
    return pl.pallas_call(
        body,
        in_specs=specs,
        out_specs=[pl.BlockSpec(memory_space=pltpu.VMEM)] * n_outs
        + [pl.BlockSpec(memory_space=pl.ANY)] * len(passed),
        out_shape=list(outs) + [pltpu.VMEM(x.shape, x.dtype) for x in passed],
        input_output_aliases={first_passed + i: n_outs + i for i in range(len(passed))},
        scratch_shapes=list(scratch),
        compiler_params=pltpu.CompilerParams(vmem_limit_bytes=8 * MIB),
        cost_estimate=pl.CostEstimate(flops=0, bytes_accessed=work, transcendentals=0),
        name=name,
    )(*operands)


def low_parts(acts, cots, down, up):
    tokens = acts.shape[1]
    rank = down.shape[1]

    def kernel(acts, cots, down, up, low, acts_in, cots_in, down_in, up_in, sems):
        jobs = []
        for spot, (x, x_in, f, f_in) in enumerate(
            ((cots, cots_in, up, up_in), (acts, acts_in, down, down_in))
        ):
            for p in range(2):
                i = 2 * spot + p
                pair = (
                    pltpu.make_async_copy(x.at[p], x_in.at[p], sems.at[2 * i]),
                    pltpu.make_async_copy(f.at[p], f_in.at[p], sems.at[2 * i + 1]),
                )
                for copy in pair:
                    copy.start()
                jobs.append((pair, x_in, f_in, p, i))
        for pair, x_in, f_in, p, i in jobs:
            for copy in pair:
                copy.wait()
            low[pl.ds(i * rank, rank), :] = lax.dot_general(
                f_in[p].astype(jnp.bfloat16),
                x_in[p],
                (((1,), (1,)), ((), ())),
                preferred_element_type=jnp.float32,
            ).astype(low.dtype)

    return local(
        kernel,
        "low_parts",
        [vmem(4 * rank, tokens), vmem(*acts.shape), vmem(*cots.shape)],
        hbm=(acts, cots, down, up),
        scratch=[
            vmem(*down.shape, dtype=jnp.float32),
            vmem(*up.shape, dtype=jnp.float32),
            pltpu.SemaphoreType.DMA((8,)),
        ],
    )


def load_state(down_state, up_state, projection_index, owner, t_size, r_size, tie):
    rank = down_state[0].shape[1]

    def kernel(*refs):
        sources, (index, owner), targets, (flags, sems) = refs[:6], refs[6:8], refs[8:14], refs[14:]
        copies = [
            pltpu.make_async_copy(x, y, sems.at[i]) for i, (x, y) in enumerate(zip(sources, targets))
        ]
        for copy in copies:
            copy.start()
        t, r = lax.axis_index("tensor"), lax.axis_index("replica")
        values = (index[r], index[t * r_size // t_size], owner[t], owner[t ^ (t_size // 2)])
        for i, value in enumerate(values):
            flags[pl.ds(i * rank, rank), :] = jnp.full((rank, 128), value, jnp.int32)
        for copy in copies:
            copy.wait()

    *state, flags = local(
        kernel,
        "load_state",
        [vmem(*x.shape, dtype=jnp.float32) for x in (*down_state, *up_state)]
        + [vmem(len(FLAGS) * rank, 128, dtype=jnp.int32)],
        hbm=(*down_state, *up_state),
        smem=(projection_index, owner),
        ties=(tie,),
        scratch=[pltpu.SemaphoreType.DMA((6,))],
    )
    return state[:3], state[3:], flags


def flag(flags, name, rank):
    return flags[pl.ds(FLAGS.index(name) * rank, rank), :]


def column_tiles(width):
    return [pl.ds(k, 128) for k in range(0, width, 128)]


def down_parity(flags, rank, t_size, r_size):
    t, r = lax.axis_index("tensor"), lax.axis_index("replica")
    return flag(flags, "column_proj", rank) ^ ((r + t * r_size // t_size) % 2)


def up_parity(flags, rank, t_size, r_size):
    r = lax.axis_index("replica")
    return jnp.full((rank, 128), r % 2, jnp.int32)


def gradient_parts(lows, tokens, flags, base, coefficient, half, ties=()):
    rank = lows[0].shape[0] // 4
    width = tokens.shape[2]
    parts = len(lows)

    def kernel(*refs):
        lows, tokens, flags, (send, keep) = refs[:parts], refs[parts], refs[parts + 1 : -2], refs[-2:]
        rows = pl.ds(base * rank, 2 * rank)
        total = functools.reduce(jnp.add, [f32(x[rows, :]) for x in lows]).astype(jnp.bfloat16)
        kept = half(flags[0] if flags else None, rank) == 0
        cut = min(width, 512)
        for k in range(0, width, cut):
            grads = [
                coefficient
                * jnp.dot(
                    total[p * rank : (p + 1) * rank],
                    tokens[p, :, pl.ds(k, cut)],
                    preferred_element_type=jnp.float32,
                )
                for p in range(2)
            ]
            for j in range(0, cut, 128):
                first, second = [g[:, j : j + 128] for g in grads]
                tile = pl.ds(k + j, 128)
                keep[:, tile] = jnp.where(kept, first, second).astype(keep.dtype)
                send[:, tile] = jnp.where(kept, second, first).astype(send.dtype)

    return local(
        kernel,
        "gradient_parts",
        [vmem(rank, width), vmem(rank, width)],
        ins=(*lows, tokens, *flags),
        ties=ties,
    )


def join(*sums, ties=(), after=(), passed=()):
    terms = [x for group in sums for x in group]

    def kernel(*refs):
        refs, outs = list(refs[: len(terms)]), refs[len(terms) :]
        for group, out in zip(sums, outs):
            total = functools.reduce(jnp.add, [f32(refs.pop(0)[...]) for _ in group])
            out[...] = total.astype(out.dtype)

    return local(
        kernel,
        "join",
        [vmem(*group[0].shape) for group in sums],
        ins=terms,
        ties=ties,
        after=after,
        passed=passed,
    )


def chosen_factor(state, own, other, flags, half, ties=(), after=(), passed=()):
    rank, width = own[0].shape
    n_own, n_other = len(own), len(other)

    def total(refs, tile):
        return f32(functools.reduce(jnp.add, [f32(x[:, tile]) for x in refs]).astype(jnp.bfloat16))

    def kernel(*refs):
        state, own, other = refs[:3], refs[3 : 3 + n_own], refs[3 + n_own : 3 + n_own + n_other]
        flags, out = refs[3 + n_own + n_other :]
        p = jnp.max(flag(flags, "proj", rank)[0:1, :])
        for tile in column_tiles(width):
            grad = total(own, tile)
            if other:
                mine = flag(flags, "proj", rank) == half(flags, rank)
                grad = jnp.where(mine, grad, total(other, tile))
            held = [x[p, :, tile] for x in state]
            out[:, tile] = moment_update(*held, grad)[0].astype(out.dtype)

    return local(
        kernel,
        "chosen_factor",
        [vmem(rank, width)],
        ins=(*state, *own, *other, flags),
        ties=ties,
        after=after,
        passed=passed,
    )


def adam(state, own, other, flags, half, ties=()):
    rank, width = own.shape
    cuts = max(1, width // 1024)
    cut = width // cuts

    def kernel(*refs):
        state, own, other, flags, outs, (fresh, sems) = refs[:3], *refs[3:6], refs[-5:-2], refs[-2:]
        kept = half(flags, rank)
        copies = []
        for k in range(cuts):
            for j in range(k * cut, (k + 1) * cut, 128):
                tile = pl.ds(j, 128)
                grads = f32(own[:, tile]), f32(other[:, tile])
                for p in range(2):
                    grad = jnp.where(kept == p, *grads)
                    values = moment_update(*[x[p, :, tile] for x in state], grad)
                    for i, value in enumerate(values):
                        fresh[i, p, :, tile] = value
            span = pl.ds(k * cut, cut)
            for i, x in enumerate(outs):
                copies.append(
                    pltpu.make_async_copy(fresh.at[i, :, :, span], x.at[:, :, span], sems.at[k, i])
                )
                copies[-1].start()
        for copy in copies:
            copy.wait()

    in_vmem = (*state, own, other, flags, *ties)
    return pl.pallas_call(
        kernel,
        in_specs=[pl.BlockSpec(memory_space=pltpu.VMEM)] * 6
        + [pl.BlockSpec(memory_space=pl.ANY)] * len(ties),
        out_specs=[pl.BlockSpec(memory_space=pltpu.HBM)] * 3,
        out_shape=[pltpu.HBM(x.shape, x.dtype) for x in state],
        scratch_shapes=[
            vmem(3, 2, rank, width, dtype=jnp.float32),
            pltpu.SemaphoreType.DMA((cuts, 3)),
        ],
        compiler_params=pltpu.CompilerParams(vmem_limit_bytes=8 * MIB),
        cost_estimate=pl.CostEstimate(flops=0, bytes_accessed=1024, transcendentals=0),
        name="adam",
    )(*[pltpu.with_memory_space_constraint(x, pltpu.VMEM) for x in in_vmem])


def adam_half(state, grad, flags, half, flip, outs, after):
    rank, width = grad.shape
    cuts = max(1, width // 1024)
    cut = width // cuts

    def kernel(*refs):
        grad, flags, state = refs[0], refs[1], refs[2:5]
        targets, (fresh, sems) = refs[-5:-2], refs[-2:]
        p = jnp.max(half(flags, rank)[0:1, :]) ^ flip
        copies = []
        for k in range(cuts):
            for j in range(k * cut, (k + 1) * cut, 128):
                tile = pl.ds(j, 128)
                values = moment_update(*[x[p, :, tile] for x in state], f32(grad[:, tile]))
                for i, value in enumerate(values):
                    fresh[i, :, tile] = value
            span = pl.ds(k * cut, cut)
            for i, x in enumerate(targets):
                copies.append(
                    pltpu.make_async_copy(fresh.at[i, :, span], x.at[p, :, span], sems.at[k, i])
                )
                copies[-1].start()
        for copy in copies:
            copy.wait()

    in_vmem, in_hbm = (grad, flags, *state), (*after, *outs)
    first = len(in_vmem) + len(after)
    return pl.pallas_call(
        kernel,
        in_specs=[pl.BlockSpec(memory_space=pltpu.VMEM)] * len(in_vmem)
        + [pl.BlockSpec(memory_space=pltpu.HBM)] * len(in_hbm),
        out_specs=[pl.BlockSpec(memory_space=pltpu.HBM)] * 3,
        out_shape=[pltpu.HBM(x.shape, x.dtype) for x in state],
        input_output_aliases={first + i: i for i in range(3)},
        scratch_shapes=[
            vmem(3, rank, width, dtype=jnp.float32),
            pltpu.SemaphoreType.DMA((cuts, 3)),
        ],
        compiler_params=pltpu.CompilerParams(vmem_limit_bytes=8 * MIB),
        cost_estimate=pl.CostEstimate(flops=0, bytes_accessed=1024, transcendentals=0),
        name="adam_half",
    )(
        *[pltpu.with_memory_space_constraint(x, pltpu.VMEM) for x in in_vmem],
        *[pltpu.with_memory_space_constraint(x, pltpu.HBM) for x in in_hbm],
    )


def pick(flags, name, held, ids, rank):
    wanted = flag(flags, name, rank)

    def tile_of(tile):
        found = f32(held[0][:, tile])
        for i in range(1, len(held)):
            found = jnp.where(wanted == ids[i], f32(held[i][:, tile]), found)
        return found

    return tile_of


def block_ids(t_size, many):
    t = lax.axis_index("tensor")
    ids, distance = [t], 1
    while distance < t_size // 2:
        ids = ids + [i ^ distance for i in ids]
        distance *= 2
    return ids[:many]


def offer(held, flags, t_size, ties=()):
    rank, width = held[0].shape

    def kernel(*refs):
        held, flags, out = refs[:-2], refs[-2], refs[-1]
        tile_of = pick(flags, "partners", held, block_ids(t_size, len(held)), rank)
        for tile in column_tiles(width):
            out[:, tile] = tile_of(tile).astype(out.dtype)

    return local(kernel, "offer", [vmem(rank, width)], ins=(*held, flags), ties=ties)


def columns_of_b(held, flags, t_size, ties=()):
    rank, width = held[0].shape

    def kernel(*refs):
        held, flags, cols = refs[:-2], refs[-2], refs[-1]
        ids = block_ids(t_size, len(held) - 1)
        tile_of = pick(flags, "mine", (held[-1], *held[:-1]), (None, *ids), rank)
        for tile in column_tiles(width):
            cols[:, tile] = (adapter_scale * tile_of(tile)).astype(cols.dtype)

    return local(
        kernel, "columns_of_b", [vmem(rank, width)], ins=(*held, flags), ties=ties
    )[0]


def rows_of_a(block):
    rank, height = block.shape

    def kernel(block, left):
        for j in range(0, height, 128):
            tile = pl.ds(j, 128)
            left[tile, :] = block[:, tile].T

    return local(kernel, "rows_of_a", [vmem(height, rank)], ins=(block,))[0]


def refresh(left, cols, flags, weight, state, grad, half):
    height, width = weight.shape
    rank = cols.shape[0]
    block = min(height, 1024)
    steps = height // block
    slots = min(2, steps)
    groups = max(1, width // 1024)
    group = width // groups
    chunks = max(1, width // 1024)
    cut, apart = width // chunks, max(1, (steps - 2) // chunks)
    turns = [min(apart * k, steps - 1) for k in range(chunks)]

    def kernel(*refs):
        left, cols, flags, weight, grad, *state = refs[:8]
        out, targets, (ring, sems, fresh, fresh_sems) = refs[8], refs[9:12], refs[12:]
        step = pl.program_id(0)
        slot = step % slots

        def emit(i, g):
            at, span = pl.ds(pl.multiple_of(i * block, block), block), pl.ds(g * group, group)
            return pltpu.make_async_copy(
                ring.at[i % slots, :, span], out.at[at, span], sems.at[i % slots, g]
            )

        def writes(p, k):
            span = pl.ds(k * cut, cut)
            return [
                pltpu.make_async_copy(fresh.at[i, :, span], x.at[p, :, span], fresh_sems.at[i, k])
                for i, x in enumerate(targets)
            ]

        @pl.when(step >= slots)
        def _():
            for g in range(groups):
                emit(step - slots, g).wait()

        wide = min(width, 256)
        at = pl.ds(pl.multiple_of(step * block, block), block)
        for g in range(groups):
            for k in range(g * group, (g + 1) * group, wide):
                span = pl.ds(k, wide)
                change = jnp.dot(left[at, :], cols[:, span], preferred_element_type=jnp.float32)
                ring[slot, :, span] = (f32(weight[at, span]) + change).astype(ring.dtype)
            emit(step, g).start()

        for chunk, turn in enumerate(turns):

            @pl.when(step == turn)
            def _():
                p = jnp.max(half(flags, rank)[0:1, :])
                for k in range(chunk * cut, (chunk + 1) * cut, 128):
                    tile = pl.ds(k, 128)
                    values = moment_update(*[x[p, :, tile] for x in state], f32(grad[:, tile]))
                    for i, value in enumerate(values):
                        fresh[i, :, tile] = value
                for copy in writes(p, chunk):
                    copy.start()

        @pl.when(step == steps - 1)
        def _():
            p = jnp.max(half(flags, rank)[0:1, :])
            for k in range(chunks):
                for copy in writes(p, k):
                    copy.wait()
            for i in range(steps - slots, steps):
                for g in range(groups):
                    emit(i, g).wait()

    operands = (left, cols, flags, weight, grad, *state)
    outs = [pltpu.HBM((height, width), weight.dtype)] + [pltpu.HBM(x.shape, x.dtype) for x in state]
    result, *fresh = pl.pallas_call(
        kernel,
        grid=(steps,),
        in_specs=[pl.BlockSpec(memory_space=pltpu.VMEM)] * len(operands),
        out_specs=[pl.BlockSpec(memory_space=pltpu.HBM)] * len(outs),
        out_shape=outs,
        scratch_shapes=[
            vmem(slots, block, width),
            pltpu.SemaphoreType.DMA((slots, groups)),
            vmem(3, rank, width, dtype=jnp.float32),
            pltpu.SemaphoreType.DMA((3, chunks)),
        ],
        compiler_params=pltpu.CompilerParams(vmem_limit_bytes=20 * MIB),
        cost_estimate=pl.CostEstimate(flops=0, bytes_accessed=1024, transcendentals=0),
        name="refresh",
    )(*[pltpu.with_memory_space_constraint(x, pltpu.VMEM) for x in operands])
    return result, fresh


def tensor_sum_parts(low, size):
    parts, stride = [low], 1
    while stride < size:
        if len(parts) > 1:
            total = functools.reduce(jnp.add, [f32(x) for x in parts])
            parts = [total.astype(jnp.bfloat16)]
        radix = min(4, size // stride)
        mine = parts[0]
        for hop in range(1, radix):
            pairs = [
                (i, i - i % (stride * radix) + (i + hop * stride) % (stride * radix))
                for i in range(size)
            ]
            parts.append(lax.ppermute(mine, "tensor", pairs))
        stride *= radix
    return parts


def toward(block, distance, t_size, r_size, first):
    pairs = []
    for t in range(t_size):
        root = t * r_size // t_size
        for r in range(r_size):
            same_side = ((r ^ root) & distance) == 0
            same_half = (r ^ root) % 2 == 0
            if (same_side != same_half) == first:
                pairs.append((t * r_size + r, t * r_size + (r ^ distance)))
    return lax.ppermute(block, ("tensor", "replica"), pairs)


def gather_rows(block, t_size, r_size):
    t = lax.axis_index("tensor")
    distance = 1
    while distance < max(1, t_size // r_size):
        other = swap(block, "tensor", t_size, distance)
        block = jnp.where(
            (t & distance) == 0,
            jnp.concatenate([block, other], axis=1),
            jnp.concatenate([other, block], axis=1),
        )
        distance *= 2
    return block


def spread_steps(t_size, r_size):
    distance, steps = t_size // 2, []
    while distance >= max(1, t_size // r_size):
        steps.append(distance)
        distance //= 2
    return steps


def spread_rest(distance, t_size, r_size):
    return functools.reduce(
        lambda a, b: a | b, [d for d in spread_steps(t_size, r_size) if d <= distance]
    )


def spread_send(block, distance, t_size, r_size):
    rest = spread_rest(distance, t_size, r_size)
    pairs = []
    for r in range(r_size):
        root = r * t_size // r_size
        for t in range(t_size):
            if (t ^ root) & rest == 0:
                pairs.append((t * r_size + r, (t ^ distance) * r_size + r))
    return lax.ppermute(block, ("tensor", "replica"), pairs)


def spread_take(came, block, distance, t_size, r_size, ties=()):
    rest = spread_rest(distance, t_size, r_size)

    def kernel(came, block, out):
        t, r = lax.axis_index("tensor"), lax.axis_index("replica")
        takes = ((t ^ (r * t_size // r_size)) & rest) == distance

        @pl.when(takes)
        def _():
            out[...] = came[...]

        @pl.when(jnp.logical_not(takes))
        def _():
            out[...] = block[...]

    return local(kernel, "spread", [vmem(*block.shape)], ins=(came, block), ties=ties)[0]


def own_rows(block, t_size, r_size):
    parts = max(1, r_size // t_size)
    if parts == 1:
        return block
    size = block.shape[1] // parts
    return lax.dynamic_slice_in_dim(block, (lax.axis_index("replica") % parts) * size, size, 1)


def per_device(
    acts,
    cots,
    down_factor,
    up_factor,
    down_first_moment,
    down_second_moment,
    up_first_moment,
    up_second_moment,
    rollout_weight,
    owner,
    projection_index,
):
    t_size, r_size = lax.axis_size("tensor"), lax.axis_size("replica")
    turn = lambda x: jnp.transpose(x, (0, 2, 1))
    down_state = tuple(map(turn, (down_factor, down_first_moment, down_second_moment)))
    up_state = (up_factor, up_first_moment, up_second_moment)
    coefficient = adapter_scale / (acts.shape[1] * r_size)
    down_half = functools.partial(down_parity, t_size=t_size, r_size=r_size)
    up_half = functools.partial(up_parity, t_size=t_size, r_size=r_size)
    exchange = lambda x, distance: swap(x, "replica", r_size, distance)

    low, acts_in, cots_in = low_parts(acts, cots, down_state[0], up_state[0])
    lows = tensor_sum_parts(low, t_size)
    up_send, up_own = gradient_parts(
        lows, cots_in, (), 2, coefficient, up_half,
    )
    up_came = exchange(up_send, 1)
    down_held, up_held, flags = load_state(
        down_state, up_state, projection_index, owner, t_size, r_size, up_send
    )
    down_send, down_own = gradient_parts(lows, acts_in, (flags,), 0, coefficient, down_half)
    up_own, down_send = join((up_own, up_came), passed=(down_send,))
    up_came, distance = exchange(up_own, 2), 4
    down_came = exchange(down_send, 1)
    while distance < r_size:
        (up_own,) = join((up_own, up_came))
        up_came, distance = exchange(up_own, distance), 2 * distance
    (up_own,) = join((up_own, up_came))
    down_own, again = join(*[(down_own, down_came)] * 2, ties=(up_own,))
    up_other = exchange(up_own, 1)
    distance = 2
    while 2 * distance < r_size:
        down_own, again = join(*[(down_own, exchange(down_own, distance))] * 2)
        distance *= 2
    down_first = toward(down_own, distance, t_size, r_size, True)

    (up_mine,) = chosen_factor(up_held, [up_own], [up_other], flags, up_half)
    held, shift = [up_mine], 1
    while shift < t_size // 2:
        held = held + [swap(x, "tensor", t_size, shift) for x in held]
        shift *= 2
    block, again = chosen_factor(
        down_held, [down_own, down_first], [], flags, down_half, ties=(up_mine,), passed=(again,)
    )
    block = gather_rows(block, t_size, r_size)
    steps = spread_steps(t_size, r_size)
    came = spread_send(block, steps[0], t_size, r_size)
    down_rest = toward(again, distance, t_size, r_size, False)
    (offered,) = offer(held, flags, t_size, ties=(block,))
    held = held + [swap(offered, "tensor", t_size, t_size // 2)]
    rows = spread_take(came, block, steps[0], t_size, r_size, ties=(offered,))
    fresh_up = adam(up_held, up_own, up_other, flags, up_half, ties=(offered,))
    (down_own,) = join((down_own, down_first, down_rest), after=(fresh_up[0],))
    down_other = exchange(down_own, 1)
    cols = columns_of_b(held, flags, t_size, ties=(down_own,))
    for shift in steps[1:]:
        came = spread_send(rows, shift, t_size, r_size)
        rows = spread_take(came, rows, shift, t_size, r_size, ties=(cols,))
    left = rows_of_a(own_rows(rows, t_size, r_size))
    fresh_rollout_weight, fresh_down = refresh(
        left, cols, flags, rollout_weight, down_held, down_own, down_half
    )
    fresh_down = adam_half(
        down_held, down_other, flags, down_half, 1, fresh_down, (fresh_rollout_weight,)
    )
    return (
        turn(fresh_down[0]),
        fresh_up[0],
        turn(fresh_down[1]),
        turn(fresh_down[2]),
        fresh_up[1],
        fresh_up[2],
        fresh_rollout_weight,
    )


def solution(mesh):
    placed = (
        P(None, ("groups", "replica"), "tensor"),
        P(None, ("groups", "replica"), "tensor"),
        P("groups", "tensor", None),
        P("groups", None, "tensor"),
        P("groups", "tensor", None),
        P("groups", "tensor", None),
        P("groups", None, "tensor"),
        P("groups", None, "tensor"),
        P("replica", "tensor"),
        P(),
        P("groups"),
    )
    return jax.shard_map(
        per_device,
        mesh=mesh,
        in_specs=placed,
        out_specs=(
            P("groups", "tensor", None),
            P("groups", None, "tensor"),
            P("groups", "tensor", None),
            P("groups", "tensor", None),
            P("groups", None, "tensor"),
            P("groups", None, "tensor"),
            P(("groups", "replica"), "tensor"),
        ),
        check_vma=False,
    )
```

```python
import functools

import jax
import jax.numpy as jnp
from jax import lax
from jax.experimental import pallas as pl
from jax.experimental.pallas import tpu as pltpu
from jax.sharding import PartitionSpec as P

adapter_scale = 2.0
learn_rate = 0.05
beta_one = 0.9
beta_two = 0.999
adam_eps = 1e-08
fix_one = 1.0 - 0.9**10
fix_two = 1.0 - 0.999**10

MIB = 1024 * 1024
FLAGS = ("proj", "column_proj", "mine", "partners")


def moment_update(param, first, second, grad):
    first_new = beta_one * first + (1.0 - beta_one) * grad
    second_new = beta_two * second + (1.0 - beta_two) * grad * grad
    size = second_new * (1.0 / fix_two)
    param_new = param - (learn_rate / fix_one) * first_new / (size * lax.rsqrt(size) + adam_eps)
    return (param_new, first_new, second_new)


def f32(x):
    return x.astype(jnp.float32)


def swap(x, axis, size, distance):
    return lax.ppermute(x, axis, [(i, i ^ distance) for i in range(size)])


def vmem(*shape, dtype=jnp.bfloat16):
    return pltpu.VMEM(shape, dtype)


def local(kernel, name, outs, ins=(), hbm=(), smem=(), ties=(), after=(), passed=(), scratch=(), work=1024):
    n_ins, n_first = len(ins), len(ins) + len(hbm) + len(smem)
    n_outs = len(outs)

    def body(*refs):
        front = refs[:n_first]
        rest = refs[n_first + len(ties) + len(after) + len(passed) :]
        kernel(*front, *rest[:n_outs], *rest[n_outs + len(passed) :])

    operands = (
        [pltpu.with_memory_space_constraint(x, pltpu.VMEM) for x in ins]
        + [pltpu.with_memory_space_constraint(x, pltpu.HBM) for x in hbm]
        + [pltpu.with_memory_space_constraint(x, pltpu.HBM) for x in smem]
        + [pltpu.with_memory_space_constraint(x, pltpu.VMEM) for x in ties]
        + [pltpu.with_memory_space_constraint(x, pltpu.HBM) for x in after]
        + [pltpu.with_memory_space_constraint(x, pltpu.VMEM) for x in passed]
    )
    specs = (
        [pl.BlockSpec(memory_space=pltpu.VMEM)] * n_ins
        + [pl.BlockSpec(memory_space=pltpu.HBM)] * len(hbm)
        + [pl.BlockSpec(memory_space=pltpu.SMEM)] * len(smem)
        + [pl.BlockSpec(memory_space=pl.ANY)] * (len(ties) + len(after) + len(passed))
    )
    first_passed = n_first + len(ties) + len(after)
    return pl.pallas_call(
        body,
        in_specs=specs,
        out_specs=[pl.BlockSpec(memory_space=pltpu.VMEM)] * n_outs
        + [pl.BlockSpec(memory_space=pl.ANY)] * len(passed),
        out_shape=list(outs) + [pltpu.VMEM(x.shape, x.dtype) for x in passed],
        input_output_aliases={first_passed + i: n_outs + i for i in range(len(passed))},
        scratch_shapes=list(scratch),
        compiler_params=pltpu.CompilerParams(vmem_limit_bytes=8 * MIB),
        cost_estimate=pl.CostEstimate(flops=0, bytes_accessed=work, transcendentals=0),
        name=name,
    )(*operands)


def low_parts(acts, cots, down, up):
    tokens = acts.shape[1]
    rank = down.shape[1]

    def kernel(acts, cots, down, up, low, acts_in, cots_in, down_in, up_in, sems):
        jobs = []
        for spot, (x, x_in, f, f_in) in enumerate(
            ((cots, cots_in, up, up_in), (acts, acts_in, down, down_in))
        ):
            for p in range(2):
                i = 2 * spot + p
                pair = (
                    pltpu.make_async_copy(x.at[p], x_in.at[p], sems.at[2 * i]),
                    pltpu.make_async_copy(f.at[p], f_in.at[p], sems.at[2 * i + 1]),
                )
                for copy in pair:
                    copy.start()
                jobs.append((pair, x_in, f_in, p, i))
        for pair, x_in, f_in, p, i in jobs:
            for copy in pair:
                copy.wait()
            low[pl.ds(i * rank, rank), :] = lax.dot_general(
                f_in[p].astype(jnp.bfloat16),
                x_in[p],
                (((1,), (1,)), ((), ())),
                preferred_element_type=jnp.float32,
            ).astype(low.dtype)

    return local(
        kernel,
        "low_parts",
        [vmem(4 * rank, tokens), vmem(*acts.shape), vmem(*cots.shape)],
        hbm=(acts, cots, down, up),
        scratch=[
            vmem(*down.shape, dtype=jnp.float32),
            vmem(*up.shape, dtype=jnp.float32),
            pltpu.SemaphoreType.DMA((8,)),
        ],
    )


def load_state(down_state, up_state, projection_index, owner, t_size, r_size, tie):
    rank = down_state[0].shape[1]

    def kernel(*refs):
        sources, (index, owner), targets, (flags, sems) = refs[:6], refs[6:8], refs[8:14], refs[14:]
        copies = [
            pltpu.make_async_copy(x, y, sems.at[i]) for i, (x, y) in enumerate(zip(sources, targets))
        ]
        for copy in copies:
            copy.start()
        t, r = lax.axis_index("tensor"), lax.axis_index("replica")
        values = (index[r], index[t * r_size // t_size], owner[t], owner[t ^ (t_size // 2)])
        for i, value in enumerate(values):
            flags[pl.ds(i * rank, rank), :] = jnp.full((rank, 128), value, jnp.int32)
        for copy in copies:
            copy.wait()

    *state, flags = local(
        kernel,
        "load_state",
        [vmem(*x.shape, dtype=jnp.float32) for x in (*down_state, *up_state)]
        + [vmem(len(FLAGS) * rank, 128, dtype=jnp.int32)],
        hbm=(*down_state, *up_state),
        smem=(projection_index, owner),
        ties=(tie,),
        scratch=[pltpu.SemaphoreType.DMA((6,))],
    )
    return state[:3], state[3:], flags


def flag(flags, name, rank):
    return flags[pl.ds(FLAGS.index(name) * rank, rank), :]


def column_tiles(width):
    return [pl.ds(k, 128) for k in range(0, width, 128)]


def down_parity(flags, rank, t_size, r_size):
    t, r = lax.axis_index("tensor"), lax.axis_index("replica")
    return flag(flags, "column_proj", rank) ^ ((r + t * r_size // t_size) % 2)


def up_parity(flags, rank, t_size, r_size):
    r = lax.axis_index("replica")
    return jnp.full((rank, 128), r % 2, jnp.int32)


def gradient_parts(lows, tokens, flags, base, coefficient, half, ties=()):
    rank = lows[0].shape[0] // 4
    width = tokens.shape[2]
    parts = len(lows)

    def kernel(*refs):
        lows, tokens, flags, (send, keep) = refs[:parts], refs[parts], refs[parts + 1 : -2], refs[-2:]
        rows = pl.ds(base * rank, 2 * rank)
        total = functools.reduce(jnp.add, [f32(x[rows, :]) for x in lows]).astype(jnp.bfloat16)
        kept = half(flags[0] if flags else None, rank) == 0
        cut = min(width, 512)
        for k in range(0, width, cut):
            grads = [
                coefficient
                * jnp.dot(
                    total[p * rank : (p + 1) * rank],
                    tokens[p, :, pl.ds(k, cut)],
                    preferred_element_type=jnp.float32,
                )
                for p in range(2)
            ]
            for j in range(0, cut, 128):
                first, second = [g[:, j : j + 128] for g in grads]
                tile = pl.ds(k + j, 128)
                keep[:, tile] = jnp.where(kept, first, second).astype(keep.dtype)
                send[:, tile] = jnp.where(kept, second, first).astype(send.dtype)

    return local(
        kernel,
        "gradient_parts",
        [vmem(rank, width), vmem(rank, width)],
        ins=(*lows, tokens, *flags),
        ties=ties,
    )


def join(*sums, ties=(), after=(), passed=()):
    terms = [x for group in sums for x in group]

    def kernel(*refs):
        refs, outs = list(refs[: len(terms)]), refs[len(terms) :]
        for group, out in zip(sums, outs):
            total = functools.reduce(jnp.add, [f32(refs.pop(0)[...]) for _ in group])
            out[...] = total.astype(out.dtype)

    return local(
        kernel,
        "join",
        [vmem(*group[0].shape) for group in sums],
        ins=terms,
        ties=ties,
        after=after,
        passed=passed,
    )


def chosen_factor(state, own, other, flags, half, ties=(), after=(), passed=()):
    rank, width = own[0].shape
    n_own, n_other = len(own), len(other)

    def total(refs, tile):
        return f32(functools.reduce(jnp.add, [f32(x[:, tile]) for x in refs]).astype(jnp.bfloat16))

    def kernel(*refs):
        state, own, other = refs[:3], refs[3 : 3 + n_own], refs[3 + n_own : 3 + n_own + n_other]
        flags, out = refs[3 + n_own + n_other :]
        p = jnp.max(flag(flags, "proj", rank)[0:1, :])
        for tile in column_tiles(width):
            grad = total(own, tile)
            if other:
                mine = flag(flags, "proj", rank) == half(flags, rank)
                grad = jnp.where(mine, grad, total(other, tile))
            held = [x[p, :, tile] for x in state]
            out[:, tile] = moment_update(*held, grad)[0].astype(out.dtype)

    return local(
        kernel,
        "chosen_factor",
        [vmem(rank, width)],
        ins=(*state, *own, *other, flags),
        ties=ties,
        after=after,
        passed=passed,
    )


def adam(state, own, other, flags, half, ties=()):
    rank, width = own.shape
    cuts = max(1, width // 1024)
    cut = width // cuts

    def kernel(*refs):
        state, own, other, flags, outs, (fresh, sems) = refs[:3], *refs[3:6], refs[-5:-2], refs[-2:]
        kept = half(flags, rank)
        copies = []
        for k in range(cuts):
            for j in range(k * cut, (k + 1) * cut, 128):
                tile = pl.ds(j, 128)
                grads = f32(own[:, tile]), f32(other[:, tile])
                for p in range(2):
                    grad = jnp.where(kept == p, *grads)
                    values = moment_update(*[x[p, :, tile] for x in state], grad)
                    for i, value in enumerate(values):
                        fresh[i, p, :, tile] = value
            span = pl.ds(k * cut, cut)
            for i, x in enumerate(outs):
                copies.append(
                    pltpu.make_async_copy(fresh.at[i, :, :, span], x.at[:, :, span], sems.at[k, i])
                )
                copies[-1].start()
        for copy in copies:
            copy.wait()

    in_vmem = (*state, own, other, flags, *ties)
    return pl.pallas_call(
        kernel,
        in_specs=[pl.BlockSpec(memory_space=pltpu.VMEM)] * 6
        + [pl.BlockSpec(memory_space=pl.ANY)] * len(ties),
        out_specs=[pl.BlockSpec(memory_space=pltpu.HBM)] * 3,
        out_shape=[pltpu.HBM(x.shape, x.dtype) for x in state],
        scratch_shapes=[
            vmem(3, 2, rank, width, dtype=jnp.float32),
            pltpu.SemaphoreType.DMA((cuts, 3)),
        ],
        compiler_params=pltpu.CompilerParams(vmem_limit_bytes=8 * MIB),
        cost_estimate=pl.CostEstimate(flops=0, bytes_accessed=1024, transcendentals=0),
        name="adam",
    )(*[pltpu.with_memory_space_constraint(x, pltpu.VMEM) for x in in_vmem])


def pick(flags, name, held, ids, rank):
    wanted = flag(flags, name, rank)

    def tile_of(tile):
        found = f32(held[0][:, tile])
        for i in range(1, len(held)):
            found = jnp.where(wanted == ids[i], f32(held[i][:, tile]), found)
        return found

    return tile_of


def block_ids(t_size, many):
    t = lax.axis_index("tensor")
    ids, distance = [t], 1
    while distance < t_size // 2:
        ids = ids + [i ^ distance for i in ids]
        distance *= 2
    return ids[:many]


def offer(held, flags, t_size, ties=()):
    rank, width = held[0].shape

    def kernel(*refs):
        held, flags, out = refs[:-2], refs[-2], refs[-1]
        tile_of = pick(flags, "partners", held, block_ids(t_size, len(held)), rank)
        for tile in column_tiles(width):
            out[:, tile] = tile_of(tile).astype(out.dtype)

    return local(kernel, "offer", [vmem(rank, width)], ins=(*held, flags), ties=ties)


def columns_of_b(held, flags, t_size, after=()):
    rank, width = held[0].shape

    def kernel(*refs):
        held, flags, cols = refs[:-2], refs[-2], refs[-1]
        ids = block_ids(t_size, len(held) - 1)
        tile_of = pick(flags, "mine", (held[-1], *held[:-1]), (None, *ids), rank)
        for tile in column_tiles(width):
            cols[:, tile] = (adapter_scale * tile_of(tile)).astype(cols.dtype)

    return local(
        kernel, "columns_of_b", [vmem(rank, width)], ins=(*held, flags), after=after
    )[0]


def rows_of_a(block):
    rank, height = block.shape

    def kernel(block, left):
        for j in range(0, height, 128):
            tile = pl.ds(j, 128)
            left[tile, :] = block[:, tile].T

    return local(kernel, "rows_of_a", [vmem(height, rank)], ins=(block,))[0]


def refresh(left, cols, flags, weight, state, own, other, half):
    height, width = weight.shape
    rank = cols.shape[0]
    block = min(height, 1024)
    steps = height // block
    slots = min(2, steps)
    groups = max(1, width // 1024)
    group = width // groups
    chunks = max(1, width // 1024)
    cut, apart = width // chunks, max(1, (steps - 2) // chunks)
    turns = [min(apart * k, steps - 1) for k in range(chunks)]

    def kernel(*refs):
        left, cols, flags, weight, *grads = refs[:6]
        state, out, targets, (ring, sems, fresh, fresh_sems) = refs[6:9], refs[9], refs[10:13], refs[13:]
        step = pl.program_id(0)
        slot = step % slots

        def emit(i, g):
            at, span = pl.ds(pl.multiple_of(i * block, block), block), pl.ds(g * group, group)
            return pltpu.make_async_copy(
                ring.at[i % slots, :, span], out.at[at, span], sems.at[i % slots, g]
            )

        def writes(p, k):
            span = pl.ds(k * cut, cut)
            return [
                pltpu.make_async_copy(
                    fresh.at[h, i, :, span], x.at[p ^ h, :, span], fresh_sems.at[h, i, k]
                )
                for h in range(2)
                for i, x in enumerate(targets)
            ]

        @pl.when(step >= slots)
        def _():
            for g in range(groups):
                emit(step - slots, g).wait()

        wide = min(width, 256)
        at = pl.ds(pl.multiple_of(step * block, block), block)
        for g in range(groups):
            for k in range(g * group, (g + 1) * group, wide):
                span = pl.ds(k, wide)
                change = jnp.dot(left[at, :], cols[:, span], preferred_element_type=jnp.float32)
                ring[slot, :, span] = (f32(weight[at, span]) + change).astype(ring.dtype)
            emit(step, g).start()

        for chunk, turn in enumerate(turns):

            @pl.when(step == turn)
            def _():
                p = jnp.max(half(flags, rank)[0:1, :])
                for k in range(chunk * cut, (chunk + 1) * cut, 128):
                    tile = pl.ds(k, 128)
                    for h, grad in enumerate(grads):
                        values = moment_update(
                            *[x[p ^ h, :, tile] for x in state], f32(grad[:, tile])
                        )
                        for i, value in enumerate(values):
                            fresh[h, i, :, tile] = value
                for copy in writes(p, chunk):
                    copy.start()

        @pl.when(step == steps - 1)
        def _():
            p = jnp.max(half(flags, rank)[0:1, :])
            for k in range(chunks):
                for copy in writes(p, k):
                    copy.wait()
            for i in range(steps - slots, steps):
                for g in range(groups):
                    emit(i, g).wait()

    operands = (left, cols, flags, weight, own, other, *state)
    outs = [pltpu.HBM((height, width), weight.dtype)] + [pltpu.HBM(x.shape, x.dtype) for x in state]
    result, *fresh = pl.pallas_call(
        kernel,
        grid=(steps,),
        in_specs=[pl.BlockSpec(memory_space=pltpu.VMEM)] * len(operands),
        out_specs=[pl.BlockSpec(memory_space=pltpu.HBM)] * len(outs),
        out_shape=outs,
        scratch_shapes=[
            vmem(slots, block, width),
            pltpu.SemaphoreType.DMA((slots, groups)),
            vmem(2, 3, rank, width, dtype=jnp.float32),
            pltpu.SemaphoreType.DMA((2, 3, chunks)),
        ],
        compiler_params=pltpu.CompilerParams(vmem_limit_bytes=21 * MIB),
        cost_estimate=pl.CostEstimate(flops=0, bytes_accessed=1024, transcendentals=0),
        name="refresh",
    )(*[pltpu.with_memory_space_constraint(x, pltpu.VMEM) for x in operands])
    return result, fresh


def tensor_sum_parts(low, size):
    parts, stride = [low], 1
    while stride < size:
        if len(parts) > 1:
            total = functools.reduce(jnp.add, [f32(x) for x in parts])
            parts = [total.astype(jnp.bfloat16)]
        radix = min(4, size // stride)
        mine = parts[0]
        for hop in range(1, radix):
            pairs = [
                (i, i - i % (stride * radix) + (i + hop * stride) % (stride * radix))
                for i in range(size)
            ]
            parts.append(lax.ppermute(mine, "tensor", pairs))
        stride *= radix
    return parts


def gather_rows(block, t_size, r_size):
    t = lax.axis_index("tensor")
    distance = 1
    while distance < max(1, t_size // r_size):
        other = swap(block, "tensor", t_size, distance)
        block = jnp.where(
            (t & distance) == 0,
            jnp.concatenate([block, other], axis=1),
            jnp.concatenate([other, block], axis=1),
        )
        distance *= 2
    return block


def spread_steps(t_size, r_size):
    distance, steps = t_size // 2, []
    while distance >= max(1, t_size // r_size):
        steps.append(distance)
        distance //= 2
    return steps


def spread_rest(distance, t_size, r_size):
    return functools.reduce(
        lambda a, b: a | b, [d for d in spread_steps(t_size, r_size) if d <= distance]
    )


def spread_send(block, distance, t_size, r_size):
    rest = spread_rest(distance, t_size, r_size)
    pairs = []
    for r in range(r_size):
        root = r * t_size // r_size
        for t in range(t_size):
            if (t ^ root) & rest == 0:
                pairs.append((t * r_size + r, (t ^ distance) * r_size + r))
    return lax.ppermute(block, ("tensor", "replica"), pairs)


def spread_take(came, block, distance, t_size, r_size, ties=()):
    rest = spread_rest(distance, t_size, r_size)

    def kernel(came, block, out):
        t, r = lax.axis_index("tensor"), lax.axis_index("replica")
        takes = ((t ^ (r * t_size // r_size)) & rest) == distance

        @pl.when(takes)
        def _():
            out[...] = came[...]

        @pl.when(jnp.logical_not(takes))
        def _():
            out[...] = block[...]

    return local(kernel, "spread", [vmem(*block.shape)], ins=(came, block), ties=ties)[0]


def own_rows(block, t_size, r_size):
    parts = max(1, r_size // t_size)
    if parts == 1:
        return block
    size = block.shape[1] // parts
    return lax.dynamic_slice_in_dim(block, (lax.axis_index("replica") % parts) * size, size, 1)


def per_device(
    acts,
    cots,
    down_factor,
    up_factor,
    down_first_moment,
    down_second_moment,
    up_first_moment,
    up_second_moment,
    rollout_weight,
    owner,
    projection_index,
):
    t_size, r_size = lax.axis_size("tensor"), lax.axis_size("replica")
    turn = lambda x: jnp.transpose(x, (0, 2, 1))
    down_state = tuple(map(turn, (down_factor, down_first_moment, down_second_moment)))
    up_state = (up_factor, up_first_moment, up_second_moment)
    coefficient = adapter_scale / (acts.shape[1] * r_size)
    down_half = functools.partial(down_parity, t_size=t_size, r_size=r_size)
    up_half = functools.partial(up_parity, t_size=t_size, r_size=r_size)
    exchange = lambda x, distance: swap(x, "replica", r_size, distance)

    low, acts_in, cots_in = low_parts(acts, cots, down_state[0], up_state[0])
    lows = tensor_sum_parts(low, t_size)
    up_send, up_own = gradient_parts(
        lows, cots_in, (), 2, coefficient, up_half,
    )
    up_came = exchange(up_send, 1)
    down_held, up_held, flags = load_state(
        down_state, up_state, projection_index, owner, t_size, r_size, up_send
    )
    down_send, down_own = gradient_parts(lows, acts_in, (flags,), 0, coefficient, down_half)
    up_own, down_send = join((up_own, up_came), passed=(down_send,))
    up_came, distance = exchange(up_own, 2), 4
    down_came = exchange(down_send, 1)
    while distance < r_size:
        (up_own,) = join((up_own, up_came))
        up_came, distance = exchange(up_own, distance), 2 * distance
    (up_own,) = join((up_own, up_came))
    (down_own,) = join((down_own, down_came), ties=(up_own,))
    up_other = exchange(up_own, 1)
    distance = 2
    while 2 * distance < r_size:
        (down_own,) = join((down_own, exchange(down_own, distance)))
        distance *= 2
    down_came = exchange(down_own, distance)

    (up_mine,) = chosen_factor(up_held, [up_own], [up_other], flags, up_half)
    held, shift = [up_mine], 1
    while shift < t_size // 2:
        held = held + [swap(x, "tensor", t_size, shift) for x in held]
        shift *= 2
    (offered,) = offer(held, flags, t_size, ties=(down_came,))
    held = held + [swap(offered, "tensor", t_size, t_size // 2)]
    (block,) = chosen_factor(
        down_held, [down_own, down_came], [], flags, down_half, ties=(offered,)
    )
    block = gather_rows(block, t_size, r_size)
    first, *others = spread_steps(t_size, r_size)
    came = spread_send(block, first, t_size, r_size)
    (down_own,) = join((down_own, down_came), ties=(block,))
    down_other = exchange(down_own, 1)
    fresh_up = adam(up_held, up_own, up_other, flags, up_half, ties=(down_own,))
    cols = columns_of_b(held, flags, t_size, after=(fresh_up[0],))
    rows = spread_take(came, block, first, t_size, r_size, ties=(cols,))
    for shift in others:
        came = spread_send(rows, shift, t_size, r_size)
        rows = spread_take(came, rows, shift, t_size, r_size, ties=(down_other,))
    left = rows_of_a(own_rows(rows, t_size, r_size))
    fresh_rollout_weight, fresh_down = refresh(
        left, cols, flags, rollout_weight, down_held, down_own, down_other, down_half
    )
    return (
        turn(fresh_down[0]),
        fresh_up[0],
        turn(fresh_down[1]),
        turn(fresh_down[2]),
        fresh_up[1],
        fresh_up[2],
        fresh_rollout_weight,
    )


def solution(mesh):
    placed = (
        P(None, ("groups", "replica"), "tensor"),
        P(None, ("groups", "replica"), "tensor"),
        P("groups", "tensor", None),
        P("groups", None, "tensor"),
        P("groups", "tensor", None),
        P("groups", "tensor", None),
        P("groups", None, "tensor"),
        P("groups", None, "tensor"),
        P("replica", "tensor"),
        P(),
        P("groups"),
    )
    return jax.shard_map(
        per_device,
        mesh=mesh,
        in_specs=placed,
        out_specs=(
            P("groups", "tensor", None),
            P("groups", None, "tensor"),
            P("groups", "tensor", None),
            P("groups", "tensor", None),
            P("groups", None, "tensor"),
            P("groups", None, "tensor"),
            P(("groups", "replica"), "tensor"),
        ),
        check_vma=False,
    )
```

```python
import functools

import jax
import jax.numpy as jnp
from jax import lax
from jax.experimental import pallas as pl
from jax.experimental.pallas import tpu as pltpu
from jax.sharding import PartitionSpec as P

adapter_scale = 2.0
learn_rate = 0.05
beta_one = 0.9
beta_two = 0.999
adam_eps = 1e-08
fix_one = 1.0 - 0.9**10
fix_two = 1.0 - 0.999**10

MIB = 1024 * 1024
FLAGS = ("proj", "column_proj", "mine", "partners")


def moment_update(param, first, second, grad):
    first_new = beta_one * first + (1.0 - beta_one) * grad
    second_new = beta_two * second + (1.0 - beta_two) * grad * grad
    size = second_new * (1.0 / fix_two)
    param_new = param - (learn_rate / fix_one) * first_new / (size * lax.rsqrt(size) + adam_eps)
    return (param_new, first_new, second_new)


def f32(x):
    return x.astype(jnp.float32)


def swap(x, axis, size, distance):
    return lax.ppermute(x, axis, [(i, i ^ distance) for i in range(size)])


def vmem(*shape, dtype=jnp.bfloat16):
    return pltpu.VMEM(shape, dtype)


def local(kernel, name, outs, ins=(), hbm=(), smem=(), ties=(), after=(), passed=(), scratch=(), work=1024):
    n_ins, n_first = len(ins), len(ins) + len(hbm) + len(smem)
    n_outs = len(outs)

    def body(*refs):
        front = refs[:n_first]
        rest = refs[n_first + len(ties) + len(after) + len(passed) :]
        kernel(*front, *rest[:n_outs], *rest[n_outs + len(passed) :])

    operands = (
        [pltpu.with_memory_space_constraint(x, pltpu.VMEM) for x in ins]
        + [pltpu.with_memory_space_constraint(x, pltpu.HBM) for x in hbm]
        + [pltpu.with_memory_space_constraint(x, pltpu.HBM) for x in smem]
        + [pltpu.with_memory_space_constraint(x, pltpu.VMEM) for x in ties]
        + [pltpu.with_memory_space_constraint(x, pltpu.HBM) for x in after]
        + [pltpu.with_memory_space_constraint(x, pltpu.VMEM) for x in passed]
    )
    specs = (
        [pl.BlockSpec(memory_space=pltpu.VMEM)] * n_ins
        + [pl.BlockSpec(memory_space=pltpu.HBM)] * len(hbm)
        + [pl.BlockSpec(memory_space=pltpu.SMEM)] * len(smem)
        + [pl.BlockSpec(memory_space=pl.ANY)] * (len(ties) + len(after) + len(passed))
    )
    first_passed = n_first + len(ties) + len(after)
    return pl.pallas_call(
        body,
        in_specs=specs,
        out_specs=[pl.BlockSpec(memory_space=pltpu.VMEM)] * n_outs
        + [pl.BlockSpec(memory_space=pl.ANY)] * len(passed),
        out_shape=list(outs) + [pltpu.VMEM(x.shape, x.dtype) for x in passed],
        input_output_aliases={first_passed + i: n_outs + i for i in range(len(passed))},
        scratch_shapes=list(scratch),
        compiler_params=pltpu.CompilerParams(vmem_limit_bytes=8 * MIB),
        cost_estimate=pl.CostEstimate(flops=0, bytes_accessed=work, transcendentals=0),
        name=name,
    )(*operands)


def low_parts(acts, cots, down, up):
    tokens = acts.shape[1]
    rank = down.shape[1]

    def kernel(acts, cots, down, up, low, acts_in, cots_in, down_in, up_in, sems):
        jobs = []
        for spot, (x, x_in, f, f_in) in enumerate(
            ((cots, cots_in, up, up_in), (acts, acts_in, down, down_in))
        ):
            for p in range(2):
                i = 2 * spot + p
                pair = (
                    pltpu.make_async_copy(x.at[p], x_in.at[p], sems.at[2 * i]),
                    pltpu.make_async_copy(f.at[p], f_in.at[p], sems.at[2 * i + 1]),
                )
                for copy in pair:
                    copy.start()
                jobs.append((pair, x_in, f_in, p, i))
        for pair, x_in, f_in, p, i in jobs:
            for copy in pair:
                copy.wait()
            low[pl.ds(i * rank, rank), :] = lax.dot_general(
                f_in[p].astype(jnp.bfloat16),
                x_in[p],
                (((1,), (1,)), ((), ())),
                preferred_element_type=jnp.float32,
            ).astype(low.dtype)

    return local(
        kernel,
        "low_parts",
        [vmem(4 * rank, tokens), vmem(*acts.shape), vmem(*cots.shape)],
        hbm=(acts, cots, down, up),
        scratch=[
            vmem(*down.shape, dtype=jnp.float32),
            vmem(*up.shape, dtype=jnp.float32),
            pltpu.SemaphoreType.DMA((8,)),
        ],
    )


def load_state(down_state, up_state, projection_index, owner, t_size, r_size, tie):
    rank = down_state[0].shape[1]

    def kernel(*refs):
        sources, (index, owner), targets, (flags, sems) = refs[:6], refs[6:8], refs[8:14], refs[14:]
        copies = [
            pltpu.make_async_copy(x, y, sems.at[i]) for i, (x, y) in enumerate(zip(sources, targets))
        ]
        for copy in copies:
            copy.start()
        t, r = lax.axis_index("tensor"), lax.axis_index("replica")
        values = (index[r], index[t * r_size // t_size], owner[t], owner[t ^ (t_size // 2)])
        for i, value in enumerate(values):
            flags[pl.ds(i * rank, rank), :] = jnp.full((rank, 128), value, jnp.int32)
        for copy in copies:
            copy.wait()

    *state, flags = local(
        kernel,
        "load_state",
        [vmem(*x.shape, dtype=jnp.float32) for x in (*down_state, *up_state)]
        + [vmem(len(FLAGS) * rank, 128, dtype=jnp.int32)],
        hbm=(*down_state, *up_state),
        smem=(projection_index, owner),
        ties=(tie,),
        scratch=[pltpu.SemaphoreType.DMA((6,))],
    )
    return state[:3], state[3:], flags


def flag(flags, name, rank):
    return flags[pl.ds(FLAGS.index(name) * rank, rank), :]


def column_tiles(width):
    return [pl.ds(k, 128) for k in range(0, width, 128)]


def down_parity(flags, rank, t_size, r_size):
    t, r = lax.axis_index("tensor"), lax.axis_index("replica")
    return flag(flags, "column_proj", rank) ^ ((r + t * r_size // t_size) % 2)


def up_parity(flags, rank, t_size, r_size):
    r = lax.axis_index("replica")
    return jnp.full((rank, 128), r % 2, jnp.int32)


def gradient_parts(lows, tokens, flags, base, coefficient, half, ties=()):
    rank = lows[0].shape[0] // 4
    width = tokens.shape[2]
    parts = len(lows)

    def kernel(*refs):
        lows, tokens, flags, (send, keep) = refs[:parts], refs[parts], refs[parts + 1 : -2], refs[-2:]
        rows = pl.ds(base * rank, 2 * rank)
        total = functools.reduce(jnp.add, [f32(x[rows, :]) for x in lows]).astype(jnp.bfloat16)
        kept = half(flags[0] if flags else None, rank) == 0
        cut = min(width, 512)
        for k in range(0, width, cut):
            grads = [
                coefficient
                * jnp.dot(
                    total[p * rank : (p + 1) * rank],
                    tokens[p, :, pl.ds(k, cut)],
                    preferred_element_type=jnp.float32,
                )
                for p in range(2)
            ]
            for j in range(0, cut, 128):
                first, second = [g[:, j : j + 128] for g in grads]
                tile = pl.ds(k + j, 128)
                keep[:, tile] = jnp.where(kept, first, second).astype(keep.dtype)
                send[:, tile] = jnp.where(kept, second, first).astype(send.dtype)

    return local(
        kernel,
        "gradient_parts",
        [vmem(rank, width), vmem(rank, width)],
        ins=(*lows, tokens, *flags),
        ties=ties,
    )


def join(*sums, ties=(), after=(), passed=()):
    terms = [x for group in sums for x in group]

    def kernel(*refs):
        refs, outs = list(refs[: len(terms)]), refs[len(terms) :]
        for group, out in zip(sums, outs):
            total = functools.reduce(jnp.add, [f32(refs.pop(0)[...]) for _ in group])
            out[...] = total.astype(out.dtype)

    return local(
        kernel,
        "join",
        [vmem(*group[0].shape) for group in sums],
        ins=terms,
        ties=ties,
        after=after,
        passed=passed,
    )


def chosen_factor(state, own, other, flags, half, ties=(), after=(), passed=()):
    rank, width = own[0].shape
    n_own, n_other = len(own), len(other)

    def total(refs, tile):
        return f32(functools.reduce(jnp.add, [f32(x[:, tile]) for x in refs]).astype(jnp.bfloat16))

    def kernel(*refs):
        state, own, other = refs[:3], refs[3 : 3 + n_own], refs[3 + n_own : 3 + n_own + n_other]
        flags, out = refs[3 + n_own + n_other :]
        p = jnp.max(flag(flags, "proj", rank)[0:1, :])
        for tile in column_tiles(width):
            grad = total(own, tile)
            if other:
                mine = flag(flags, "proj", rank) == half(flags, rank)
                grad = jnp.where(mine, grad, total(other, tile))
            held = [x[p, :, tile] for x in state]
            out[:, tile] = moment_update(*held, grad)[0].astype(out.dtype)

    return local(
        kernel,
        "chosen_factor",
        [vmem(rank, width)],
        ins=(*state, *own, *other, flags),
        ties=ties,
        after=after,
        passed=passed,
    )


def adam(state, own, other, flags, half, ties=()):
    rank, width = own.shape
    cuts = max(1, width // 1024)
    cut = width // cuts

    def kernel(*refs):
        state, own, other, flags, outs, (fresh, sems) = refs[:3], *refs[3:6], refs[-5:-2], refs[-2:]
        kept = half(flags, rank)
        copies = []
        for k in range(cuts):
            for j in range(k * cut, (k + 1) * cut, 128):
                tile = pl.ds(j, 128)
                grads = f32(own[:, tile]), f32(other[:, tile])
                for p in range(2):
                    grad = jnp.where(kept == p, *grads)
                    values = moment_update(*[x[p, :, tile] for x in state], grad)
                    for i, value in enumerate(values):
                        fresh[i, p, :, tile] = value
            span = pl.ds(k * cut, cut)
            for i, x in enumerate(outs):
                copies.append(
                    pltpu.make_async_copy(fresh.at[i, :, :, span], x.at[:, :, span], sems.at[k, i])
                )
                copies[-1].start()
        for copy in copies:
            copy.wait()

    in_vmem = (*state, own, other, flags, *ties)
    return pl.pallas_call(
        kernel,
        in_specs=[pl.BlockSpec(memory_space=pltpu.VMEM)] * 6
        + [pl.BlockSpec(memory_space=pl.ANY)] * len(ties),
        out_specs=[pl.BlockSpec(memory_space=pltpu.HBM)] * 3,
        out_shape=[pltpu.HBM(x.shape, x.dtype) for x in state],
        scratch_shapes=[
            vmem(3, 2, rank, width, dtype=jnp.float32),
            pltpu.SemaphoreType.DMA((cuts, 3)),
        ],
        compiler_params=pltpu.CompilerParams(vmem_limit_bytes=8 * MIB),
        cost_estimate=pl.CostEstimate(flops=0, bytes_accessed=1024, transcendentals=0),
        name="adam",
    )(*[pltpu.with_memory_space_constraint(x, pltpu.VMEM) for x in in_vmem])


def adam_half(state, grad, flags, half, flip, outs, after):
    rank, width = grad.shape
    cuts = max(1, width // 1024)
    cut = width // cuts

    def kernel(*refs):
        grad, flags, state = refs[0], refs[1], refs[2:5]
        targets, (fresh, sems) = refs[-5:-2], refs[-2:]
        p = jnp.max(half(flags, rank)[0:1, :]) ^ flip
        copies = []
        for k in range(cuts):
            for j in range(k * cut, (k + 1) * cut, 128):
                tile = pl.ds(j, 128)
                values = moment_update(*[x[p, :, tile] for x in state], f32(grad[:, tile]))
                for i, value in enumerate(values):
                    fresh[i, :, tile] = value
            span = pl.ds(k * cut, cut)
            for i, x in enumerate(targets):
                copies.append(
                    pltpu.make_async_copy(fresh.at[i, :, span], x.at[p, :, span], sems.at[k, i])
                )
                copies[-1].start()
        for copy in copies:
            copy.wait()

    in_vmem, in_hbm = (grad, flags, *state), (*after, *outs)
    first = len(in_vmem) + len(after)
    return pl.pallas_call(
        kernel,
        in_specs=[pl.BlockSpec(memory_space=pltpu.VMEM)] * len(in_vmem)
        + [pl.BlockSpec(memory_space=pltpu.HBM)] * len(in_hbm),
        out_specs=[pl.BlockSpec(memory_space=pltpu.HBM)] * 3,
        out_shape=[pltpu.HBM(x.shape, x.dtype) for x in state],
        input_output_aliases={first + i: i for i in range(3)},
        scratch_shapes=[
            vmem(3, rank, width, dtype=jnp.float32),
            pltpu.SemaphoreType.DMA((cuts, 3)),
        ],
        compiler_params=pltpu.CompilerParams(vmem_limit_bytes=8 * MIB),
        cost_estimate=pl.CostEstimate(flops=0, bytes_accessed=1024, transcendentals=0),
        name="adam_half",
    )(
        *[pltpu.with_memory_space_constraint(x, pltpu.VMEM) for x in in_vmem],
        *[pltpu.with_memory_space_constraint(x, pltpu.HBM) for x in in_hbm],
    )


def pick(flags, name, held, ids, rank):
    wanted = flag(flags, name, rank)

    def tile_of(tile):
        found = f32(held[0][:, tile])
        for i in range(1, len(held)):
            found = jnp.where(wanted == ids[i], f32(held[i][:, tile]), found)
        return found

    return tile_of


def block_ids(t_size, many):
    t = lax.axis_index("tensor")
    ids, distance = [t], 1
    while distance < t_size // 2:
        ids = ids + [i ^ distance for i in ids]
        distance *= 2
    return ids[:many]


def offer(held, flags, t_size, ties=()):
    rank, width = held[0].shape

    def kernel(*refs):
        held, flags, out = refs[:-2], refs[-2], refs[-1]
        tile_of = pick(flags, "partners", held, block_ids(t_size, len(held)), rank)
        for tile in column_tiles(width):
            out[:, tile] = tile_of(tile).astype(out.dtype)

    return local(kernel, "offer", [vmem(rank, width)], ins=(*held, flags), ties=ties)


def columns_of_b(held, flags, t_size, ties=()):
    rank, width = held[0].shape

    def kernel(*refs):
        held, flags, cols = refs[:-2], refs[-2], refs[-1]
        ids = block_ids(t_size, len(held) - 1)
        tile_of = pick(flags, "mine", (held[-1], *held[:-1]), (None, *ids), rank)
        for tile in column_tiles(width):
            cols[:, tile] = (adapter_scale * tile_of(tile)).astype(cols.dtype)

    return local(
        kernel, "columns_of_b", [vmem(rank, width)], ins=(*held, flags), ties=ties
    )[0]


def rows_of_a(block, came=None, distance=0, t_size=0, r_size=0, ties=()):
    rank, height = block.shape

    def kernel(*refs):
        left = refs[-1]
        if came is None:
            takes = None
        else:
            t, r = lax.axis_index("tensor"), lax.axis_index("replica")
            rest = spread_rest(distance, t_size, r_size)
            takes = ((t ^ (r * t_size // r_size)) & rest) == distance
        for j in range(0, height, 128):
            tile = pl.ds(j, 128)
            rows = refs[0][:, tile]
            if takes is not None:
                rows = jnp.where(takes, f32(refs[1][:, tile]), f32(rows)).astype(rows.dtype)
            left[tile, :] = rows.T

    ins = (block,) if came is None else (block, came)
    return local(kernel, "rows_of_a", [vmem(height, rank)], ins=ins, ties=ties)[0]


def refresh(left, cols, flags, weight, state, grad, half):
    height, width = weight.shape
    rank = cols.shape[0]
    block = min(height, 1024)
    steps = height // block
    slots = min(2, steps)
    groups = max(1, width // 512)
    group = width // groups
    chunks = max(1, width // 1024)
    cut, apart = width // chunks, max(1, (steps - 2) // chunks)
    turns = [min(apart * k, steps - 1) for k in range(chunks)]

    def kernel(*refs):
        left, cols, flags, weight, grad, *state = refs[:8]
        out, targets, (ring, sems, fresh, fresh_sems) = refs[8], refs[9:12], refs[12:]
        step = pl.program_id(0)
        slot = step % slots

        def emit(i, g):
            at, span = pl.ds(pl.multiple_of(i * block, block), block), pl.ds(g * group, group)
            return pltpu.make_async_copy(
                ring.at[i % slots, :, span], out.at[at, span], sems.at[i % slots, g]
            )

        def writes(p, k):
            span = pl.ds(k * cut, cut)
            return [
                pltpu.make_async_copy(fresh.at[i, :, span], x.at[p, :, span], fresh_sems.at[i, k])
                for i, x in enumerate(targets)
            ]

        for chunk, turn in enumerate(turns):

            @pl.when(step == turn)
            def _():
                p = jnp.max(half(flags, rank)[0:1, :])
                for k in range(chunk * cut, (chunk + 1) * cut, 128):
                    tile = pl.ds(k, 128)
                    values = moment_update(*[x[p, :, tile] for x in state], f32(grad[:, tile]))
                    for i, value in enumerate(values):
                        fresh[i, :, tile] = value
                for copy in writes(p, chunk):
                    copy.start()

        @pl.when(step >= slots)
        def _():
            for g in range(groups):
                emit(step - slots, g).wait()

        wide = min(width, 256)
        at = pl.ds(pl.multiple_of(step * block, block), block)
        for g in range(groups):
            for k in range(g * group, (g + 1) * group, wide):
                span = pl.ds(k, wide)
                change = jnp.dot(left[at, :], cols[:, span], preferred_element_type=jnp.float32)
                ring[slot, :, span] = (f32(weight[at, span]) + change).astype(ring.dtype)
            emit(step, g).start()

        @pl.when(step == steps - 1)
        def _():
            p = jnp.max(half(flags, rank)[0:1, :])
            for k in range(chunks):
                for copy in writes(p, k):
                    copy.wait()
            for i in range(steps - slots, steps):
                for g in range(groups):
                    emit(i, g).wait()

    operands = (left, cols, flags, weight, grad, *state)
    outs = [pltpu.HBM((height, width), weight.dtype)] + [pltpu.HBM(x.shape, x.dtype) for x in state]
    result, *fresh = pl.pallas_call(
        kernel,
        grid=(steps,),
        in_specs=[pl.BlockSpec(memory_space=pltpu.VMEM)] * len(operands),
        out_specs=[pl.BlockSpec(memory_space=pltpu.HBM)] * len(outs),
        out_shape=outs,
        scratch_shapes=[
            vmem(slots, block, width),
            pltpu.SemaphoreType.DMA((slots, groups)),
            vmem(3, rank, width, dtype=jnp.float32),
            pltpu.SemaphoreType.DMA((3, chunks)),
        ],
        compiler_params=pltpu.CompilerParams(vmem_limit_bytes=20 * MIB),
        cost_estimate=pl.CostEstimate(flops=0, bytes_accessed=1024, transcendentals=0),
        name="refresh",
    )(*[pltpu.with_memory_space_constraint(x, pltpu.VMEM) for x in operands])
    return result, fresh


def tensor_sum_parts(low, size):
    parts, stride = [low], 1
    while stride < size:
        if len(parts) > 1:
            total = functools.reduce(jnp.add, [f32(x) for x in parts])
            parts = [total.astype(jnp.bfloat16)]
        radix = min(4, size // stride)
        mine = parts[0]
        for hop in range(1, radix):
            pairs = [
                (i, i - i % (stride * radix) + (i + hop * stride) % (stride * radix))
                for i in range(size)
            ]
            parts.append(lax.ppermute(mine, "tensor", pairs))
        stride *= radix
    return parts


def toward(block, distance, t_size, r_size, first):
    pairs = []
    for t in range(t_size):
        root = t * r_size // t_size
        for r in range(r_size):
            same_side = ((r ^ root) & distance) == 0
            same_half = (r ^ root) % 2 == 0
            if (same_side != same_half) == first:
                pairs.append((t * r_size + r, t * r_size + (r ^ distance)))
    return lax.ppermute(block, ("tensor", "replica"), pairs)


def gather_rows(block, t_size, r_size):
    t = lax.axis_index("tensor")
    distance = 1
    while distance < max(1, t_size // r_size):
        other = swap(block, "tensor", t_size, distance)
        block = jnp.where(
            (t & distance) == 0,
            jnp.concatenate([block, other], axis=1),
            jnp.concatenate([other, block], axis=1),
        )
        distance *= 2
    return block


def spread_steps(t_size, r_size):
    distance, steps = t_size // 2, []
    while distance >= max(1, t_size // r_size):
        steps.append(distance)
        distance //= 2
    return steps


def spread_rest(distance, t_size, r_size):
    return functools.reduce(
        lambda a, b: a | b, [d for d in spread_steps(t_size, r_size) if d <= distance]
    )


def spread_send(block, distance, t_size, r_size):
    rest = spread_rest(distance, t_size, r_size)
    pairs = []
    for r in range(r_size):
        root = r * t_size // r_size
        for t in range(t_size):
            if (t ^ root) & rest == 0:
                pairs.append((t * r_size + r, (t ^ distance) * r_size + r))
    return lax.ppermute(block, ("tensor", "replica"), pairs)


def spread_take(came, block, distance, t_size, r_size, ties=()):
    rest = spread_rest(distance, t_size, r_size)

    def kernel(came, block, out):
        t, r = lax.axis_index("tensor"), lax.axis_index("replica")
        takes = ((t ^ (r * t_size // r_size)) & rest) == distance

        @pl.when(takes)
        def _():
            out[...] = came[...]

        @pl.when(jnp.logical_not(takes))
        def _():
            out[...] = block[...]

    return local(kernel, "spread", [vmem(*block.shape)], ins=(came, block), ties=ties)[0]


def own_rows(block, t_size, r_size):
    parts = max(1, r_size // t_size)
    if parts == 1:
        return block
    size = block.shape[1] // parts
    return lax.dynamic_slice_in_dim(block, (lax.axis_index("replica") % parts) * size, size, 1)


def per_device(
    acts,
    cots,
    down_factor,
    up_factor,
    down_first_moment,
    down_second_moment,
    up_first_moment,
    up_second_moment,
    rollout_weight,
    owner,
    projection_index,
):
    t_size, r_size = lax.axis_size("tensor"), lax.axis_size("replica")
    turn = lambda x: jnp.transpose(x, (0, 2, 1))
    down_state = tuple(map(turn, (down_factor, down_first_moment, down_second_moment)))
    up_state = (up_factor, up_first_moment, up_second_moment)
    coefficient = adapter_scale / (acts.shape[1] * r_size)
    down_half = functools.partial(down_parity, t_size=t_size, r_size=r_size)
    up_half = functools.partial(up_parity, t_size=t_size, r_size=r_size)
    exchange = lambda x, distance: swap(x, "replica", r_size, distance)

    low, acts_in, cots_in = low_parts(acts, cots, down_state[0], up_state[0])
    lows = tensor_sum_parts(low, t_size)
    up_send, up_own = gradient_parts(
        lows, cots_in, (), 2, coefficient, up_half,
    )
    up_came = exchange(up_send, 1)
    down_held, up_held, flags = load_state(
        down_state, up_state, projection_index, owner, t_size, r_size, up_send
    )
    down_send, down_own = gradient_parts(lows, acts_in, (flags,), 0, coefficient, down_half)
    up_own, down_send = join((up_own, up_came), passed=(down_send,))
    up_came, distance = exchange(up_own, 2), 4
    down_came = exchange(down_send, 1)
    while distance < r_size:
        (up_own,) = join((up_own, up_came))
        up_came, distance = exchange(up_own, distance), 2 * distance
    down_own, again = join(*[(down_own, down_came)] * 2)
    (up_own,) = join((up_own, up_came), ties=(down_own,))
    up_other = exchange(up_own, 1)
    distance = 2
    while 2 * distance < r_size:
        down_own, again = join(*[(down_own, exchange(down_own, distance))] * 2)
        distance *= 2
    down_first = toward(down_own, distance, t_size, r_size, True)

    (block,) = chosen_factor(down_held, [down_own, down_first], [], flags, down_half)
    block = gather_rows(block, t_size, r_size)
    steps = spread_steps(t_size, r_size)
    rows = spread_send(block, steps[0], t_size, r_size)
    up_mine, again = chosen_factor(
        up_held, [up_own], [up_other], flags, up_half, ties=(block,), passed=(again,)
    )
    down_rest = toward(again, distance, t_size, r_size, False)
    held, shift = [up_mine], 1
    while shift < t_size // 2:
        held = held + [swap(x, "tensor", t_size, shift) for x in held]
        shift *= 2
    rows = spread_take(rows, block, steps[0], t_size, r_size)
    (offered,) = offer(held, flags, t_size, ties=(rows,))
    held = held + [swap(offered, "tensor", t_size, t_size // 2)]
    fresh_up = adam(up_held, up_own, up_other, flags, up_half, ties=(offered,))
    (down_own,) = join((down_own, down_first, down_rest), after=(fresh_up[0],))
    down_other = exchange(down_own, 1)
    cols = columns_of_b(held, flags, t_size, ties=(down_own,))
    for shift in steps[1:-1]:
        came = spread_send(rows, shift, t_size, r_size)
        rows = spread_take(came, rows, shift, t_size, r_size, ties=(cols,))
    came = spread_send(rows, steps[-1], t_size, r_size)
    if r_size <= t_size:
        left = rows_of_a(rows, came, steps[-1], t_size, r_size, ties=(cols,))
    else:
        rows = spread_take(came, rows, steps[-1], t_size, r_size, ties=(cols,))
        left = rows_of_a(own_rows(rows, t_size, r_size))
    fresh_rollout_weight, fresh_down = refresh(
        left, cols, flags, rollout_weight, down_held, down_own, down_half
    )
    fresh_down = adam_half(
        down_held, down_other, flags, down_half, 1, fresh_down, (fresh_rollout_weight,)
    )
    return (
        turn(fresh_down[0]),
        fresh_up[0],
        turn(fresh_down[1]),
        turn(fresh_down[2]),
        fresh_up[1],
        fresh_up[2],
        fresh_rollout_weight,
    )


def solution(mesh):
    placed = (
        P(None, ("groups", "replica"), "tensor"),
        P(None, ("groups", "replica"), "tensor"),
        P("groups", "tensor", None),
        P("groups", None, "tensor"),
        P("groups", "tensor", None),
        P("groups", "tensor", None),
        P("groups", None, "tensor"),
        P("groups", None, "tensor"),
        P("replica", "tensor"),
        P(),
        P("groups"),
    )
    return jax.shard_map(
        per_device,
        mesh=mesh,
        in_specs=placed,
        out_specs=(
            P("groups", "tensor", None),
            P("groups", None, "tensor"),
            P("groups", "tensor", None),
            P("groups", "tensor", None),
            P("groups", None, "tensor"),
            P("groups", None, "tensor"),
            P(("groups", "replica"), "tensor"),
        ),
        check_vma=False,
    )
```

```python
import functools

import jax
import jax.numpy as jnp
from jax import lax
from jax.experimental import pallas as pl
from jax.experimental.pallas import tpu as pltpu
from jax.sharding import PartitionSpec as P

adapter_scale = 2.0
learn_rate = 0.05
beta_one = 0.9
beta_two = 0.999
adam_eps = 1e-08
fix_one = 1.0 - 0.9**10
fix_two = 1.0 - 0.999**10

MIB = 1024 * 1024
FLAGS = ("proj", "column_proj", "mine", "partners")


def moment_update(param, first, second, grad):
    first_new = beta_one * first + (1.0 - beta_one) * grad
    second_new = beta_two * second + (1.0 - beta_two) * grad * grad
    size = second_new * (1.0 / fix_two)
    param_new = param - (learn_rate / fix_one) * first_new / (size * lax.rsqrt(size) + adam_eps)
    return (param_new, first_new, second_new)


def f32(x):
    return x.astype(jnp.float32)


def swap(x, axis, size, distance):
    return lax.ppermute(x, axis, [(i, i ^ distance) for i in range(size)])


def vmem(*shape, dtype=jnp.bfloat16):
    return pltpu.VMEM(shape, dtype)


def local(kernel, name, outs, ins=(), hbm=(), smem=(), ties=(), after=(), passed=(), scratch=(), work=1024):
    n_ins, n_first = len(ins), len(ins) + len(hbm) + len(smem)
    n_outs = len(outs)

    def body(*refs):
        front = refs[:n_first]
        rest = refs[n_first + len(ties) + len(after) + len(passed) :]
        kernel(*front, *rest[:n_outs], *rest[n_outs + len(passed) :])

    operands = (
        [pltpu.with_memory_space_constraint(x, pltpu.VMEM) for x in ins]
        + [pltpu.with_memory_space_constraint(x, pltpu.HBM) for x in hbm]
        + [pltpu.with_memory_space_constraint(x, pltpu.HBM) for x in smem]
        + [pltpu.with_memory_space_constraint(x, pltpu.VMEM) for x in ties]
        + [pltpu.with_memory_space_constraint(x, pltpu.HBM) for x in after]
        + [pltpu.with_memory_space_constraint(x, pltpu.VMEM) for x in passed]
    )
    specs = (
        [pl.BlockSpec(memory_space=pltpu.VMEM)] * n_ins
        + [pl.BlockSpec(memory_space=pltpu.HBM)] * len(hbm)
        + [pl.BlockSpec(memory_space=pltpu.SMEM)] * len(smem)
        + [pl.BlockSpec(memory_space=pl.ANY)] * (len(ties) + len(after) + len(passed))
    )
    first_passed = n_first + len(ties) + len(after)
    return pl.pallas_call(
        body,
        in_specs=specs,
        out_specs=[pl.BlockSpec(memory_space=pltpu.VMEM)] * n_outs
        + [pl.BlockSpec(memory_space=pl.ANY)] * len(passed),
        out_shape=list(outs) + [pltpu.VMEM(x.shape, x.dtype) for x in passed],
        input_output_aliases={first_passed + i: n_outs + i for i in range(len(passed))},
        scratch_shapes=list(scratch),
        compiler_params=pltpu.CompilerParams(vmem_limit_bytes=8 * MIB),
        cost_estimate=pl.CostEstimate(flops=0, bytes_accessed=work, transcendentals=0),
        name=name,
    )(*operands)


def low_parts(acts, cots, down, up):
    tokens = acts.shape[1]
    rank = down.shape[1]

    def kernel(acts, cots, down, up, low, acts_in, cots_in, down_in, up_in, sems):
        jobs = []
        for spot, (x, x_in, f, f_in) in enumerate(
            ((cots, cots_in, up, up_in), (acts, acts_in, down, down_in))
        ):
            for p in range(2):
                i = 2 * spot + p
                pair = (
                    pltpu.make_async_copy(x.at[p], x_in.at[p], sems.at[2 * i]),
                    pltpu.make_async_copy(f.at[p], f_in.at[p], sems.at[2 * i + 1]),
                )
                for copy in pair:
                    copy.start()
                jobs.append((pair, x_in, f_in, p, i))
        for pair, x_in, f_in, p, i in jobs:
            for copy in pair:
                copy.wait()
            low[pl.ds(i * rank, rank), :] = lax.dot_general(
                f_in[p].astype(jnp.bfloat16),
                x_in[p],
                (((1,), (1,)), ((), ())),
                preferred_element_type=jnp.float32,
            ).astype(low.dtype)

    return local(
        kernel,
        "low_parts",
        [vmem(4 * rank, tokens), vmem(*acts.shape), vmem(*cots.shape)],
        hbm=(acts, cots, down, up),
        scratch=[
            vmem(*down.shape, dtype=jnp.float32),
            vmem(*up.shape, dtype=jnp.float32),
            pltpu.SemaphoreType.DMA((8,)),
        ],
    )


def load_state(down_state, up_state, projection_index, owner, t_size, r_size, tie):
    rank = down_state[0].shape[1]

    def kernel(*refs):
        sources, (index, owner), targets, (flags, sems) = refs[:6], refs[6:8], refs[8:14], refs[14:]
        copies = [
            pltpu.make_async_copy(x, y, sems.at[i]) for i, (x, y) in enumerate(zip(sources, targets))
        ]
        for copy in copies:
            copy.start()
        t, r = lax.axis_index("tensor"), lax.axis_index("replica")
        values = (index[r], index[t * r_size // t_size], owner[t], owner[t ^ (t_size // 2)])
        for i, value in enumerate(values):
            flags[pl.ds(i * rank, rank), :] = jnp.full((rank, 128), value, jnp.int32)
        for copy in copies:
            copy.wait()

    *state, flags = local(
        kernel,
        "load_state",
        [vmem(*x.shape, dtype=jnp.float32) for x in (*down_state, *up_state)]
        + [vmem(len(FLAGS) * rank, 128, dtype=jnp.int32)],
        hbm=(*down_state, *up_state),
        smem=(projection_index, owner),
        ties=(tie,),
        scratch=[pltpu.SemaphoreType.DMA((6,))],
    )
    return state[:3], state[3:], flags


def flag(flags, name, rank):
    return flags[pl.ds(FLAGS.index(name) * rank, rank), :]


def column_tiles(width):
    return [pl.ds(k, 128) for k in range(0, width, 128)]


def down_parity(flags, rank, t_size, r_size):
    t, r = lax.axis_index("tensor"), lax.axis_index("replica")
    return flag(flags, "column_proj", rank) ^ ((r + t * r_size // t_size) % 2)


def up_parity(flags, rank, t_size, r_size):
    r = lax.axis_index("replica")
    return jnp.full((rank, 128), r % 2, jnp.int32)


def gradient_half(lows, tokens, base, coefficient, flip, ties=()):
    rank = lows[0].shape[0] // 4
    width = tokens.shape[2]
    parts = len(lows)

    def kernel(*refs):
        lows, tokens, out = refs[:parts], refs[parts], refs[parts + 1]
        p = (lax.axis_index("replica") % 2) ^ flip
        rows = pl.ds(pl.multiple_of((base + p) * rank, rank), rank)
        total = functools.reduce(jnp.add, [f32(x[rows, :]) for x in lows]).astype(jnp.bfloat16)
        cut = min(width, 512)
        for k in range(0, width, cut):
            span = pl.ds(k, cut)
            grad = coefficient * jnp.dot(
                total, tokens[p, :, span], preferred_element_type=jnp.float32
            )
            out[:, span] = grad.astype(out.dtype)

    return local(
        kernel, "gradient_half", [vmem(rank, width)], ins=(*lows, tokens), ties=ties
    )[0]


def gradient_parts(lows, tokens, flags, base, coefficient, half, ties=()):
    rank = lows[0].shape[0] // 4
    width = tokens.shape[2]
    parts = len(lows)

    def kernel(*refs):
        lows, tokens, flags, (send, keep) = refs[:parts], refs[parts], refs[parts + 1 : -2], refs[-2:]
        rows = pl.ds(base * rank, 2 * rank)
        total = functools.reduce(jnp.add, [f32(x[rows, :]) for x in lows]).astype(jnp.bfloat16)
        kept = half(flags[0] if flags else None, rank) == 0
        cut = min(width, 512)
        for k in range(0, width, cut):
            grads = [
                coefficient
                * jnp.dot(
                    total[p * rank : (p + 1) * rank],
                    tokens[p, :, pl.ds(k, cut)],
                    preferred_element_type=jnp.float32,
                )
                for p in range(2)
            ]
            for j in range(0, cut, 128):
                first, second = [g[:, j : j + 128] for g in grads]
                tile = pl.ds(k + j, 128)
                keep[:, tile] = jnp.where(kept, first, second).astype(keep.dtype)
                send[:, tile] = jnp.where(kept, second, first).astype(send.dtype)

    return local(
        kernel,
        "gradient_parts",
        [vmem(rank, width), vmem(rank, width)],
        ins=(*lows, tokens, *flags),
        ties=ties,
    )


def join(*sums, ties=(), after=(), passed=()):
    terms = [x for group in sums for x in group]

    def kernel(*refs):
        refs, outs = list(refs[: len(terms)]), refs[len(terms) :]
        for group, out in zip(sums, outs):
            total = functools.reduce(jnp.add, [f32(refs.pop(0)[...]) for _ in group])
            out[...] = total.astype(out.dtype)

    return local(
        kernel,
        "join",
        [vmem(*group[0].shape) for group in sums],
        ins=terms,
        ties=ties,
        after=after,
        passed=passed,
    )


def chosen_factor(state, own, other, flags, half, ties=(), after=(), passed=()):
    rank, width = own[0].shape
    n_own, n_other = len(own), len(other)

    def total(refs, tile):
        return f32(functools.reduce(jnp.add, [f32(x[:, tile]) for x in refs]).astype(jnp.bfloat16))

    def kernel(*refs):
        state, own, other = refs[:3], refs[3 : 3 + n_own], refs[3 + n_own : 3 + n_own + n_other]
        flags, out = refs[3 + n_own + n_other :]
        p = jnp.max(flag(flags, "proj", rank)[0:1, :])
        for tile in column_tiles(width):
            grad = total(own, tile)
            if other:
                mine = flag(flags, "proj", rank) == half(flags, rank)
                grad = jnp.where(mine, grad, total(other, tile))
            held = [x[p, :, tile] for x in state]
            out[:, tile] = moment_update(*held, grad)[0].astype(out.dtype)

    return local(
        kernel,
        "chosen_factor",
        [vmem(rank, width)],
        ins=(*state, *own, *other, flags),
        ties=ties,
        after=after,
        passed=passed,
    )


def adam(state, own, other, flags, half, ties=()):
    rank, width = own.shape
    cuts = max(1, width // 1024)
    cut = width // cuts

    def kernel(*refs):
        state, own, other, flags, outs, (fresh, sems) = refs[:3], *refs[3:6], refs[-5:-2], refs[-2:]
        kept = half(flags, rank)
        copies = []
        for k in range(cuts):
            for j in range(k * cut, (k + 1) * cut, 128):
                tile = pl.ds(j, 128)
                grads = f32(own[:, tile]), f32(other[:, tile])
                for p in range(2):
                    grad = jnp.where(kept == p, *grads)
                    values = moment_update(*[x[p, :, tile] for x in state], grad)
                    for i, value in enumerate(values):
                        fresh[i, p, :, tile] = value
            span = pl.ds(k * cut, cut)
            for i, x in enumerate(outs):
                copies.append(
                    pltpu.make_async_copy(fresh.at[i, :, :, span], x.at[:, :, span], sems.at[k, i])
                )
                copies[-1].start()
        for copy in copies:
            copy.wait()

    in_vmem = (*state, own, other, flags, *ties)
    return pl.pallas_call(
        kernel,
        in_specs=[pl.BlockSpec(memory_space=pltpu.VMEM)] * 6
        + [pl.BlockSpec(memory_space=pl.ANY)] * len(ties),
        out_specs=[pl.BlockSpec(memory_space=pltpu.HBM)] * 3,
        out_shape=[pltpu.HBM(x.shape, x.dtype) for x in state],
        scratch_shapes=[
            vmem(3, 2, rank, width, dtype=jnp.float32),
            pltpu.SemaphoreType.DMA((cuts, 3)),
        ],
        compiler_params=pltpu.CompilerParams(vmem_limit_bytes=8 * MIB),
        cost_estimate=pl.CostEstimate(flops=0, bytes_accessed=1024, transcendentals=0),
        name="adam",
    )(*[pltpu.with_memory_space_constraint(x, pltpu.VMEM) for x in in_vmem])


def adam_half(state, grad, flags, half, flip, outs, after):
    rank, width = grad.shape
    cuts = max(1, width // 1024)
    cut = width // cuts

    def kernel(*refs):
        grad, flags, state = refs[0], refs[1], refs[2:5]
        targets, (fresh, sems) = refs[-5:-2], refs[-2:]
        p = jnp.max(half(flags, rank)[0:1, :]) ^ flip
        copies = []
        for k in range(cuts):
            for j in range(k * cut, (k + 1) * cut, 128):
                tile = pl.ds(j, 128)
                values = moment_update(*[x[p, :, tile] for x in state], f32(grad[:, tile]))
                for i, value in enumerate(values):
                    fresh[i, :, tile] = value
            span = pl.ds(k * cut, cut)
            for i, x in enumerate(targets):
                copies.append(
                    pltpu.make_async_copy(fresh.at[i, :, span], x.at[p, :, span], sems.at[k, i])
                )
                copies[-1].start()
        for copy in copies:
            copy.wait()

    in_vmem, in_hbm = (grad, flags, *state), (*after, *outs)
    first = len(in_vmem) + len(after)
    return pl.pallas_call(
        kernel,
        in_specs=[pl.BlockSpec(memory_space=pltpu.VMEM)] * len(in_vmem)
        + [pl.BlockSpec(memory_space=pltpu.HBM)] * len(in_hbm),
        out_specs=[pl.BlockSpec(memory_space=pltpu.HBM)] * 3,
        out_shape=[pltpu.HBM(x.shape, x.dtype) for x in state],
        input_output_aliases={first + i: i for i in range(3)},
        scratch_shapes=[
            vmem(3, rank, width, dtype=jnp.float32),
            pltpu.SemaphoreType.DMA((cuts, 3)),
        ],
        compiler_params=pltpu.CompilerParams(vmem_limit_bytes=8 * MIB),
        cost_estimate=pl.CostEstimate(flops=0, bytes_accessed=1024, transcendentals=0),
        name="adam_half",
    )(
        *[pltpu.with_memory_space_constraint(x, pltpu.VMEM) for x in in_vmem],
        *[pltpu.with_memory_space_constraint(x, pltpu.HBM) for x in in_hbm],
    )


def pick(flags, name, held, ids, rank):
    wanted = flag(flags, name, rank)

    def tile_of(tile):
        found = f32(held[0][:, tile])
        for i in range(1, len(held)):
            found = jnp.where(wanted == ids[i], f32(held[i][:, tile]), found)
        return found

    return tile_of


def block_ids(t_size, many):
    t = lax.axis_index("tensor")
    ids, distance = [t], 1
    while distance < t_size // 2:
        ids = ids + [i ^ distance for i in ids]
        distance *= 2
    return ids[:many]


def offer(held, flags, t_size, ties=()):
    rank, width = held[0].shape

    def kernel(*refs):
        held, flags, out = refs[:-2], refs[-2], refs[-1]
        tile_of = pick(flags, "partners", held, block_ids(t_size, len(held)), rank)
        for tile in column_tiles(width):
            out[:, tile] = tile_of(tile).astype(out.dtype)

    return local(kernel, "offer", [vmem(rank, width)], ins=(*held, flags), ties=ties)


def columns_of_b(held, flags, t_size, ties=()):
    rank, width = held[0].shape

    def kernel(*refs):
        held, flags, cols = refs[:-2], refs[-2], refs[-1]
        ids = block_ids(t_size, len(held) - 1)
        tile_of = pick(flags, "mine", (held[-1], *held[:-1]), (None, *ids), rank)
        for tile in column_tiles(width):
            cols[:, tile] = (adapter_scale * tile_of(tile)).astype(cols.dtype)

    return local(
        kernel, "columns_of_b", [vmem(rank, width)], ins=(*held, flags), ties=ties
    )[0]


def rows_of_a(block):
    rank, height = block.shape

    def kernel(block, left):
        for j in range(0, height, 128):
            tile = pl.ds(j, 128)
            left[tile, :] = block[:, tile].T

    return local(kernel, "rows_of_a", [vmem(height, rank)], ins=(block,))[0]


def refresh(left, cols, flags, weight, state, grad, half):
    height, width = weight.shape
    rank = cols.shape[0]
    block = min(height, 1024)
    steps = height // block
    slots = min(2, steps)
    groups = max(1, width // 1024)
    group = width // groups
    chunks = max(1, width // 1024)
    cut, apart = width // chunks, max(1, (steps - 2) // chunks)
    turns = [min(apart * k, steps - 1) for k in range(chunks)]

    def kernel(*refs):
        left, cols, flags, weight, grad, *state = refs[:8]
        out, targets, (ring, sems, fresh, fresh_sems) = refs[8], refs[9:12], refs[12:]
        step = pl.program_id(0)
        slot = step % slots

        def emit(i, g):
            at, span = pl.ds(pl.multiple_of(i * block, block), block), pl.ds(g * group, group)
            return pltpu.make_async_copy(
                ring.at[i % slots, :, span], out.at[at, span], sems.at[i % slots, g]
            )

        def writes(p, k):
            span = pl.ds(k * cut, cut)
            return [
                pltpu.make_async_copy(fresh.at[i, :, span], x.at[p, :, span], fresh_sems.at[i, k])
                for i, x in enumerate(targets)
            ]

        @pl.when(step >= slots)
        def _():
            for g in range(groups):
                emit(step - slots, g).wait()

        wide = min(width, 256)
        at = pl.ds(pl.multiple_of(step * block, block), block)
        for g in range(groups):
            for k in range(g * group, (g + 1) * group, wide):
                span = pl.ds(k, wide)
                change = jnp.dot(left[at, :], cols[:, span], preferred_element_type=jnp.float32)
                ring[slot, :, span] = (f32(weight[at, span]) + change).astype(ring.dtype)
            emit(step, g).start()

        for chunk, turn in enumerate(turns):

            @pl.when(step == turn)
            def _():
                p = jnp.max(half(flags, rank)[0:1, :])
                for k in range(chunk * cut, (chunk + 1) * cut, 128):
                    tile = pl.ds(k, 128)
                    values = moment_update(*[x[p, :, tile] for x in state], f32(grad[:, tile]))
                    for i, value in enumerate(values):
                        fresh[i, :, tile] = value
                for copy in writes(p, chunk):
                    copy.start()

        @pl.when(step == steps - 1)
        def _():
            p = jnp.max(half(flags, rank)[0:1, :])
            for k in range(chunks):
                for copy in writes(p, k):
                    copy.wait()
            for i in range(steps - slots, steps):
                for g in range(groups):
                    emit(i, g).wait()

    operands = (left, cols, flags, weight, grad, *state)
    outs = [pltpu.HBM((height, width), weight.dtype)] + [pltpu.HBM(x.shape, x.dtype) for x in state]
    result, *fresh = pl.pallas_call(
        kernel,
        grid=(steps,),
        in_specs=[pl.BlockSpec(memory_space=pltpu.VMEM)] * len(operands),
        out_specs=[pl.BlockSpec(memory_space=pltpu.HBM)] * len(outs),
        out_shape=outs,
        scratch_shapes=[
            vmem(slots, block, width),
            pltpu.SemaphoreType.DMA((slots, groups)),
            vmem(3, rank, width, dtype=jnp.float32),
            pltpu.SemaphoreType.DMA((3, chunks)),
        ],
        compiler_params=pltpu.CompilerParams(vmem_limit_bytes=20 * MIB),
        cost_estimate=pl.CostEstimate(flops=0, bytes_accessed=1024, transcendentals=0),
        name="refresh",
    )(*[pltpu.with_memory_space_constraint(x, pltpu.VMEM) for x in operands])
    return result, fresh


def tensor_sum_parts(low, size):
    parts, stride = [low], 1
    while stride < size:
        if len(parts) > 1:
            total = functools.reduce(jnp.add, [f32(x) for x in parts])
            parts = [total.astype(jnp.bfloat16)]
        radix = min(4, size // stride)
        mine = parts[0]
        for hop in range(1, radix):
            pairs = [
                (i, i - i % (stride * radix) + (i + hop * stride) % (stride * radix))
                for i in range(size)
            ]
            parts.append(lax.ppermute(mine, "tensor", pairs))
        stride *= radix
    return parts


def toward(block, distance, t_size, r_size, first):
    pairs = []
    for t in range(t_size):
        root = t * r_size // t_size
        for r in range(r_size):
            same_side = ((r ^ root) & distance) == 0
            same_half = (r ^ root) % 2 == 0
            if (same_side != same_half) == first:
                pairs.append((t * r_size + r, t * r_size + (r ^ distance)))
    return lax.ppermute(block, ("tensor", "replica"), pairs)


def gather_rows(block, t_size, r_size):
    t = lax.axis_index("tensor")
    distance = 1
    while distance < max(1, t_size // r_size):
        other = swap(block, "tensor", t_size, distance)
        block = jnp.where(
            (t & distance) == 0,
            jnp.concatenate([block, other], axis=1),
            jnp.concatenate([other, block], axis=1),
        )
        distance *= 2
    return block


def spread_steps(t_size, r_size):
    distance, steps = t_size // 2, []
    while distance >= max(1, t_size // r_size):
        steps.append(distance)
        distance //= 2
    return steps


def spread_rest(distance, t_size, r_size):
    return functools.reduce(
        lambda a, b: a | b, [d for d in spread_steps(t_size, r_size) if d <= distance]
    )


def spread_send(block, distance, t_size, r_size):
    rest = spread_rest(distance, t_size, r_size)
    pairs = []
    for r in range(r_size):
        root = r * t_size // r_size
        for t in range(t_size):
            if (t ^ root) & rest == 0:
                pairs.append((t * r_size + r, (t ^ distance) * r_size + r))
    return lax.ppermute(block, ("tensor", "replica"), pairs)


def spread_take(came, block, distance, t_size, r_size, ties=()):
    rest = spread_rest(distance, t_size, r_size)

    def kernel(came, block, out):
        t, r = lax.axis_index("tensor"), lax.axis_index("replica")
        takes = ((t ^ (r * t_size // r_size)) & rest) == distance

        @pl.when(takes)
        def _():
            out[...] = came[...]

        @pl.when(jnp.logical_not(takes))
        def _():
            out[...] = block[...]

    return local(kernel, "spread", [vmem(*block.shape)], ins=(came, block), ties=ties)[0]


def own_rows(block, t_size, r_size):
    parts = max(1, r_size // t_size)
    if parts == 1:
        return block
    size = block.shape[1] // parts
    return lax.dynamic_slice_in_dim(block, (lax.axis_index("replica") % parts) * size, size, 1)


def per_device(
    acts,
    cots,
    down_factor,
    up_factor,
    down_first_moment,
    down_second_moment,
    up_first_moment,
    up_second_moment,
    rollout_weight,
    owner,
    projection_index,
):
    t_size, r_size = lax.axis_size("tensor"), lax.axis_size("replica")
    turn = lambda x: jnp.transpose(x, (0, 2, 1))
    down_state = tuple(map(turn, (down_factor, down_first_moment, down_second_moment)))
    up_state = (up_factor, up_first_moment, up_second_moment)
    coefficient = adapter_scale / (acts.shape[1] * r_size)
    down_half = functools.partial(down_parity, t_size=t_size, r_size=r_size)
    up_half = functools.partial(up_parity, t_size=t_size, r_size=r_size)
    exchange = lambda x, distance: swap(x, "replica", r_size, distance)

    low, acts_in, cots_in = low_parts(acts, cots, down_state[0], up_state[0])
    lows = tensor_sum_parts(low, t_size)
    up_send = gradient_half(lows, cots_in, 2, coefficient, 1)
    up_own = gradient_half(lows, cots_in, 2, coefficient, 0, ties=(up_send,))
    up_came = exchange(up_send, 1)
    down_held, up_held, flags = load_state(
        down_state, up_state, projection_index, owner, t_size, r_size, up_send
    )
    down_send, down_own = gradient_parts(lows, acts_in, (flags,), 0, coefficient, down_half)
    up_own, down_send = join((up_own, up_came), passed=(down_send,))
    up_came, distance = exchange(up_own, 2), 4
    down_came = exchange(down_send, 1)
    while distance < r_size:
        (up_own,) = join((up_own, up_came))
        up_came, distance = exchange(up_own, distance), 2 * distance
    down_own, again = join(*[(down_own, down_came)] * 2)
    (up_own,) = join((up_own, up_came), ties=(down_own,))
    up_other = exchange(up_own, 1)
    distance = 2
    while 2 * distance < r_size:
        down_own, again = join(*[(down_own, exchange(down_own, distance))] * 2)
        distance *= 2
    down_first = toward(down_own, distance, t_size, r_size, True)

    (block,) = chosen_factor(down_held, [down_own, down_first], [], flags, down_half)
    block = gather_rows(block, t_size, r_size)
    steps = spread_steps(t_size, r_size)
    rows = spread_send(block, steps[0], t_size, r_size)
    up_mine, again = chosen_factor(
        up_held, [up_own], [up_other], flags, up_half, ties=(block,), passed=(again,)
    )
    down_rest = toward(again, distance, t_size, r_size, False)
    held, shift = [up_mine], 1
    while shift < t_size // 2:
        held = held + [swap(x, "tensor", t_size, shift) for x in held]
        shift *= 2
    rows = spread_take(rows, block, steps[0], t_size, r_size)
    (offered,) = offer(held, flags, t_size, ties=(rows,))
    held = held + [swap(offered, "tensor", t_size, t_size // 2)]
    fresh_up = adam(up_held, up_own, up_other, flags, up_half, ties=(offered,))
    (down_own,) = join((down_own, down_first, down_rest), after=(fresh_up[0],))
    down_other = exchange(down_own, 1)
    cols = columns_of_b(held, flags, t_size, ties=(down_own,))
    for shift in steps[1:]:
        came = spread_send(rows, shift, t_size, r_size)
        rows = spread_take(came, rows, shift, t_size, r_size, ties=(cols,))
    left = rows_of_a(own_rows(rows, t_size, r_size))
    fresh_rollout_weight, fresh_down = refresh(
        left, cols, flags, rollout_weight, down_held, down_own, down_half
    )
    fresh_down = adam_half(
        down_held, down_other, flags, down_half, 1, fresh_down, (fresh_rollout_weight,)
    )
    return (
        turn(fresh_down[0]),
        fresh_up[0],
        turn(fresh_down[1]),
        turn(fresh_down[2]),
        fresh_up[1],
        fresh_up[2],
        fresh_rollout_weight,
    )


def solution(mesh):
    placed = (
        P(None, ("groups", "replica"), "tensor"),
        P(None, ("groups", "replica"), "tensor"),
        P("groups", "tensor", None),
        P("groups", None, "tensor"),
        P("groups", "tensor", None),
        P("groups", "tensor", None),
        P("groups", None, "tensor"),
        P("groups", None, "tensor"),
        P("replica", "tensor"),
        P(),
        P("groups"),
    )
    return jax.shard_map(
        per_device,
        mesh=mesh,
        in_specs=placed,
        out_specs=(
            P("groups", "tensor", None),
            P("groups", None, "tensor"),
            P("groups", "tensor", None),
            P("groups", "tensor", None),
            P("groups", None, "tensor"),
            P("groups", None, "tensor"),
            P(("groups", "replica"), "tensor"),
        ),
        check_vma=False,
    )
```
